32 devices in a mesh: expert: 8 (over z, x), tensor: 4 (over y, core).
Axes of the slice: x: 2, y: 2, z: 4, core: 2. Of those that a mesh axis runs over, the one named last changes fastest.
Arguments:
- tokens: bfloat16 [4096, 2560], P(('expert', 'tensor')), may hold values from -6 to 6
- expert_ids: int32 [4096, 1], P(('expert', 'tensor')), may hold values from 0 to 7; in each aligned block of 128 rows (0 to 127, 128 to 255, ...) at most 24 rows name the same one
- live_counts: int32 [32], P(('expert', 'tensor')), may hold values from 1 to 128, 2560 in all
- router: bfloat16 [2560, 8], replicated, may hold values from -0.125 to 0.125
- up_weight: bfloat16 [8, 2560, 4096], P('expert', None, 'tensor'), may hold values from -0.125 to 0.125
- down_weight: bfloat16 [8, 4096, 2560], P('expert', 'tensor'), may hold values from -0.09375 to 0.09375
- out_grad: bfloat16 [4096, 2560], P(('expert', 'tensor')), may hold values from -6 to 6
Outputs:
- mixed: bfloat16 [4096, 2560], P(('expert', 'tensor'))
- token_grad: bfloat16 [4096, 2560], P(('expert', 'tensor'))
- up_grad: bfloat16 [8, 2560, 4096], P('expert', None, 'tensor')
- down_grad: bfloat16 [8, 4096, 2560], P('expert', 'tensor')
- router_grad: float32 [2560, 8], replicated
The draws below stay inside these ranges and needn't reach their ends.
Inputs may be any that keep to these rules, and one draw needn't show every extreme that they name: `expert_ids`: within the rows of one device (aligned blocks of 128 rows) no expert is named by more than 24 rows; in every draw some expert is named by exactly 24 rows of some device. live_counts[k] real token rows lead device k's 128 rows, the rest are padding; some device holds exactly 128 real rows in every draw.
All inputs are finite; a program needn't handle non-finite values.
Results may differ from the reference program's by a relative error of at most 0.0063.
Values may be sent and summed in bfloat16 or wider, within the bound.
No kernel may reach another device: no remote copies, remote signals or barrier semaphores. Data moves between devices by JAX's collectives and lax.ppermute only.
A program may use at most 128 MiB of HBM per device.

```python
import math
import jax
import jax.numpy as jnp
import numpy as np
from jax import lax

D = 2560
FFW = 4096
TOK_DEV = 128
EXPERTS = 8
MOST = 24
TOKENS = 4096
N_EXPERT = 8
N_TENSOR = 4


def levels(own_key, shape, split, least, largest):
    gain, own = 1.0, jax.random.fold_in(own_key, 6)
    for dim, shards_of in split:
        heights = jnp.exp(jax.random.uniform(jax.random.fold_in(own, dim), (shards_of,), jnp.float32, least / len(split), largest / len(split)))
        gain = gain * jnp.repeat(heights, shape[dim] // shards_of).reshape([-1 if axis == dim else 1 for axis in range(len(shape))])
    return gain


def length_profile(amount, total, limit, lean):
    weights = [(1 << 20) // math.isqrt(grade ** lean) + 1 for grade in range(2, amount + 1)]
    spare, given = total - limit - (amount - 1), [1] * (amount - 1)
    while spare > 0:
        candidates = [i for i in range(amount - 1) if given[i] < limit]
        whole, budget = sum([weights[i] for i in candidates]), spare
        for i in candidates:
            addition = min(limit - given[i], max(1, budget * weights[i] // whole), spare)
            given[i] = given[i] + addition
            spare = spare - addition
    return np.array([limit] + given)


def uneven(key, count, total, reach, lean):
    if count == 2:
        one = jax.random.randint(key, (), max(1, total - reach), min(reach, total - 1) + 1)
        return jnp.stack([one, total - one])
    sizes = jnp.asarray(length_profile(count, total, reach, lean), jnp.int32)
    pairs = (count - 1) // 2
    source_of, receiver = sizes[1:1 + 2 * pairs:2], sizes[2:2 + 2 * pairs:2]
    slack = jnp.minimum(source_of - 1, reach - receiver)
    moved = jax.random.randint(jax.random.fold_in(key, 1), (pairs,), 0, 1 << 20) % (slack + 1)
    sizes = sizes.at[1:1 + 2 * pairs:2].set(source_of - moved).at[2:2 + 2 * pairs:2].set(receiver + moved)
    return sizes[jax.random.permutation(jax.random.fold_in(key, 2), count)]


def routed_block(stream_key, own, number, rows, number_of, top, limit, lean):
    order = jax.random.permutation(stream_key, number_of)
    packed, ordinary = load_shares(number_of, rows * top, limit, lean, True), load_shares(number_of, rows * top, limit, lean, False)
    places = jnp.arange(number_of)

    def named(sizes, rotation):
        used = int((sizes > 0).sum())
        fixed = max(1, used // 4)
        passed = fixed + (places - fixed + rotation * (used - fixed)) % max(1, number_of - fixed)
        return jnp.zeros((number_of,), jnp.int32).at[order[jnp.where(places < fixed, places, passed)]].set(jnp.asarray(sizes, jnp.int32))

    sizes = jnp.where(number % 4 == 0, named(packed, number // 4), named(ordinary, number - number // 4 - 1))
    mixed = jax.random.permutation(jax.random.fold_in(own, 3), number_of)
    giver, receiver = mixed[0:number_of // 2 * 2:2], mixed[1:number_of // 2 * 2:2]
    room = jnp.minimum(sizes[giver] - 1, limit - sizes[receiver]) // 2
    room = jnp.where((giver == order[0]) | (receiver == order[0]) | (sizes[receiver] == 0), 0, jnp.maximum(room, 0))
    passed = jax.random.randint(jax.random.fold_in(own, 4), (number_of // 2,), 0, 1 << 20) % (room + 1)
    sizes = sizes.at[giver].add(-passed).at[receiver].add(passed)
    members = jnp.searchsorted(jnp.cumsum(sizes), jnp.arange(rows * top), side="right").astype(jnp.int32)
    table = members.reshape(top, rows).T
    table = table[jax.random.permutation(jax.random.fold_in(own, 1), rows)]
    rotation = jax.random.randint(jax.random.fold_in(own, 2), (rows, 1), 0, top)
    return jnp.take_along_axis(table, (jnp.arange(top)[None, :] + rotation) % top, axis=1)


def load_shares(count, total, bound, lean, full):
    loads = [(1 << 20) // math.isqrt(rank ** lean) + 1 for rank in range(1, count + 1)]
    largest = bound if full else min(bound, max(-(-total // count), total * loads[0] // sum(loads)))
    least = 1 if total - largest >= count - 1 else 0
    counts, rest = [largest] + [least] * (count - 1), total - largest - least * (count - 1)
    while rest > 0:
        movable = [i for i in range(1, count) if counts[i] < largest] or [i for i in range(1, count) if counts[i] < bound]
        pool, left = sum([loads[i] for i in movable]), rest
        for i in movable:
            addition = min(bound - counts[i], max(1, left * loads[i] // pool), rest)
            counts[i] = counts[i] + addition
            rest = rest - addition
    return np.array(counts)


def scatter_about(own_key, dims, deviation, reach, shards=(), kind=jnp.bfloat16):
    array = deviation * jax.random.normal(own_key, dims, jnp.float32)
    if shards:
        array = array * levels(own_key, dims, shards, -0.22, 0.18)
    return jnp.clip(array, -reach, reach).astype(kind)


def setup_inputs(seed: int = 0) -> dict:
    splits = jax.random.split(jax.random.key(seed), 8)
    tokens = scatter_about(splits[0], (TOKENS, D), 1.0, 6.0, ((0, 32),))
    expert_ids_keys = jax.random.split(jax.random.fold_in(splits[1], 1), TOKENS // TOK_DEV)
    expert_ids_turns = jax.random.permutation(jax.random.fold_in(splits[1], 3), TOKENS // TOK_DEV)
    expert_ids = jax.vmap(lambda own, number: routed_block(jax.random.fold_in(splits[1], 2), own, number, TOK_DEV, EXPERTS, 1, MOST, 2))(expert_ids_keys, expert_ids_turns).reshape((TOKENS, 1))
    live_counts = uneven(splits[2], N_EXPERT * N_TENSOR, N_EXPERT * N_TENSOR * TOK_DEV * 5 // 8, TOK_DEV, 2).astype(jnp.int32)
    router = scatter_about(splits[3], (D, EXPERTS), D ** -0.5, 0.125)
    up_weight = scatter_about(splits[4], (EXPERTS, D, FFW), D ** -0.5, 0.125, ((0, 8), (2, 4)))
    down_weight = scatter_about(splits[5], (EXPERTS, FFW, D), FFW ** -0.5, 0.09375, ((0, 8), (1, 4)))
    out_grad = scatter_about(splits[6], (TOKENS, D), 1.0, 6.0, ((0, 32),))
    return {"tokens": tokens, "expert_ids": expert_ids, "live_counts": live_counts, "router": router, "up_weight": up_weight, "down_weight": down_weight, "out_grad": out_grad}


def silu_slope(hidden):
    sig = jax.nn.sigmoid(hidden)
    return sig * (1.0 + hidden * (1.0 - sig))


def reference(tokens, expert_ids, live_counts, router, up_weight, down_weight, out_grad):
    total = tokens.shape[0]
    width = tokens.shape[1]
    per_dev = total // live_counts.shape[0]
    row_ids = jnp.arange(total, dtype=jnp.int32)
    owner = row_ids // per_dev
    live = (row_ids - owner * per_dev) < live_counts[owner]
    live_rows = jnp.where(live[:, None], tokens, jnp.zeros_like(tokens))
    ids = expert_ids[:, 0]
    logits = jnp.dot(tokens, router, preferred_element_type=jnp.float32)
    onehot = (ids[:, None] == jnp.arange(EXPERTS, dtype=jnp.int32)[None, :]).astype(jnp.float32)
    gate = jax.nn.sigmoid(jnp.sum(logits * onehot, axis=1))
    out_cot = jnp.where(live[:, None], gate[:, None] * out_grad.astype(jnp.float32), 0.0).astype(jnp.bfloat16)
    pad_b = jnp.zeros((1, width), jnp.bfloat16)
    x_pad = jnp.concatenate([live_rows, pad_b], axis=0)
    cot_pad = jnp.concatenate([out_cot, pad_b], axis=0)
    dy_pad = jnp.concatenate([out_grad, pad_b], axis=0)
    gate_pad = jnp.concatenate([gate, jnp.zeros((1,), jnp.float32)], axis=0)
    capacity = N_EXPERT * N_TENSOR * MOST

    def one_expert(index):
        picks = jnp.nonzero(ids == index, size=capacity, fill_value=total)[0].astype(jnp.int32)
        x_e = x_pad[picks]
        cot_e = cot_pad[picks]
        dy_e = dy_pad[picks]
        gate_e = gate_pad[picks]
        w_up = up_weight[index]
        w_down = down_weight[index]
        hidden = jnp.dot(x_e, w_up, preferred_element_type=jnp.float32)
        active = jax.nn.silu(hidden).astype(jnp.bfloat16)
        expert_out = jnp.dot(active, w_down, preferred_element_type=jnp.float32).astype(jnp.bfloat16)
        mixed_e = (gate_e[:, None] * expert_out.astype(jnp.float32)).astype(jnp.bfloat16)
        slope = jnp.sum(dy_e.astype(jnp.float32) * expert_out.astype(jnp.float32), axis=1) * gate_e * (1.0 - gate_e)
        hidden_cot = (jnp.dot(cot_e, w_down.T, preferred_element_type=jnp.float32) * silu_slope(hidden)).astype(jnp.bfloat16)
        down_g = jnp.dot(active.T, cot_e, preferred_element_type=jnp.float32).astype(jnp.bfloat16)
        up_g = jnp.dot(x_e.T, hidden_cot, preferred_element_type=jnp.float32).astype(jnp.bfloat16)
        expert_cot = jnp.dot(hidden_cot, w_up.T, preferred_element_type=jnp.float32).astype(jnp.bfloat16)
        column = router[:, index].astype(jnp.float32)
        grad_e = (expert_cot.astype(jnp.float32) + slope[:, None] * column[None, :]).astype(jnp.bfloat16)
        router_e = jnp.dot(x_e.astype(jnp.float32).T, slope, precision=lax.Precision.HIGHEST)
        return picks, mixed_e, grad_e, up_g, down_g, router_e

    picks, mixed_all, grad_all, up_grad, down_grad, router_cols = lax.map(one_expert, jnp.arange(EXPERTS, dtype=jnp.int32))
    flat = picks.reshape(-1)
    mixed = jnp.zeros((total + 1, width), jnp.bfloat16).at[flat].set(mixed_all.reshape(-1, width))[:total]
    token_grad = jnp.zeros((total + 1, width), jnp.bfloat16).at[flat].set(grad_all.reshape(-1, width))[:total]
    return mixed, token_grad, up_grad, down_grad, router_cols.T
```

```python
import jax
import jax.numpy as jnp
from jax import lax
from jax.sharding import PartitionSpec as P


def dot(a, b, out=jnp.float32, dims=((1,), (0,))):
    return lax.dot_general(a, b, (dims, ((), ())), preferred_element_type=jnp.float32).astype(out)


def shifted(x, axis, size, step):
    return lax.ppermute(x, axis, [(i, (i + step) % size) for i in range(size)])


def crossed(x, axis, size, bit):
    return lax.ppermute(x, axis, [(i, i ^ bit) for i in range(size)])


def spread(boxes, axis, size):
    return [boxes[0]] + [shifted(boxes[s], axis, size, s) for s in range(1, size)]


def collect(boxes, axis, size):
    return [boxes[0]] + [shifted(boxes[s], axis, size, -s) for s in range(1, size)]


def gather_rows(rows, axis, size):
    held = {0: rows}
    bit = size // 2
    while bit:
        for m in sorted(held):
            held[m | bit] = crossed(held[m], axis, size, bit)
        bit //= 2
    return held


def sum_rows(terms, axis, size):
    bit = 1
    while bit < size:
        sums = {}
        for m in sorted(terms, reverse=True):
            if not m & bit:
                came = crossed(terms[m | bit].astype(jnp.bfloat16), axis, size, bit)
                sums[m] = terms[m].astype(jnp.float32) + came.astype(jnp.float32)
        terms = sums
        bit *= 2
    return terms[0].astype(jnp.bfloat16)


def make(n_expert, n_tensor):
    half = max(n_tensor // 2, 1)
    batches = [list(range(i, i + half)) for i in reversed(range(0, n_tensor, half))]

    def per_device(tokens, expert_ids, live_counts, router, up_weight, down_weight, out_grad):
        tok_rows, width = tokens.shape
        experts = router.shape[1]
        most = 3 * tok_rows // (2 * experts)
        slots = experts * most
        me = lax.axis_index("expert")
        ids = expert_ids[:, 0]
        live = lax.iota(jnp.int32, tok_rows) < live_counts[0]
        chosen = ids[:, None] == lax.iota(jnp.int32, experts)[None, :]
        chosen_int = chosen.astype(jnp.int32)
        rank = jnp.sum(jnp.cumsum(chosen_int, axis=0) * chosen_int, axis=1) - 1
        target = jnp.where(live, lax.rem(ids - me + experts, experts) * most + rank, -1)
        placing = (lax.iota(jnp.int32, slots)[:, None] == target[None, :]).astype(jnp.bfloat16)
        w_up = up_weight[0]
        w_down = down_weight[0]

        def dispatch(array):
            box = dot(placing, array, jnp.bfloat16).reshape(experts, most, width)
            got = spread([box[s] for s in range(experts)], "expert", n_expert)
            return gather_rows(jnp.concatenate(got, axis=0), "tensor", n_tensor)

        def send_back(terms):
            share = sum_rows(terms, "tensor", n_tensor).reshape(experts, most, width)
            got = collect([share[s] for s in range(experts)], "expert", n_expert)
            return dot(placing, jnp.concatenate(got, axis=0), jnp.bfloat16, ((0,), (0,)))

        logits = dot(tokens, router)
        gate = jax.nn.sigmoid(jnp.sum(logits * chosen.astype(jnp.float32), axis=1))
        in_rows = dispatch(tokens)
        out_cot = (gate[:, None] * out_grad.astype(jnp.float32)).astype(jnp.bfloat16)
        in_cots = dispatch(out_cot)

        rows, hidden, active = {}, {}, {}
        terms = {}
        for b, batch in enumerate(batches):
            rows[b] = jnp.concatenate([in_rows[m] for m in batch], axis=0)
            hidden[b] = dot(rows[b], w_up)
            active[b] = jax.nn.silu(hidden[b]).astype(jnp.bfloat16)
            term = dot(active[b], w_down, jnp.bfloat16)
            for i, m in enumerate(batch):
                terms[m] = term[i * slots : (i + 1) * slots]
        out_rows = send_back(terms)

        column = lax.dynamic_slice_in_dim(router, me, 1, axis=1)
        cots, hidden_cot, slope = {}, {}, {}
        terms = {}
        for b, batch in enumerate(batches):
            cots[b] = jnp.concatenate([in_cots[m] for m in batch], axis=0)
            back = dot(cots[b], w_down, dims=((1,), (1,)))
            sig = jax.nn.sigmoid(hidden[b])
            hidden_cot[b] = (back * (sig * (1.0 + hidden[b] * (1.0 - sig)))).astype(jnp.bfloat16)
            off = 1.0 - jax.nn.sigmoid(dot(rows[b], column))
            slope[b] = jnp.sum(back * active[b].astype(jnp.float32), axis=1, keepdims=True) * off
            term = dot(hidden_cot[b], w_up, jnp.bfloat16, ((1,), (1,)))
            for i, m in enumerate(batch):
                terms[m] = term[i * slots : (i + 1) * slots]
        cot_rows = send_back(terms)

        order = range(len(batches))
        all_rows = jnp.concatenate([rows[b] for b in order], axis=0)
        all_slope = jnp.concatenate([slope[b] for b in order], axis=0)
        high = all_slope.astype(jnp.bfloat16)
        rest = all_slope - high.astype(jnp.float32)
        middle = rest.astype(jnp.bfloat16)
        low = (rest - middle.astype(jnp.float32)).astype(jnp.bfloat16)
        pieces = jnp.concatenate([high, middle, low], axis=1)
        own_column = jnp.sum(dot(pieces, all_rows, dims=((0,), (0,))), axis=0)
        columns = lax.all_gather(own_column, ("expert", "tensor"))
        router_grad = jnp.sum(columns.reshape(n_expert, n_tensor, width), axis=1).T

        down_grad = dot(
            jnp.concatenate([active[b] for b in order], axis=0),
            jnp.concatenate([cots[b] for b in order], axis=0),
            jnp.bfloat16,
            ((0,), (0,)),
        )[None]
        up_grad = dot(
            all_rows,
            jnp.concatenate([hidden_cot[b] for b in order], axis=0),
            jnp.bfloat16,
            ((0,), (0,)),
        )[None]

        out_wide = out_rows.astype(jnp.float32)
        mixed = (gate[:, None] * out_wide).astype(jnp.bfloat16)
        own_slope = jnp.sum(out_grad.astype(jnp.float32) * out_wide, axis=1) * gate * (1.0 - gate)
        named = dot(chosen.astype(jnp.bfloat16), router, dims=((1,), (1,)))
        token_grad = (cot_rows.astype(jnp.float32) + own_slope[:, None] * named).astype(jnp.bfloat16)
        return (mixed, token_grad, up_grad, down_grad, router_grad)

    return per_device


def solution(mesh):
    in_specs = (
        P(("expert", "tensor"), None),
        P(("expert", "tensor"), None),
        P(("expert", "tensor")),
        P(),
        P("expert", None, "tensor"),
        P("expert", "tensor", None),
        P(("expert", "tensor"), None),
    )
    out_specs = (
        P(("expert", "tensor"), None),
        P(("expert", "tensor"), None),
        P("expert", None, "tensor"),
        P("expert", "tensor", None),
        P(),
    )
    return jax.shard_map(
        make(mesh.shape["expert"], mesh.shape["tensor"]),
        mesh=mesh,
        in_specs=in_specs,
        out_specs=out_specs,
        check_vma=False,
    )
```

```python
import jax
import jax.numpy as jnp
from jax import lax
from jax.sharding import PartitionSpec as P


def dot(a, b, out=jnp.float32, dims=((1,), (0,))):
    return lax.dot_general(a, b, (dims, ((), ())), preferred_element_type=jnp.float32).astype(out)


def joined(blocks):
    return jnp.concatenate(blocks, axis=0)


def after(x, *earlier):
    return lax.optimization_barrier((x,) + earlier)[0]


def added(a, b):
    return (a.astype(jnp.float32) + b.astype(jnp.float32)).astype(jnp.bfloat16)


def make(n_expert, n_tensor):
    pairs = n_expert // 2
    top, low = n_tensor // 2, n_tensor // 2

    def step_pairs(x, step):
        return lax.ppermute(
            x, "expert", [(i, (i + 2 * step) % n_expert) for i in range(n_expert)]
        )

    def to_partner(x):
        return lax.ppermute(x, "expert", [(i, i ^ 1) for i in range(n_expert)])

    def cross(x, bit):
        return lax.ppermute(x, "tensor", [(i, i ^ bit) for i in range(n_tensor)])

    def gather_low(rows):
        held = [rows]
        bit = 1
        while bit < low:
            held = held + [cross(h, bit) for h in held]
            bit *= 2
        return held

    def sum_low(terms):
        while len(terms) > 1:
            bit = len(terms) // 2
            terms = [added(a, cross(b, bit)) for a, b in zip(terms[:bit], terms[bit:])]
        return terms[0]

    def per_device(tokens, expert_ids, live_counts, router, up_weight, down_weight, out_grad):
        tok_rows, width = tokens.shape
        experts = router.shape[1]
        most = 3 * tok_rows // (2 * experts)
        slots = experts * most
        half = slots // 2
        me = lax.axis_index("expert")
        ids = expert_ids[:, 0]
        live = lax.iota(jnp.int32, tok_rows) < live_counts[0]
        chosen = ids[:, None] == lax.iota(jnp.int32, experts)[None, :]
        chosen_int = chosen.astype(jnp.int32)
        rank = jnp.sum(jnp.cumsum(chosen_int, axis=0) * chosen_int, axis=1) - 1
        box = lax.rem(ids // 2 - me // 2 + pairs, pairs) * 2 + (ids + me) % 2
        target = jnp.where(live, box * most + rank, -1)
        placing = (lax.iota(jnp.int32, slots)[:, None] == target[None, :]).astype(jnp.bfloat16)
        w_up = up_weight[0]
        w_down = down_weight[0]

        def pieces(x):
            return [x[s * 2 * most : (s + 1) * 2 * most] for s in range(pairs)]

        def over_pairs(parts):
            return [parts[0]] + [step_pairs(parts[s], s) for s in range(1, pairs)]

        def home_pairs(parts):
            return [parts[0]] + [step_pairs(parts[s], -s) for s in range(1, pairs)]

        def inward(got):
            first = joined([g[:most] for g in got])
            second = to_partner(joined([g[most:] for g in got]))
            return (first, second), (cross(first, top), cross(second, top))

        def outward(first, second):
            back = to_partner(second)
            parts = [
                joined([x[s * most : (s + 1) * most] for x in (first, back)]) for s in range(pairs)
            ]
            return home_pairs(parts), back

        def parts_of(term):
            return [term[i * slots : (i + 1) * slots] for i in range(low)]

        logits = dot(tokens, router)
        gate = jax.nn.sigmoid(jnp.sum(logits * chosen.astype(jnp.float32), axis=1))
        out_cot = (gate[:, None] * out_grad.astype(jnp.float32)).astype(jnp.bfloat16)
        tok_got = over_pairs(pieces(dot(placing, tokens, jnp.bfloat16)))
        cot_box = after(dot(placing, out_cot, jnp.bfloat16), *tok_got[1:])
        cot_got = over_pairs(pieces(cot_box))
        tok_near, tok_far = inward(tok_got)
        cot_near, cot_far = inward(cot_got)

        column = lax.dynamic_slice_in_dim(router, me, 1, axis=1)

        def forward(blocks):
            rows = joined(gather_low(joined(blocks)))
            hidden = dot(rows, w_up)
            active = jax.nn.silu(hidden).astype(jnp.bfloat16)
            return rows, hidden, active, dot(active, w_down, jnp.bfloat16)

        def backward(blocks, rows, hidden, active):
            cots = joined(gather_low(joined(blocks)))
            back = dot(cots, w_down, dims=((1,), (1,)))
            sig = jax.nn.sigmoid(hidden)
            hidden_cot = (back * (sig * (1.0 + hidden * (1.0 - sig)))).astype(jnp.bfloat16)
            off = 1.0 - jax.nn.sigmoid(dot(rows, column))
            slope = jnp.sum(back * active.astype(jnp.float32), axis=1, keepdims=True) * off
            return cots, hidden_cot, slope, dot(hidden_cot, w_up, jnp.bfloat16, ((1,), (1,)))

        far_rows, far_hidden, far_active, far_out = forward(tok_far)
        far_sum = after(sum_low(parts_of(far_out)), *cot_far)
        out_second = cross(far_sum[half:], top)
        out_first = cross(far_sum[:half], top)
        near_rows, near_hidden, near_active, near_out = forward(tok_near)
        near_sum = sum_low(parts_of(near_out))
        out_home, out_back = outward(added(near_sum[:half], out_first), added(near_sum[half:], out_second))

        cot_far = tuple(after(x, near_sum) for x in cot_far)
        far_cots, far_hc, far_slope, far_back = backward(cot_far, far_rows, far_hidden, far_active)
        far_sum = after(sum_low(parts_of(far_back)), out_first)
        cot_second = cross(far_sum[half:], top)
        cot_first = cross(far_sum[:half], top)
        near_cots, near_hc, near_slope, near_back = backward(
            cot_near, near_rows, near_hidden, near_active
        )
        near_sum = sum_low(parts_of(near_back))
        cot_home, _ = outward(
            added(near_sum[:half], cot_first), added(near_sum[half:], cot_second)
        )

        rows = joined([far_rows, near_rows])
        slope = after(joined([far_slope, near_slope]), near_sum, out_back)
        high = slope.astype(jnp.bfloat16)
        rest = slope - high.astype(jnp.float32)
        middle = rest.astype(jnp.bfloat16)
        least = (rest - middle.astype(jnp.float32)).astype(jnp.bfloat16)
        split = jnp.concatenate([high, middle, least], axis=1)
        columns = jnp.sum(dot(split, rows, dims=((0,), (0,))), axis=0, keepdims=True)
        bit = 1
        while bit < n_tensor:
            columns = columns + cross(columns, bit)
            bit *= 2
        bit = 1
        while bit < n_expert:
            came = lax.ppermute(columns, "expert", [(i, i ^ bit) for i in range(n_expert)])
            upper = (me // bit) % 2 == 1
            columns = jnp.where(upper, joined([came, columns]), joined([columns, came]))
            bit *= 2
        router_grad = columns.T

        down_grad = dot(
            after(joined([far_active, near_active]), out_back),
            joined([far_cots, near_cots]),
            jnp.bfloat16,
            ((0,), (0,)),
        )[None]
        up_grad = dot(rows, after(joined([far_hc, near_hc]), out_back), jnp.bfloat16, ((0,), (0,)))[None]

        out_rows = dot(placing, joined(out_home), jnp.bfloat16, ((0,), (0,)))
        cot_rows = dot(placing, joined(cot_home), jnp.bfloat16, ((0,), (0,)))
        out_wide = out_rows.astype(jnp.float32)
        mixed = (gate[:, None] * out_wide).astype(jnp.bfloat16)
        own_slope = jnp.sum(out_grad.astype(jnp.float32) * out_wide, axis=1) * gate * (1.0 - gate)
        named = dot(chosen.astype(jnp.bfloat16), router, dims=((1,), (1,)))
        token_grad = (cot_rows.astype(jnp.float32) + own_slope[:, None] * named).astype(jnp.bfloat16)
        return (mixed, token_grad, up_grad, down_grad, router_grad)

    return per_device


def solution(mesh):
    in_specs = (
        P(("expert", "tensor"), None),
        P(("expert", "tensor"), None),
        P(("expert", "tensor")),
        P(),
        P("expert", None, "tensor"),
        P("expert", "tensor", None),
        P(("expert", "tensor"), None),
    )
    out_specs = (
        P(("expert", "tensor"), None),
        P(("expert", "tensor"), None),
        P("expert", None, "tensor"),
        P("expert", "tensor", None),
        P(),
    )
    return jax.shard_map(
        make(mesh.shape["expert"], mesh.shape["tensor"]),
        mesh=mesh,
        in_specs=in_specs,
        out_specs=out_specs,
        check_vma=False,
    )
```

```python
import jax
import jax.numpy as jnp
from jax import lax
from jax.sharding import PartitionSpec as P


def dot(a, b, out=jnp.float32, dims=((1,), (0,))):
    return lax.dot_general(a, b, (dims, ((), ())), preferred_element_type=jnp.float32).astype(out)


def joined(blocks):
    return jnp.concatenate(blocks, axis=0)


def after(x, *earlier):
    return lax.optimization_barrier((x,) + earlier)[0]


def added(a, b):
    return (a.astype(jnp.float32) + b.astype(jnp.float32)).astype(jnp.bfloat16)


def make(n_expert, n_tensor):
    pairs = n_expert // 2
    top, low = n_tensor // 2, n_tensor // 2

    def step_pairs(x, step):
        return lax.ppermute(
            x, "expert", [(i, (i + 2 * step) % n_expert) for i in range(n_expert)]
        )

    def to_partner(x):
        return lax.ppermute(x, "expert", [(i, i ^ 1) for i in range(n_expert)])

    def cross(x, bit):
        return lax.ppermute(x, "tensor", [(i, i ^ bit) for i in range(n_tensor)])

    def gather_low(rows):
        held = [rows]
        bit = 1
        while bit < low:
            held = held + [cross(h, bit) for h in held]
            bit *= 2
        return held

    def sum_low(terms):
        while len(terms) > 1:
            bit = len(terms) // 2
            terms = [added(a, cross(b, bit)) for a, b in zip(terms[:bit], terms[bit:])]
        return terms[0]

    def per_device(tokens, expert_ids, live_counts, router, up_weight, down_weight, out_grad):
        tok_rows, width = tokens.shape
        experts = router.shape[1]
        most = 3 * tok_rows // (2 * experts)
        slots = experts * most
        half = slots // 2
        me = lax.axis_index("expert")
        ids = expert_ids[:, 0]
        live = lax.iota(jnp.int32, tok_rows) < live_counts[0]
        chosen = ids[:, None] == lax.iota(jnp.int32, experts)[None, :]
        chosen_int = chosen.astype(jnp.int32)
        rank = jnp.sum(jnp.cumsum(chosen_int, axis=0) * chosen_int, axis=1) - 1
        box = lax.rem(ids // 2 - me // 2 + pairs, pairs) * 2 + (ids + me) % 2
        target = jnp.where(live, box * most + rank, -1)
        placing = (lax.iota(jnp.int32, slots)[:, None] == target[None, :]).astype(jnp.bfloat16)
        w_up = up_weight[0]
        w_down = down_weight[0]

        def stay(x):
            return x[: 2 * most]

        def go(x):
            return [x[s * 2 * most : (s + 1) * 2 * most] for s in range(1, pairs)]

        def over_pairs(parts):
            return [step_pairs(part, s) for s, part in enumerate(parts, 1)]

        def home_pairs(parts):
            return [step_pairs(part, -s) for s, part in enumerate(parts, 1)]

        def parts_of(term):
            return [term[i * slots : (i + 1) * slots] for i in range(low)]

        tok_box = dot(placing, tokens, jnp.bfloat16)
        tok_got = over_pairs(go(tok_box))
        logits = dot(tokens, router)
        gate = jax.nn.sigmoid(jnp.sum(logits * chosen.astype(jnp.float32), axis=1))
        out_cot = (gate[:, None] * out_grad.astype(jnp.float32)).astype(jnp.bfloat16)
        cot_box = dot(placing, out_cot, jnp.bfloat16)
        stay_came = to_partner(joined([tok_box[most : 2 * most], cot_box[most : 2 * most]]))
        tok_stay = joined([tok_box[:most], stay_came[:most]])
        cot_stay = joined([cot_box[:most], stay_came[most:]])
        stay_far = cross(joined([tok_stay, cot_stay]), top)
        tok_stay_far, cot_stay_far = stay_far[: 2 * most], stay_far[2 * most :]

        tok_first = joined([g[:most] for g in tok_got])
        tok_second = to_partner(joined([g[most:] for g in tok_got]))
        tok_first_far = cross(after(tok_first, stay_far), top)
        cot_got = over_pairs(go(after(cot_box, *tok_got)))
        tok_second_far = cross(after(tok_second, tok_first_far, cot_got[0]), top)

        column = lax.dynamic_slice_in_dim(router, me, 1, axis=1)

        def forward(blocks):
            rows = joined(gather_low(joined(blocks)))
            hidden = dot(rows, w_up)
            active = jax.nn.silu(hidden).astype(jnp.bfloat16)
            return rows, hidden, active, dot(active, w_down, jnp.bfloat16)

        def backward(blocks, rows, hidden, active):
            cots = joined(gather_low(joined(blocks)))
            back = dot(cots, w_down, dims=((1,), (1,)))
            sig = jax.nn.sigmoid(hidden)
            hidden_cot = (back * (sig * (1.0 + hidden * (1.0 - sig)))).astype(jnp.bfloat16)
            off = 1.0 - jax.nn.sigmoid(dot(rows, column))
            slope = jnp.sum(back * active.astype(jnp.float32), axis=1, keepdims=True) * off
            return cots, hidden_cot, slope, dot(hidden_cot, w_up, jnp.bfloat16, ((1,), (1,)))

        far_rows, far_hidden, far_active, far_out = forward(
            [tok_stay_far, tok_first_far, tok_second_far]
        )
        cot_got = [after(g, tok_second_far) for g in cot_got]
        cot_first = joined([g[:most] for g in cot_got])
        cot_second = to_partner(joined([g[most:] for g in cot_got]))
        cot_first_far = cross(cot_first, top)
        cot_second_far = cross(after(cot_second, cot_first_far), top)

        def share(far_sum, earlier):
            second = cross(after(far_sum[half + most :], earlier), top)
            first = cross(after(far_sum[2 * most : half + most], second), top)
            return first, second

        def outward(near_sum, first, second, earlier=()):
            second = added(near_sum[half + most :], second)
            back = to_partner(after(second, *earlier[:1]))
            first = added(near_sum[2 * most : half + most], first)
            parts = [
                joined([x[s * most : (s + 1) * most] for x in (first, back)])
                for s in range(pairs - 1)
            ]
            return home_pairs([after(part, *earlier) for part in parts]), back

        out_far_sum = sum_low(parts_of(far_out))
        out_first, out_second = share(out_far_sum, cot_second_far)
        near_rows, near_hidden, near_active, near_out = forward([tok_stay, tok_first, tok_second])
        out_near_sum = sum_low(parts_of(near_out))
        out_home, out_back = outward(out_near_sum, out_first, out_second)

        cot_far = [after(x, out_near_sum) for x in (cot_stay_far, cot_first_far, cot_second_far)]
        far_cots, far_hc, far_slope, far_back = backward(cot_far, far_rows, far_hidden, far_active)
        back_far_sum = sum_low(parts_of(far_back))
        back_first, back_second = share(back_far_sum, out_first)
        near_cots, near_hc, near_slope, near_back = backward(
            [cot_stay, cot_first, cot_second], near_rows, near_hidden, near_active
        )
        back_near_sum = sum_low(parts_of(near_back))
        out_pairs = out_home
        back_home, back_back = outward(back_near_sum, back_first, back_second, out_home)
        stay_sums = cross(
            after(joined([out_far_sum[: 2 * most], back_far_sum[: 2 * most]]), back_first), top
        )
        out_stay = added(out_near_sum[: 2 * most], stay_sums[: 2 * most])
        back_stay = added(back_near_sum[: 2 * most], stay_sums[2 * most :])
        stay_home = to_partner(joined([out_stay[most:], back_stay[most:]]))
        out_home = [out_stay[:most], stay_home[:most]] + out_home
        back_home = [back_stay[:most], stay_home[most:]] + back_home

        down_grad = dot(
            after(joined([far_active, near_active]), out_back),
            joined([far_cots, near_cots]),
            jnp.bfloat16,
            ((0,), (0,)),
        )[None]
        rows = joined([far_rows, near_rows])
        up_grad = dot(
            rows, after(joined([far_hc, near_hc]), back_back), jnp.bfloat16, ((0,), (0,))
        )[None]

        slope = after(joined([far_slope, near_slope]), back_second)
        high = slope.astype(jnp.bfloat16)
        rest = slope - high.astype(jnp.float32)
        middle = rest.astype(jnp.bfloat16)
        least = (rest - middle.astype(jnp.float32)).astype(jnp.bfloat16)
        split = jnp.concatenate([high, middle, least], axis=1)
        columns = jnp.sum(dot(split, rows, dims=((0,), (0,))), axis=0, keepdims=True)
        bit = 1
        while bit < n_tensor:
            columns = columns + cross(columns, bit)
            columns = after(columns, down_grad, *([] if bit == 1 else [back_back]))
            bit *= 2
        bit = 1
        while bit < n_expert:
            came = lax.ppermute(columns, "expert", [(i, i ^ bit) for i in range(n_expert)])
            upper = (me // bit) % 2 == 1
            columns = jnp.where(upper, joined([came, columns]), joined([columns, came]))
            bit *= 2
        router_grad = columns.T

        out_rows = dot(placing, joined(out_home), jnp.bfloat16, ((0,), (0,)))
        cot_rows = dot(placing, joined(back_home), jnp.bfloat16, ((0,), (0,)))
        out_wide = out_rows.astype(jnp.float32)
        mixed = (gate[:, None] * out_wide).astype(jnp.bfloat16)
        own_slope = jnp.sum(out_grad.astype(jnp.float32) * out_wide, axis=1) * gate * (1.0 - gate)
        named = dot(chosen.astype(jnp.bfloat16), router, dims=((1,), (1,)))
        token_grad = (cot_rows.astype(jnp.float32) + own_slope[:, None] * named).astype(jnp.bfloat16)
        return (mixed, token_grad, up_grad, down_grad, router_grad)

    return per_device


def solution(mesh):
    in_specs = (
        P(("expert", "tensor"), None),
        P(("expert", "tensor"), None),
        P(("expert", "tensor")),
        P(),
        P("expert", None, "tensor"),
        P("expert", "tensor", None),
        P(("expert", "tensor"), None),
    )
    out_specs = (
        P(("expert", "tensor"), None),
        P(("expert", "tensor"), None),
        P("expert", None, "tensor"),
        P("expert", "tensor", None),
        P(),
    )
    return jax.shard_map(
        make(mesh.shape["expert"], mesh.shape["tensor"]),
        mesh=mesh,
        in_specs=in_specs,
        out_specs=out_specs,
        check_vma=False,
    )
```

```python
import jax
import jax.numpy as jnp
from jax import lax
from jax.sharding import PartitionSpec as P


def dot(a, b, out=jnp.float32, dims=((1,), (0,))):
    return lax.dot_general(a, b, (dims, ((), ())), preferred_element_type=jnp.float32).astype(out)


def joined(blocks):
    return jnp.concatenate(blocks, axis=0)


def after(x, *earlier):
    return lax.optimization_barrier((x,) + earlier)[0]


def added(a, b):
    return (a.astype(jnp.float32) + b.astype(jnp.float32)).astype(jnp.bfloat16)


def make(n_expert, n_tensor):
    pairs = n_expert // 2
    top, low = n_tensor // 2, n_tensor // 2

    def step_pairs(x, step):
        return lax.ppermute(
            x, "expert", [(i, (i + 2 * step) % n_expert) for i in range(n_expert)]
        )

    def to_partner(x):
        return lax.ppermute(x, "expert", [(i, i ^ 1) for i in range(n_expert)])

    def cross(x, bit):
        return lax.ppermute(x, "tensor", [(i, i ^ bit) for i in range(n_tensor)])

    def gather_low(rows):
        held = [rows]
        bit = 1
        while bit < low:
            held = held + [cross(h, bit) for h in held]
            bit *= 2
        return held

    def sum_low(terms):
        while len(terms) > 1:
            bit = len(terms) // 2
            terms = [added(a, cross(b, bit)) for a, b in zip(terms[:bit], terms[bit:])]
        return terms[0]

    def per_device(tokens, expert_ids, live_counts, router, up_weight, down_weight, out_grad):
        tok_rows, width = tokens.shape
        experts = router.shape[1]
        most = 3 * tok_rows // (2 * experts)
        slots = experts * most
        half = slots // 2
        me = lax.axis_index("expert")
        ids = expert_ids[:, 0]
        live = lax.iota(jnp.int32, tok_rows) < live_counts[0]
        chosen = ids[:, None] == lax.iota(jnp.int32, experts)[None, :]
        chosen_int = chosen.astype(jnp.int32)
        rank = jnp.sum(jnp.cumsum(chosen_int, axis=0) * chosen_int, axis=1) - 1
        box = lax.rem(ids // 2 - me // 2 + pairs, pairs) * 2 + (ids + me) % 2
        target = jnp.where(live, box * most + rank, -1)
        placing = (lax.iota(jnp.int32, slots)[:, None] == target[None, :]).astype(jnp.bfloat16)
        w_up = up_weight[0]
        w_down = down_weight[0]

        def stay(x):
            return x[: 2 * most]

        def go(x):
            return [x[s * 2 * most : (s + 1) * 2 * most] for s in range(1, pairs)]

        def over_pairs(parts):
            return [step_pairs(part, s) for s, part in enumerate(parts, 1)]

        def home_pairs(parts):
            return [step_pairs(part, -s) for s, part in enumerate(parts, 1)]

        tok_box = dot(placing, tokens, jnp.bfloat16)
        tok_got = over_pairs(go(tok_box))
        logits = dot(tokens, router)
        gate = jax.nn.sigmoid(jnp.sum(logits * chosen.astype(jnp.float32), axis=1))
        out_cot = (gate[:, None] * out_grad.astype(jnp.float32)).astype(jnp.bfloat16)
        cot_box = dot(placing, out_cot, jnp.bfloat16)
        stay_came = to_partner(joined([tok_box[most : 2 * most], cot_box[most : 2 * most]]))
        tok_stay = joined([tok_box[:most], stay_came[:most]])
        cot_stay = joined([cot_box[:most], stay_came[most:]])
        stay_far = cross(after(joined([tok_stay, cot_stay]), tok_got[0]), top)
        tok_stay_far, cot_stay_far = stay_far[: 2 * most], stay_far[2 * most :]

        tok_got = [after(g, stay_far) for g in tok_got]
        tok_first = joined([g[:most] for g in tok_got])
        tok_second = to_partner(joined([g[most:] for g in tok_got]))
        tok_first_far = cross(tok_first, top)
        cot_got = over_pairs(go(after(cot_box, *tok_got)))
        tok_second_far = cross(after(tok_second, tok_first_far, cot_got[0]), top)
        tok_far = joined([tok_stay_far, tok_first_far, after(tok_second_far, *cot_got)])
        cot_got = [after(g, tok_second_far) for g in cot_got]
        cot_first = joined([g[:most] for g in cot_got])
        cot_second = to_partner(joined([g[most:] for g in cot_got]))
        cot_first_far = cross(cot_first, top)

        column = lax.dynamic_slice_in_dim(router, me, 1, axis=1)

        def forward(rows):
            hidden = dot(rows, w_up)
            active = jax.nn.silu(hidden).astype(jnp.bfloat16)
            hidden, active = lax.optimization_barrier((hidden, active))
            return hidden, active, dot(active, w_down, jnp.bfloat16)

        def backward(cots, hidden, active):
            back = dot(cots, w_down, dims=((1,), (1,)))
            sig = jax.nn.sigmoid(hidden)
            hidden_cot = (back * (sig * (1.0 + hidden * (1.0 - sig)))).astype(jnp.bfloat16)
            slope = jnp.sum(back * active.astype(jnp.float32), axis=1, keepdims=True)
            return hidden_cot, slope, dot(hidden_cot, w_up, jnp.bfloat16, ((1,), (1,)))

        def share(far_sum, earlier):
            second = cross(after(far_sum[half + most :], earlier), top)
            first = cross(after(far_sum[2 * most : half + most], second), top)
            return first, second

        def partner_back(near_sum, second, *earlier):
            return to_partner(after(added(near_sum[half + most :], second), *earlier))

        def outward(near_sum, first, back, *earlier):
            first = added(near_sum[2 * most : half + most], first)
            parts = [
                joined([x[s * most : (s + 1) * most] for x in (first, back)])
                for s in range(pairs - 1)
            ]
            return home_pairs([after(part, *earlier) for part in parts])

        def last_after(terms, *earlier):
            return terms[:1] + [after(t, *earlier) for t in terms[1:]]

        rows = gather_low(tok_far)
        hidden, active, term = map(list, zip(*[forward(r) for r in rows]))
        out_far_sum = sum_low(last_after(term, cot_first_far, cot_second))
        cot_second_far = cross(after(cot_second, cot_first_far), top)
        out_first, out_second = share(out_far_sum, cot_second_far)
        near = gather_low(joined([tok_stay, tok_first, tok_second]))
        near_hidden, near_active, term = map(list, zip(*[forward(r) for r in near]))
        rows, hidden, active = rows + near, hidden + near_hidden, active + near_active
        out_near_sum = sum_low(term)
        out_back = partner_back(out_near_sum, out_second)
        out_home = outward(out_near_sum, out_first, out_back)

        cots = gather_low(joined([cot_stay_far, cot_first_far, after(cot_second_far, *term)]))
        hidden_cot, slope, term = map(
            list, zip(*[backward(*a) for a in zip(cots, hidden[:low], active[:low])])
        )
        back_far_sum = sum_low(last_after(term, out_second))
        back_first, back_second = share(back_far_sum, out_first)
        near = gather_low(joined([cot_stay, cot_first, cot_second]))
        near_hidden_cot, near_slope, term = map(
            list, zip(*[backward(*a) for a in zip(near, hidden[low:], active[low:])])
        )
        cots, hidden_cot, slope = cots + near, hidden_cot + near_hidden_cot, slope + near_slope
        back_near_sum = sum_low(last_after(term, out_first, out_back))
        stay_sums = cross(
            after(joined([out_far_sum[: 2 * most], back_far_sum[: 2 * most]]), back_first), top
        )

        back_back = partner_back(back_near_sum, back_second, out_home[0])
        back_home = outward(back_near_sum, back_first, back_back, *out_home, stay_sums)

        rows, hidden_cot, slope = (
            joined([after(x, out_home[0], back_second) for x in xs])
            for xs in (rows, hidden_cot, slope)
        )
        up_grad = dot(rows, hidden_cot, jnp.bfloat16, ((0,), (0,)))[None]
        active, cots = (
            joined([after(x, out_home[1], back_first, back_back) for x in xs])
            for xs in (active, cots)
        )
        down_grad = dot(active, cots, jnp.bfloat16, ((0,), (0,)))[None]

        slope = slope * (1.0 - jax.nn.sigmoid(dot(rows, column)))
        high = slope.astype(jnp.bfloat16)
        rest = slope - high.astype(jnp.float32)
        middle = rest.astype(jnp.bfloat16)
        least = (rest - middle.astype(jnp.float32)).astype(jnp.bfloat16)
        split = jnp.concatenate([high, middle, least], axis=1)
        columns = jnp.sum(dot(split, rows, dims=((0,), (0,))), axis=0, keepdims=True)
        bit = 1
        while bit < n_tensor:
            columns = columns + cross(columns, bit)
            columns = after(columns, up_grad if bit == 1 else down_grad)
            bit *= 2
        bit = 1
        while bit < n_expert:
            came = lax.ppermute(columns, "expert", [(i, i ^ bit) for i in range(n_expert)])
            upper = (me // bit) % 2 == 1
            columns = jnp.where(upper, joined([came, columns]), joined([columns, came]))
            columns = after(columns, back_home[0])
            bit *= 2
        router_grad = columns.T

        out_stay = added(out_near_sum[: 2 * most], stay_sums[: 2 * most])
        back_stay = added(back_near_sum[: 2 * most], stay_sums[2 * most :])
        stay_home = to_partner(joined([out_stay[most:], back_stay[most:]]))
        out_home = [out_stay[:most], stay_home[:most]] + out_home
        back_home = [back_stay[:most], stay_home[most:]] + [after(x, columns) for x in back_home]

        out_rows = dot(placing, joined(out_home), jnp.bfloat16, ((0,), (0,)))
        cot_rows = dot(placing, joined(back_home), jnp.bfloat16, ((0,), (0,)))
        out_wide = out_rows.astype(jnp.float32)
        mixed = (gate[:, None] * out_wide).astype(jnp.bfloat16)
        own_slope = jnp.sum(out_grad.astype(jnp.float32) * out_wide, axis=1) * gate * (1.0 - gate)
        named = dot(chosen.astype(jnp.bfloat16), router, dims=((1,), (1,)))
        token_grad = (cot_rows.astype(jnp.float32) + own_slope[:, None] * named).astype(jnp.bfloat16)
        return (mixed, token_grad, up_grad, down_grad, router_grad)

    return per_device


def solution(mesh):
    in_specs = (
        P(("expert", "tensor"), None),
        P(("expert", "tensor"), None),
        P(("expert", "tensor")),
        P(),
        P("expert", None, "tensor"),
        P("expert", "tensor", None),
        P(("expert", "tensor"), None),
    )
    out_specs = (
        P(("expert", "tensor"), None),
        P(("expert", "tensor"), None),
        P("expert", None, "tensor"),
        P("expert", "tensor", None),
        P(),
    )
    return jax.shard_map(
        make(mesh.shape["expert"], mesh.shape["tensor"]),
        mesh=mesh,
        in_specs=in_specs,
        out_specs=out_specs,
        check_vma=False,
    )
```

```python
import jax
import jax.numpy as jnp
from jax import lax
from jax.sharding import PartitionSpec as P


def dot(a, b, out=jnp.float32, dims=((1,), (0,))):
    return lax.dot_general(a, b, (dims, ((), ())), preferred_element_type=jnp.float32).astype(out)


def joined(blocks):
    return jnp.concatenate(blocks, axis=0)


def after(x, *earlier):
    return lax.optimization_barrier((x,) + earlier)[0]


def added(a, b):
    return (a.astype(jnp.float32) + b.astype(jnp.float32)).astype(jnp.bfloat16)


def make(n_expert, n_tensor):
    pairs = n_expert // 2
    top, low = n_tensor // 2, n_tensor // 2

    def step_pairs(x, step):
        return lax.ppermute(
            x, "expert", [(i, (i + 2 * step) % n_expert) for i in range(n_expert)]
        )

    def to_partner(x):
        return lax.ppermute(x, "expert", [(i, i ^ 1) for i in range(n_expert)])

    def cross(x, bit):
        return lax.ppermute(x, "tensor", [(i, i ^ bit) for i in range(n_tensor)])

    def gather_low(rows):
        held = [rows]
        bit = 1
        while bit < low:
            held = held + [cross(h, bit) for h in held]
            bit *= 2
        return held

    def sum_low(terms):
        while len(terms) > 1:
            bit = len(terms) // 2
            terms = [added(a, cross(b, bit)) for a, b in zip(terms[:bit], terms[bit:])]
        return terms[0]

    def per_device(tokens, expert_ids, live_counts, router, up_weight, down_weight, out_grad):
        tok_rows, width = tokens.shape
        experts = router.shape[1]
        most = 3 * tok_rows // (2 * experts)
        slots = experts * most
        half = slots // 2
        me = lax.axis_index("expert")
        ids = expert_ids[:, 0]
        live = lax.iota(jnp.int32, tok_rows) < live_counts[0]
        chosen = ids[:, None] == lax.iota(jnp.int32, experts)[None, :]
        chosen_int = chosen.astype(jnp.int32)
        rank = jnp.sum(jnp.cumsum(chosen_int, axis=0) * chosen_int, axis=1) - 1
        box = lax.rem(ids // 2 - me // 2 + pairs, pairs) * 2 + (ids + me) % 2
        target = jnp.where(live, box * most + rank, -1)
        placing = (lax.iota(jnp.int32, slots)[:, None] == target[None, :]).astype(jnp.bfloat16)
        w_up = up_weight[0]
        w_down = down_weight[0]

        def stay(x):
            return x[: 2 * most]

        def go(x):
            return [x[s * 2 * most : (s + 1) * 2 * most] for s in range(1, pairs)]

        def over_pairs(parts):
            return [step_pairs(part, s) for s, part in enumerate(parts, 1)]

        def home_pairs(parts):
            return [step_pairs(part, -s) for s, part in enumerate(parts, 1)]

        tok_box = dot(placing, tokens, jnp.bfloat16)
        tok_got = over_pairs(go(tok_box))
        logits = dot(tokens, router)
        gate = jax.nn.sigmoid(jnp.sum(logits * chosen.astype(jnp.float32), axis=1))
        out_cot = (gate[:, None] * out_grad.astype(jnp.float32)).astype(jnp.bfloat16)
        cot_box = dot(placing, out_cot, jnp.bfloat16)
        stay_sent = joined([tok_box[most : 2 * most], cot_box[most : 2 * most]])
        stay_came = to_partner(after(stay_sent, tok_got[0]))
        tok_stay = joined([tok_box[:most], stay_came[:most]])
        cot_stay = joined([cot_box[:most], stay_came[most:]])
        stay_far = cross(after(joined([tok_stay, cot_stay]), tok_got[1]), top)
        tok_stay_far, cot_stay_far = stay_far[: 2 * most], stay_far[2 * most :]

        tok_got = [after(g, stay_far) for g in tok_got]
        tok_first = joined([g[:most] for g in tok_got])
        tok_second = to_partner(joined([g[most:] for g in tok_got]))
        tok_first_far = cross(tok_first, top)
        cot_got = over_pairs(go(after(cot_box, *tok_got)))
        tok_second_far = cross(after(tok_second, tok_first_far, cot_got[0]), top)
        tok_far = joined([tok_stay_far, tok_first_far, after(tok_second_far, cot_got[1])])
        cot_got = [after(g, tok_second_far) for g in cot_got]
        cot_first = joined([g[:most] for g in cot_got])
        cot_second = to_partner(joined([g[most:] for g in cot_got]))
        cot_first_far = cross(cot_first, top)

        column = lax.dynamic_slice_in_dim(router, me, 1, axis=1)

        def forward(rows):
            hidden = dot(rows, w_up)
            active = jax.nn.silu(hidden).astype(jnp.bfloat16)
            hidden, active = lax.optimization_barrier((hidden, active))
            return hidden, active, dot(active, w_down, jnp.bfloat16)

        def backward(cots, hidden, active):
            back = dot(cots, w_down, dims=((1,), (1,)))
            sig = jax.nn.sigmoid(hidden)
            hidden_cot = (back * (sig * (1.0 + hidden * (1.0 - sig)))).astype(jnp.bfloat16)
            slope = jnp.sum(back * active.astype(jnp.float32), axis=1, keepdims=True)
            return hidden_cot, slope, dot(hidden_cot, w_up, jnp.bfloat16, ((1,), (1,)))

        def share(far_sum, earlier):
            second = cross(after(far_sum[half + most :], earlier), top)
            first = cross(after(far_sum[2 * most : half + most], second), top)
            return first, second

        def partner_back(near_sum, second, *earlier):
            return to_partner(after(added(near_sum[half + most :], second), *earlier))

        def outward(near_sum, first, back, *earlier):
            first = added(near_sum[2 * most : half + most], first)
            parts = [
                joined([x[s * most : (s + 1) * most] for x in (first, back)])
                for s in range(pairs - 1)
            ]
            return home_pairs([after(part, *earlier) for part in parts])

        def last_after(terms, *earlier):
            return terms[:1] + [after(t, *earlier) for t in terms[1:]]

        rows = gather_low(tok_far)
        hidden, active, term = map(list, zip(*[forward(r) for r in rows]))
        out_far_sum = sum_low(last_after(term, cot_first_far, cot_second))
        cot_second_far = cross(after(cot_second, cot_first_far), top)
        out_first, out_second = share(out_far_sum, cot_second_far)
        near = gather_low(joined([tok_stay, tok_first, tok_second]))
        near_hidden, near_active, term = map(list, zip(*[forward(r) for r in near]))
        rows, hidden, active = rows + near, hidden + near_hidden, active + near_active
        out_near_sum = sum_low(term)
        out_back = partner_back(out_near_sum, out_second)
        out_home = outward(out_near_sum, out_first, out_back)

        cots = gather_low(joined([cot_stay_far, cot_first_far, after(cot_second_far, *term)]))
        hidden_cot, slope, term = map(
            list, zip(*[backward(*a) for a in zip(cots, hidden[:low], active[:low])])
        )
        back_far_sum = sum_low(last_after(term, out_second))
        back_first, back_second = share(back_far_sum, out_first)
        near = gather_low(after(joined([cot_stay, cot_first, cot_second]), out_second))
        near_hidden_cot, near_slope, term = map(
            list, zip(*[backward(*a) for a in zip(near, hidden[low:], active[low:])])
        )
        cots, hidden_cot, slope = cots + near, hidden_cot + near_hidden_cot, slope + near_slope
        back_near_sum = sum_low(last_after(term, out_first, out_back))
        stay_sums = cross(
            after(
                joined([out_far_sum[: 2 * most], back_far_sum[: 2 * most]]), back_first, out_home[1]
            ),
            top,
        )

        back_back = partner_back(back_near_sum, back_second, out_home[0])
        back_home = outward(back_near_sum, back_first, back_back, *out_home, stay_sums)

        rows, hidden_cot, slope = (
            joined([after(x, back_first, back_back) for x in xs])
            for xs in (rows, hidden_cot, slope)
        )
        up_grad = dot(rows, hidden_cot, jnp.bfloat16, ((0,), (0,)))[None]
        active, cots = (
            joined([after(x, back_home[1]) for x in xs])
            for xs in (active, cots)
        )
        down_grad = dot(active, cots, jnp.bfloat16, ((0,), (0,)))[None]

        slope = slope * (1.0 - jax.nn.sigmoid(dot(rows, column)))
        high = slope.astype(jnp.bfloat16)
        rest = slope - high.astype(jnp.float32)
        middle = rest.astype(jnp.bfloat16)
        least = (rest - middle.astype(jnp.float32)).astype(jnp.bfloat16)
        split = jnp.concatenate([high, middle, least], axis=1)
        columns = jnp.sum(dot(split, rows, dims=((0,), (0,))), axis=0, keepdims=True)
        bit = 1
        while bit < n_tensor:
            columns = columns + cross(columns, bit)
            columns = after(columns, up_grad)
            bit *= 2
        bit = 1
        while bit < n_expert:
            came = lax.ppermute(columns, "expert", [(i, i ^ bit) for i in range(n_expert)])
            upper = (me // bit) % 2 == 1
            columns = jnp.where(upper, joined([came, columns]), joined([columns, came]))
            columns = after(columns, back_home[0])
            bit *= 2
        router_grad = columns.T

        out_stay = added(out_near_sum[: 2 * most], stay_sums[: 2 * most])
        back_stay = added(back_near_sum[: 2 * most], stay_sums[2 * most :])
        stay_home = to_partner(joined([out_stay[most:], back_stay[most:]]))
        out_home = [out_stay[:most], stay_home[:most]] + out_home
        back_home = [back_stay[:most], stay_home[most:]] + [after(x, columns) for x in back_home]

        out_rows = dot(placing, joined(out_home), jnp.bfloat16, ((0,), (0,)))
        cot_rows = dot(placing, joined(back_home), jnp.bfloat16, ((0,), (0,)))
        out_wide = out_rows.astype(jnp.float32)
        mixed = (gate[:, None] * out_wide).astype(jnp.bfloat16)
        own_slope = jnp.sum(out_grad.astype(jnp.float32) * out_wide, axis=1) * gate * (1.0 - gate)
        named = dot(chosen.astype(jnp.bfloat16), router, dims=((1,), (1,)))
        token_grad = (cot_rows.astype(jnp.float32) + own_slope[:, None] * named).astype(jnp.bfloat16)
        return (mixed, token_grad, up_grad, down_grad, router_grad)

    return per_device


def solution(mesh):
    in_specs = (
        P(("expert", "tensor"), None),
        P(("expert", "tensor"), None),
        P(("expert", "tensor")),
        P(),
        P("expert", None, "tensor"),
        P("expert", "tensor", None),
        P(("expert", "tensor"), None),
    )
    out_specs = (
        P(("expert", "tensor"), None),
        P(("expert", "tensor"), None),
        P("expert", None, "tensor"),
        P("expert", "tensor", None),
        P(),
    )
    return jax.shard_map(
        make(mesh.shape["expert"], mesh.shape["tensor"]),
        mesh=mesh,
        in_specs=in_specs,
        out_specs=out_specs,
        check_vma=False,
    )
```

```python
import jax
import jax.numpy as jnp
from jax import lax
from jax.sharding import PartitionSpec as P


def dot(a, b, out=jnp.float32, dims=((1,), (0,))):
    return lax.dot_general(a, b, (dims, ((), ())), preferred_element_type=jnp.float32).astype(out)


def joined(blocks):
    return jnp.concatenate(blocks, axis=0)


def after(x, *earlier):
    return lax.optimization_barrier((x,) + earlier)[0]


def added(a, b):
    return (a.astype(jnp.float32) + b.astype(jnp.float32)).astype(jnp.bfloat16)


def make(n_expert, n_tensor):
    top, low = n_tensor // 2, n_tensor // 2

    def cross(x, bit):
        return lax.ppermute(x, "tensor", [(i, i ^ bit) for i in range(n_tensor)])

    def gather_low(rows):
        held = [rows]
        bit = 1
        while bit < low:
            held = held + [cross(h, bit) for h in held]
            bit *= 2
        return held

    def sum_low(terms):
        while len(terms) > 1:
            bit = len(terms) // 2
            terms = [added(a, cross(b, bit)) for a, b in zip(terms[:bit], terms[bit:])]
        return terms[0]

    def per_device(tokens, expert_ids, live_counts, router, up_weight, down_weight, out_grad):
        tok_rows, width = tokens.shape
        experts = router.shape[1]
        most = 3 * tok_rows // (2 * experts)
        slots = experts * most
        me = lax.axis_index("expert")
        ids = expert_ids[:, 0]
        live = lax.iota(jnp.int32, tok_rows) < live_counts[0]
        chosen = ids[:, None] == lax.iota(jnp.int32, experts)[None, :]
        chosen_int = chosen.astype(jnp.int32)
        rank = jnp.sum(jnp.cumsum(chosen_int, axis=0) * chosen_int, axis=1) - 1
        target = jnp.where(live, ids * most + rank, -1)
        placing = (lax.iota(jnp.int32, slots)[:, None] == target[None, :]).astype(jnp.bfloat16)
        w_up = up_weight[0]
        w_down = down_weight[0]

        def exchange(x):
            x = x.reshape(experts, most, width)
            x = lax.all_to_all(x, "expert", split_axis=0, concat_axis=0, tiled=True)
            return x.reshape(slots, width)

        tok_near = exchange(dot(placing, tokens, jnp.bfloat16))
        logits = dot(tokens, router)
        gate = jax.nn.sigmoid(jnp.sum(logits * chosen.astype(jnp.float32), axis=1))
        out_cot = (gate[:, None] * out_grad.astype(jnp.float32)).astype(jnp.bfloat16)
        cot_near = exchange(after(dot(placing, out_cot, jnp.bfloat16), tok_near))
        tok_far = cross(tok_near, top)
        cot_far = cross(cot_near, top)

        column = lax.dynamic_slice_in_dim(router, me, 1, axis=1)

        def forward(rows):
            hidden = dot(rows, w_up)
            active = jax.nn.silu(hidden).astype(jnp.bfloat16)
            hidden, active = lax.optimization_barrier((hidden, active))
            return hidden, active, dot(active, w_down, jnp.bfloat16)

        def backward(cots, hidden, active):
            back = dot(cots, w_down, dims=((1,), (1,)))
            sig = jax.nn.sigmoid(hidden)
            hidden_cot = (back * (sig * (1.0 + hidden * (1.0 - sig)))).astype(jnp.bfloat16)
            slope = jnp.sum(back * active.astype(jnp.float32), axis=1, keepdims=True)
            return hidden_cot, slope, dot(hidden_cot, w_up, jnp.bfloat16, ((1,), (1,)))

        rows = gather_low(tok_far)
        hidden, active, term = map(list, zip(*[forward(r) for r in rows]))
        out_far = cross(after(sum_low(term), cot_far), top)
        near = gather_low(tok_near)
        near_hidden, near_active, term = map(list, zip(*[forward(r) for r in near]))
        rows, hidden, active = rows + near, hidden + near_hidden, active + near_active
        out_near = sum_low(term)

        cots = gather_low(after(cot_far, *term))
        hidden_cot, slope, term = map(
            list, zip(*[backward(*a) for a in zip(cots, hidden[:low], active[:low])])
        )
        back_far = cross(after(sum_low(term), out_far), top)
        near = gather_low(cot_near)
        near_hidden_cot, near_slope, term = map(
            list, zip(*[backward(*a) for a in zip(near, hidden[low:], active[low:])])
        )
        cots, hidden_cot, slope = cots + near, hidden_cot + near_hidden_cot, slope + near_slope
        back_near = sum_low(term)

        out_sum = added(out_near, out_far)
        out_home = exchange(out_sum)
        back_home = exchange(after(added(back_near, back_far), out_home))

        rows, hidden_cot, slope, active, cots = (
            joined([after(x, out_home) for x in xs]) for xs in (rows, hidden_cot, slope, active, cots)
        )
        up_grad = dot(rows, hidden_cot, jnp.bfloat16, ((0,), (0,)))[None]
        down_grad = dot(active, cots, jnp.bfloat16, ((0,), (0,)))[None]

        slope = slope * (1.0 - jax.nn.sigmoid(dot(rows, column)))
        high = slope.astype(jnp.bfloat16)
        rest = slope - high.astype(jnp.float32)
        middle = rest.astype(jnp.bfloat16)
        least = (rest - middle.astype(jnp.float32)).astype(jnp.bfloat16)
        split = jnp.concatenate([high, middle, least], axis=1)
        columns = jnp.sum(dot(split, rows, dims=((0,), (0,))), axis=0, keepdims=True)
        bit = 1
        while bit < n_tensor:
            columns = columns + cross(columns, bit)
            bit *= 2
        bit = 1
        while bit < n_expert:
            came = lax.ppermute(columns, "expert", [(i, i ^ bit) for i in range(n_expert)])
            upper = (me // bit) % 2 == 1
            columns = jnp.where(upper, joined([came, columns]), joined([columns, came]))
            bit *= 2
        router_grad = columns.T

        out_rows = dot(placing, out_home, jnp.bfloat16, ((0,), (0,)))
        cot_rows = dot(placing, back_home, jnp.bfloat16, ((0,), (0,)))
        out_wide = out_rows.astype(jnp.float32)
        mixed = (gate[:, None] * out_wide).astype(jnp.bfloat16)
        own_slope = jnp.sum(out_grad.astype(jnp.float32) * out_wide, axis=1) * gate * (1.0 - gate)
        named = dot(chosen.astype(jnp.bfloat16), router, dims=((1,), (1,)))
        token_grad = (cot_rows.astype(jnp.float32) + own_slope[:, None] * named).astype(jnp.bfloat16)
        return (mixed, token_grad, up_grad, down_grad, router_grad)

    return per_device


def solution(mesh):
    in_specs = (
        P(("expert", "tensor"), None),
        P(("expert", "tensor"), None),
        P(("expert", "tensor")),
        P(),
        P("expert", None, "tensor"),
        P("expert", "tensor", None),
        P(("expert", "tensor"), None),
    )
    out_specs = (
        P(("expert", "tensor"), None),
        P(("expert", "tensor"), None),
        P("expert", None, "tensor"),
        P("expert", "tensor", None),
        P(),
    )
    return jax.shard_map(
        make(mesh.shape["expert"], mesh.shape["tensor"]),
        mesh=mesh,
        in_specs=in_specs,
        out_specs=out_specs,
        check_vma=False,
    )
```

```python
import jax
import jax.numpy as jnp
from jax import lax
from jax.sharding import PartitionSpec as P


def dot(a, b, out=jnp.float32, dims=((1,), (0,))):
    return lax.dot_general(a, b, (dims, ((), ())), preferred_element_type=jnp.float32).astype(out)


def joined(blocks):
    return jnp.concatenate(blocks, axis=0)


def after(x, *earlier):
    return lax.optimization_barrier((x,) + earlier)[0]


def added(a, b):
    return (a.astype(jnp.float32) + b.astype(jnp.float32)).astype(jnp.bfloat16)


def make(n_expert, n_tensor):
    top, low = n_tensor // 2, n_tensor // 2

    def cross(x, bit):
        return lax.ppermute(x, "tensor", [(i, i ^ bit) for i in range(n_tensor)])

    def gather_low(rows):
        held = [rows]
        bit = 1
        while bit < low:
            held = held + [cross(h, bit) for h in held]
            bit *= 2
        return held

    def sum_low(terms):
        while len(terms) > 1:
            bit = len(terms) // 2
            terms = [added(a, cross(b, bit)) for a, b in zip(terms[:bit], terms[bit:])]
        return terms[0]

    def per_device(tokens, expert_ids, live_counts, router, up_weight, down_weight, out_grad):
        tok_rows, width = tokens.shape
        experts = router.shape[1]
        most = 3 * tok_rows // (2 * experts)
        slots = experts * most
        me = lax.axis_index("expert")
        ids = expert_ids[:, 0]
        live = lax.iota(jnp.int32, tok_rows) < live_counts[0]
        chosen = ids[:, None] == lax.iota(jnp.int32, experts)[None, :]
        chosen_int = chosen.astype(jnp.int32)
        rank = jnp.sum(jnp.cumsum(chosen_int, axis=0) * chosen_int, axis=1) - 1
        target = jnp.where(live, ids * most + rank, -1)
        placing = (lax.iota(jnp.int32, slots)[:, None] == target[None, :]).astype(jnp.bfloat16)
        w_up = up_weight[0]
        w_down = down_weight[0]

        def exchange(x):
            x = x.reshape(experts, most, width)
            x = lax.all_to_all(x, "expert", split_axis=0, concat_axis=0, tiled=True)
            return x.reshape(slots, width)

        tok_near = exchange(dot(placing, tokens, jnp.bfloat16))
        logits = dot(tokens, router)
        gate = jax.nn.sigmoid(jnp.sum(logits * chosen.astype(jnp.float32), axis=1))
        out_cot = (gate[:, None] * out_grad.astype(jnp.float32)).astype(jnp.bfloat16)
        cot_near = exchange(after(dot(placing, out_cot, jnp.bfloat16), tok_near))
        tok_far = cross(tok_near, top)
        cot_far = cross(cot_near, top)

        column = lax.dynamic_slice_in_dim(router, me, 1, axis=1)

        def forward(rows):
            hidden = dot(rows, w_up)
            active = jax.nn.silu(hidden).astype(jnp.bfloat16)
            hidden, active = lax.optimization_barrier((hidden, active))
            return hidden, active, dot(active, w_down, jnp.bfloat16)

        def backward(cots, hidden, active):
            back = dot(cots, w_down, dims=((1,), (1,)))
            sig = jax.nn.sigmoid(hidden)
            hidden_cot = (back * (sig * (1.0 + hidden * (1.0 - sig)))).astype(jnp.bfloat16)
            slope = jnp.sum(back * active.astype(jnp.float32), axis=1, keepdims=True)
            return hidden_cot, slope, dot(hidden_cot, w_up, jnp.bfloat16, ((1,), (1,)))

        rows = gather_low(after(tok_far, cot_near))
        hidden, active, term = map(list, zip(*[forward(r) for r in rows]))
        out_far = cross(after(sum_low(term), cot_far), top)
        near = gather_low(tok_near)
        near_hidden, near_active, term = map(list, zip(*[forward(r) for r in near]))
        rows, hidden, active = rows + near, hidden + near_hidden, active + near_active
        out_near = sum_low(term)

        cots = gather_low(after(cot_far, *term))
        hidden_cot, slope, term = map(
            list, zip(*[backward(*a) for a in zip(cots, hidden[:low], active[:low])])
        )
        back_far_sum = sum_low(term)
        back_far = cross(after(back_far_sum, out_far), top)
        near = gather_low(cot_near)
        near_hidden_cot, near_slope, term = map(
            list, zip(*[backward(*a) for a in zip(near, hidden[low:], active[low:])])
        )
        cots, hidden_cot, slope = cots + near, hidden_cot + near_hidden_cot, slope + near_slope
        back_near = sum_low(term)

        out_sum = added(out_near, out_far)
        out_home = exchange(after(out_sum, back_far_sum, back_near))

        rows, hidden_cot, slope, active, cots = (
            joined([after(x, out_sum) for x in xs]) for xs in (rows, hidden_cot, slope, active, cots)
        )
        up_grad = dot(rows, hidden_cot, jnp.bfloat16, ((0,), (0,)))[None]
        down_grad = dot(active, cots, jnp.bfloat16, ((0,), (0,)))[None]

        slope = slope * (1.0 - jax.nn.sigmoid(dot(rows, column)))
        high = slope.astype(jnp.bfloat16)
        rest = slope - high.astype(jnp.float32)
        middle = rest.astype(jnp.bfloat16)
        least = (rest - middle.astype(jnp.float32)).astype(jnp.bfloat16)
        split = jnp.concatenate([high, middle, least], axis=1)
        columns = jnp.sum(dot(split, rows, dims=((0,), (0,))), axis=0, keepdims=True)
        bit = 1
        while bit < n_tensor:
            columns = columns + cross(columns, bit)
            bit *= 2
        bit = 1
        while bit < n_expert:
            came = lax.ppermute(columns, "expert", [(i, i ^ bit) for i in range(n_expert)])
            upper = (me // bit) % 2 == 1
            columns = jnp.where(upper, joined([came, columns]), joined([columns, came]))
            bit *= 2
        router_grad = columns.T
        back_home = exchange(after(added(back_near, back_far), out_home, columns))

        out_rows = dot(placing, out_home, jnp.bfloat16, ((0,), (0,)))
        cot_rows = dot(placing, back_home, jnp.bfloat16, ((0,), (0,)))
        out_wide = out_rows.astype(jnp.float32)
        mixed = (gate[:, None] * out_wide).astype(jnp.bfloat16)
        own_slope = jnp.sum(out_grad.astype(jnp.float32) * out_wide, axis=1) * gate * (1.0 - gate)
        named = dot(chosen.astype(jnp.bfloat16), router, dims=((1,), (1,)))
        token_grad = (cot_rows.astype(jnp.float32) + own_slope[:, None] * named).astype(jnp.bfloat16)
        return (mixed, token_grad, up_grad, down_grad, router_grad)

    return per_device


def solution(mesh):
    in_specs = (
        P(("expert", "tensor"), None),
        P(("expert", "tensor"), None),
        P(("expert", "tensor")),
        P(),
        P("expert", None, "tensor"),
        P("expert", "tensor", None),
        P(("expert", "tensor"), None),
    )
    out_specs = (
        P(("expert", "tensor"), None),
        P(("expert", "tensor"), None),
        P("expert", None, "tensor"),
        P("expert", "tensor", None),
        P(),
    )
    return jax.shard_map(
        make(mesh.shape["expert"], mesh.shape["tensor"]),
        mesh=mesh,
        in_specs=in_specs,
        out_specs=out_specs,
        check_vma=False,
    )
```

```python
import functools

import jax
import jax.numpy as jnp
from jax import lax
from jax.experimental import pallas as pl
from jax.experimental.pallas import tpu as pltpu
from jax.sharding import PartitionSpec as P


def dot(a, b, out=jnp.float32, dims=((1,), (0,))):
    return lax.dot_general(a, b, (dims, ((), ())), preferred_element_type=jnp.float32).astype(out)


def joined(blocks):
    return jnp.concatenate(blocks, axis=0)


def after(x, *earlier):
    return lax.optimization_barrier((x,) + earlier)[0]


def added(a, b):
    return (a.astype(jnp.float32) + b.astype(jnp.float32)).astype(jnp.bfloat16)


def call(kernel, grid, in_specs, outs, out_specs, scratch=(), flops=1, moved=1):
    return pl.pallas_call(
        kernel,
        grid=(grid,),
        in_specs=in_specs,
        out_specs=out_specs,
        out_shape=outs,
        scratch_shapes=scratch,
        compiler_params=pltpu.CompilerParams(vmem_limit_bytes=40 * 1024 * 1024),
        cost_estimate=pl.CostEstimate(flops=flops, bytes_accessed=moved, transcendentals=0),
    )


def tile_of(size, want):
    return want if size % want == 0 else size


def nt(a, b):
    return lax.dot_general(a, b, (((1,), (1,)), ((), ())), preferred_element_type=jnp.float32)


def forward_kernel(blocks, steps, tile, *refs):
    rows, (up, down) = refs[:blocks], refs[blocks : blocks + 2]
    outs = refs[blocks + 2 : -1]
    hidden, active, term = outs[:blocks], outs[blocks : 2 * blocks], outs[2 * blocks :]
    held = refs[-1]
    step = pl.program_id(0)

    @pl.when(step < steps)
    def _():
        place = pl.ds(pl.multiple_of(step * tile, tile), tile)
        for i in range(blocks):
            value = jnp.dot(rows[i][...], up[...], preferred_element_type=jnp.float32)
            hidden[i][...] = value
            rounded = (value * jax.nn.sigmoid(value)).astype(jnp.bfloat16)
            active[i][...] = rounded
            held[i, :, place] = rounded

    @pl.when(step >= steps)
    def _():
        for i in range(blocks):
            total = jnp.dot(held[i], down[...], preferred_element_type=jnp.float32)
            term[i][...] = total.astype(jnp.bfloat16)


def backward_kernel(blocks, steps, tile, *refs):
    cots, hidden, active = (refs[k * blocks : (k + 1) * blocks] for k in range(3))
    down, up = refs[3 * blocks : 3 * blocks + 2]
    outs = refs[3 * blocks + 2 : -1]
    hidden_cot, slope, term = (outs[k * blocks : (k + 1) * blocks] for k in range(3))
    held = refs[-1]
    step = pl.program_id(0)

    @pl.when(step == 0)
    def _():
        for i in range(blocks):
            slope[i][...] = jnp.zeros_like(slope[i])

    @pl.when(step < steps)
    def _():
        place = pl.ds(pl.multiple_of(step * tile, tile), tile)
        for i in range(blocks):
            back = nt(cots[i][...], down[...])
            value = hidden[i][...]
            sig = jax.nn.sigmoid(value)
            rounded = (back * (sig * (1.0 + value * (1.0 - sig)))).astype(jnp.bfloat16)
            hidden_cot[i][...] = rounded
            held[i, :, place] = rounded
            product = back * active[i][...].astype(jnp.float32)
            lanes = slope[i].shape[1]
            slope[i][...] += sum(product[:, k : k + lanes] for k in range(0, tile, lanes))

    @pl.when(step >= steps)
    def _():
        for i in range(blocks):
            term[i][...] = nt(held[i], up[...]).astype(jnp.bfloat16)


def tiles_for(rows, w_up):
    width, hidden = w_up.shape
    tile, wide = tile_of(hidden, 256), tile_of(width, 512)
    return rows.shape[0], width, hidden, tile, wide, hidden // tile, width // wide


def whole(shape):
    return pl.BlockSpec(shape, lambda i: (0,) * len(shape))


def forward(rows, w_up, w_down):
    count, width, hidden, tile, wide, steps, wides = tiles_for(rows[0], w_up)
    n = len(rows)
    first, second = lambda i: jnp.minimum(i, steps - 1), lambda i: jnp.maximum(i - steps, 0)
    part = pl.BlockSpec((count, tile), lambda i: (0, first(i)))
    outs = call(
        functools.partial(forward_kernel, n, steps, tile),
        steps + wides,
        [whole((count, width))] * n
        + [
            pl.BlockSpec((width, tile), lambda i: (0, first(i))),
            pl.BlockSpec((hidden, wide), lambda i: (0, second(i))),
        ],
        [jax.ShapeDtypeStruct((count, hidden), jnp.float32)] * n
        + [jax.ShapeDtypeStruct((count, hidden), jnp.bfloat16)] * n
        + [jax.ShapeDtypeStruct((count, width), jnp.bfloat16)] * n,
        [part] * (2 * n) + [pl.BlockSpec((count, wide), lambda i: (0, second(i)))] * n,
        [pltpu.VMEM((n, count, hidden), jnp.bfloat16)],
    )(*rows, w_up, w_down)
    return list(outs[:n]), list(outs[n : 2 * n]), list(outs[2 * n :])


def backward(cots, hiddens, actives, w_up, w_down):
    count, width, hidden, tile, wide, steps, wides = tiles_for(cots[0], w_up)
    n = len(cots)
    lanes = tile_of(tile, 128)
    first, second = lambda i: jnp.minimum(i, steps - 1), lambda i: jnp.maximum(i - steps, 0)
    part = pl.BlockSpec((count, tile), lambda i: (0, first(i)))
    outs = call(
        functools.partial(backward_kernel, n, steps, tile),
        steps + wides,
        [whole((count, width))] * n
        + [part] * (2 * n)
        + [
            pl.BlockSpec((tile, width), lambda i: (first(i), 0)),
            pl.BlockSpec((wide, hidden), lambda i: (second(i), 0)),
        ],
        [jax.ShapeDtypeStruct((count, hidden), jnp.bfloat16)] * n
        + [jax.ShapeDtypeStruct((count, lanes), jnp.float32)] * n
        + [jax.ShapeDtypeStruct((count, width), jnp.bfloat16)] * n,
        [part] * n
        + [whole((count, lanes))] * n
        + [pl.BlockSpec((count, wide), lambda i: (0, second(i)))] * n,
        [pltpu.VMEM((n, count, hidden), jnp.bfloat16)],
    )(*cots, *hiddens, *actives, w_down, w_up)
    return list(outs[:n]), list(outs[n : 2 * n]), list(outs[2 * n :])


def gradient_kernel(blocks, *refs):
    left, right, out = refs[:blocks], refs[blocks : 2 * blocks], refs[-1]
    total = sum(
        lax.dot_general(
            a[...], b[...], (((0,), (0,)), ((), ())), preferred_element_type=jnp.float32
        )
        for a, b in zip(left, right)
    )
    out[...] = total.astype(out.dtype)


def gradient(lefts, rights, want):
    count, height = lefts[0].shape
    width = rights[0].shape[1]
    tile = tile_of(height, want)
    return call(
        functools.partial(gradient_kernel, len(lefts)),
        height // tile,
        [pl.BlockSpec((count, tile), lambda i: (0, i))] * len(lefts)
        + [whole((count, width))] * len(rights),
        jax.ShapeDtypeStruct((height, width), jnp.bfloat16),
        pl.BlockSpec((tile, width), lambda i: (i, 0)),
        flops=2 * len(lefts) * count * height * width,
        moved=2 * (len(lefts) * count * (height + width) + height * width),
    )(*lefts, *rights)


def make(n_expert, n_tensor):
    top, low = n_tensor // 2, n_tensor // 2

    def cross(x, bit):
        return lax.ppermute(x, "tensor", [(i, i ^ bit) for i in range(n_tensor)])

    def gather_low(rows):
        held = [rows]
        bit = 1
        while bit < low:
            held = held + [cross(h, bit) for h in held]
            bit *= 2
        return held

    def sum_low(terms):
        while len(terms) > 1:
            bit = len(terms) // 2
            terms = [added(a, cross(b, bit)) for a, b in zip(terms[:bit], terms[bit:])]
        return terms[0]

    def per_device(tokens, expert_ids, live_counts, router, up_weight, down_weight, out_grad):
        tok_rows, width = tokens.shape
        experts = router.shape[1]
        most = 3 * tok_rows // (2 * experts)
        slots = experts * most
        me = lax.axis_index("expert")
        ids = expert_ids[:, 0]
        live = lax.iota(jnp.int32, tok_rows) < live_counts[0]
        chosen = ids[:, None] == lax.iota(jnp.int32, experts)[None, :]
        chosen_int = chosen.astype(jnp.int32)
        rank = jnp.sum(jnp.cumsum(chosen_int, axis=0) * chosen_int, axis=1) - 1
        target = jnp.where(live, ids * most + rank, -1)
        placing = (lax.iota(jnp.int32, slots)[:, None] == target[None, :]).astype(jnp.bfloat16)
        w_up = up_weight[0]
        w_down = down_weight[0]

        def swap(x):
            return lax.all_to_all(x, "expert", split_axis=0, concat_axis=0, tiled=True)

        def exchange(x):
            return swap(x.reshape(experts, most, width)).reshape(slots, width)

        tok_near = exchange(dot(placing, tokens, jnp.bfloat16))
        logits = dot(tokens, router)
        gate = jax.nn.sigmoid(jnp.sum(logits * chosen.astype(jnp.float32), axis=1))
        out_cot = (gate[:, None] * out_grad.astype(jnp.float32)).astype(jnp.bfloat16)
        cot_near = exchange(after(dot(placing, out_cot, jnp.bfloat16), tok_near))
        tok_far = cross(tok_near, top)
        cot_far = cross(cot_near, top)

        tok_far_all = gather_low(after(tok_far, cot_near))
        hidden, active, term = forward(tok_far_all, w_up, w_down)
        out_far_sum = sum_low(term)
        out_far = cross(after(out_far_sum, cot_far), top)
        tok_near_all = gather_low(tok_near)
        near_hidden, near_active, near_term = forward(
            [after(x, *term) for x in tok_near_all], w_up, w_down
        )
        out_near = sum_low(near_term)
        cot_near_all = gather_low(cot_near)
        near_hidden_cot, near_slope, near_term = backward(
            cot_near_all, near_hidden, near_active, w_up, w_down
        )
        back_near = sum_low(near_term)

        cot_far_all = gather_low(after(cot_far, out_far_sum, *near_term))
        hidden_cot, slope, term = backward(cot_far_all, hidden, active, w_up, w_down)
        back_far_sum = sum_low(term)
        back_far = cross(back_far_sum, top)
        rows, cots = tok_far_all + tok_near_all, cot_far_all + cot_near_all
        active, hidden_cot = active + near_active, hidden_cot + near_hidden_cot
        slope = slope + near_slope
        out_sum = added(out_near, after(out_far, *term))

        column = lax.dynamic_slice_in_dim(router, me, 1, axis=1)
        columns = jnp.zeros((1, width), jnp.float32)
        for x, lanes in zip(rows, slope):
            own = jnp.sum(lanes, axis=1, keepdims=True) * (1.0 - jax.nn.sigmoid(dot(x, column)))
            high = own.astype(jnp.bfloat16)
            rest = own - high.astype(jnp.float32)
            middle = rest.astype(jnp.bfloat16)
            least = (rest - middle.astype(jnp.float32)).astype(jnp.bfloat16)
            split = jnp.concatenate([high, middle, least], axis=1)
            columns += jnp.sum(dot(split, x, dims=((0,), (0,))), axis=0, keepdims=True)
        bit = 1
        while bit < n_tensor:
            columns = columns + cross(columns, bit)
            bit *= 2
        out_home = exchange(after(out_sum, back_far_sum, columns))
        lanes = -(-width // (most * 128)) * 128
        high = columns.astype(jnp.bfloat16)
        rest = (columns - high.astype(jnp.float32)).astype(jnp.bfloat16)
        beside = jnp.concatenate(
            [
                jnp.pad(x, ((0, 0), (0, most * lanes - width))).reshape(1, most, lanes)
                for x in (high, rest)
            ],
            axis=2,
        )

        back_sum = added(back_near, after(back_far, out_home))

        up_grad = gradient([after(x, back_sum) for x in rows], hidden_cot, 512)[None]
        down_grad = gradient([after(x, back_sum) for x in active], cots, 256)[None]

        back_sum = back_sum.reshape(experts, most, width)
        beside = jnp.broadcast_to(beside, (experts, most, 2 * lanes))
        came = swap(jnp.concatenate([back_sum, beside], axis=2))
        back_home = came[:, :, :width].reshape(slots, width)
        high, rest = (
            came[:, :, k : k + lanes].reshape(experts, most * lanes)[:, :width].astype(jnp.float32)
            for k in (width, width + lanes)
        )
        router_grad = (high + rest).T

        out_rows = dot(placing, after(out_home, back_sum), jnp.bfloat16, ((0,), (0,)))
        cot_rows = dot(placing, back_home, jnp.bfloat16, ((0,), (0,)))
        out_wide = out_rows.astype(jnp.float32)
        mixed = (gate[:, None] * out_wide).astype(jnp.bfloat16)
        own_slope = jnp.sum(out_grad.astype(jnp.float32) * out_wide, axis=1) * gate * (1.0 - gate)
        named = dot(chosen.astype(jnp.bfloat16), router, dims=((1,), (1,)))
        token_grad = (cot_rows.astype(jnp.float32) + own_slope[:, None] * named).astype(jnp.bfloat16)
        return (mixed, token_grad, up_grad, down_grad, router_grad)

    return per_device


def solution(mesh):
    in_specs = (
        P(("expert", "tensor"), None),
        P(("expert", "tensor"), None),
        P(("expert", "tensor")),
        P(),
        P("expert", None, "tensor"),
        P("expert", "tensor", None),
        P(("expert", "tensor"), None),
    )
    out_specs = (
        P(("expert", "tensor"), None),
        P(("expert", "tensor"), None),
        P("expert", None, "tensor"),
        P("expert", "tensor", None),
        P(),
    )
    return jax.shard_map(
        make(mesh.shape["expert"], mesh.shape["tensor"]),
        mesh=mesh,
        in_specs=in_specs,
        out_specs=out_specs,
        check_vma=False,
    )
```

```python
import functools

import jax
import jax.numpy as jnp
from jax import lax
from jax.experimental import pallas as pl
from jax.experimental.pallas import tpu as pltpu
from jax.sharding import PartitionSpec as P


def dot(a, b, out=jnp.float32, dims=((1,), (0,))):
    return lax.dot_general(a, b, (dims, ((), ())), preferred_element_type=jnp.float32).astype(out)


def joined(blocks):
    return jnp.concatenate(blocks, axis=0)


def after(x, *earlier):
    return lax.optimization_barrier((x,) + earlier)[0]


def added(a, b):
    return (a.astype(jnp.float32) + b.astype(jnp.float32)).astype(jnp.bfloat16)


def call(kernel, grid, in_specs, outs, out_specs, scratch=(), flops=1, moved=1):
    return pl.pallas_call(
        kernel,
        grid=(grid,),
        in_specs=in_specs,
        out_specs=out_specs,
        out_shape=outs,
        scratch_shapes=scratch,
        compiler_params=pltpu.CompilerParams(vmem_limit_bytes=40 * 1024 * 1024),
        cost_estimate=pl.CostEstimate(flops=flops, bytes_accessed=moved, transcendentals=0),
    )


def tile_of(size, want):
    return want if size % want == 0 else size


def whole(shape):
    return pl.BlockSpec(shape, lambda i: (0,) * len(shape))


def forward(rows, w_up, w_down):
    hidden = dot(rows, w_up)
    active = jax.nn.silu(hidden).astype(jnp.bfloat16)
    hidden, active = lax.optimization_barrier((hidden, active))
    return hidden, active, dot(active, w_down, jnp.bfloat16)


def backward(cots, hidden, active, w_up, w_down):
    back = dot(cots, w_down, dims=((1,), (1,)))
    sig = jax.nn.sigmoid(hidden)
    hidden_cot = (back * (sig * (1.0 + hidden * (1.0 - sig)))).astype(jnp.bfloat16)
    slope = jnp.sum(back * active.astype(jnp.float32), axis=1, keepdims=True)
    return hidden_cot, slope, dot(hidden_cot, w_up, jnp.bfloat16, ((1,), (1,)))


def each(function, *lists):
    return map(list, zip(*[function(*items) for items in zip(*lists)]))


def gradient_kernel(blocks, *refs):
    left, right, out = refs[:blocks], refs[blocks : 2 * blocks], refs[-1]
    total = sum(
        lax.dot_general(
            a[...], b[...], (((0,), (0,)), ((), ())), preferred_element_type=jnp.float32
        )
        for a, b in zip(left, right)
    )
    out[...] = total.astype(out.dtype)


def gradient(lefts, rights, want):
    count, height = lefts[0].shape
    width = rights[0].shape[1]
    tile = tile_of(height, want)
    return call(
        functools.partial(gradient_kernel, len(lefts)),
        height // tile,
        [pl.BlockSpec((count, tile), lambda i: (0, i))] * len(lefts)
        + [whole((count, width))] * len(rights),
        jax.ShapeDtypeStruct((height, width), jnp.bfloat16),
        pl.BlockSpec((tile, width), lambda i: (i, 0)),
        flops=2 * len(lefts) * count * height * width,
        moved=2 * (len(lefts) * count * (height + width) + height * width),
    )(*lefts, *rights)


def make(n_expert, n_tensor):
    top, low = n_tensor // 2, n_tensor // 2

    def cross(x, bit):
        return lax.ppermute(x, "tensor", [(i, i ^ bit) for i in range(n_tensor)])

    def gather_low(rows):
        held = [rows]
        bit = 1
        while bit < low:
            held = held + [cross(h, bit) for h in held]
            bit *= 2
        return held

    def sum_low(terms):
        while len(terms) > 1:
            bit = len(terms) // 2
            terms = [added(a, cross(b, bit)) for a, b in zip(terms[:bit], terms[bit:])]
        return terms[0]

    def per_device(tokens, expert_ids, live_counts, router, up_weight, down_weight, out_grad):
        tok_rows, width = tokens.shape
        experts = router.shape[1]
        most = 3 * tok_rows // (2 * experts)
        slots = experts * most
        me = lax.axis_index("expert")
        ids = expert_ids[:, 0]
        live = lax.iota(jnp.int32, tok_rows) < live_counts[0]
        chosen = ids[:, None] == lax.iota(jnp.int32, experts)[None, :]
        chosen_int = chosen.astype(jnp.int32)
        rank = jnp.sum(jnp.cumsum(chosen_int, axis=0) * chosen_int, axis=1) - 1
        target = jnp.where(live, ids * most + rank, -1)
        placing = (lax.iota(jnp.int32, slots)[:, None] == target[None, :]).astype(jnp.bfloat16)
        w_up = up_weight[0]
        w_down = down_weight[0]

        def swap(x):
            return lax.all_to_all(x, "expert", split_axis=0, concat_axis=0, tiled=True)

        def exchange(x):
            return swap(x.reshape(experts, most, width)).reshape(slots, width)

        tok_near = exchange(dot(placing, tokens, jnp.bfloat16))
        logits = dot(tokens, router)
        gate = jax.nn.sigmoid(jnp.sum(logits * chosen.astype(jnp.float32), axis=1))
        out_cot = (gate[:, None] * out_grad.astype(jnp.float32)).astype(jnp.bfloat16)
        cot_near = exchange(after(dot(placing, out_cot, jnp.bfloat16), tok_near))
        tok_far = cross(tok_near, top)
        cot_far = cross(cot_near, top)

        forward_on = lambda x: forward(x, w_up, w_down)
        backward_on = lambda *xs: backward(*xs, w_up, w_down)

        rows = gather_low(after(tok_far, cot_near))
        hidden, active, term = each(forward_on, rows)
        out_far_sum = sum_low(term)
        near = gather_low(tok_near)
        near_hidden, near_active, near_term = each(forward_on, [after(x, *term) for x in near])
        rows, hidden, active = rows + near, hidden + near_hidden, active + near_active
        cot_far = after(cot_far, out_far_sum, near_term[0])
        out_far = cross(after(out_far_sum, cot_far), top)
        out_near = sum_low(near_term)

        cots = gather_low(cot_far)
        hidden_cot, slope, term = each(backward_on, cots, hidden[:low], active[:low])
        back_far_sum = sum_low(term)
        back_far = cross(back_far_sum, top)
        out_sum = added(out_near, after(out_far, term[-1]))
        out_home = exchange(after(out_sum, back_far_sum))
        near = gather_low(cot_near)
        near_hidden_cot, near_slope, term = each(
            backward_on, [after(x, out_sum) for x in near], hidden[low:], active[low:]
        )
        cots, hidden_cot, slope = cots + near, hidden_cot + near_hidden_cot, slope + near_slope
        back_near = sum_low(term)

        column = lax.dynamic_slice_in_dim(router, me, 1, axis=1)
        columns = jnp.zeros((1, width), jnp.float32)
        for x, own in zip(rows, slope):
            own = own * (1.0 - jax.nn.sigmoid(dot(after(x, out_sum), column)))
            high = own.astype(jnp.bfloat16)
            rest = own - high.astype(jnp.float32)
            middle = rest.astype(jnp.bfloat16)
            least = (rest - middle.astype(jnp.float32)).astype(jnp.bfloat16)
            split = jnp.concatenate([high, middle, least], axis=1)
            columns += jnp.sum(dot(split, x, dims=((0,), (0,))), axis=0, keepdims=True)
        bit = 1
        while bit < n_tensor:
            columns = columns + cross(after(columns, back_far) if bit == top else columns, bit)
            bit *= 2
        lanes = -(-width // (most * 128)) * 128
        high = columns.astype(jnp.bfloat16)
        rest = (columns - high.astype(jnp.float32)).astype(jnp.bfloat16)
        beside = jnp.concatenate(
            [
                jnp.pad(x, ((0, 0), (0, most * lanes - width))).reshape(1, most, lanes)
                for x in (high, rest)
            ],
            axis=2,
        )

        back_sum = added(back_near, after(back_far, out_home))

        up_grad = gradient([after(x, back_sum, columns) for x in rows], hidden_cot, 512)[None]
        down_grad = gradient([after(x, back_sum, columns) for x in active], cots, 256)[None]

        back_sum = back_sum.reshape(experts, most, width)
        beside = jnp.broadcast_to(beside, (experts, most, 2 * lanes))
        came = swap(jnp.concatenate([back_sum, beside], axis=2))
        back_home = came[:, :, :width].reshape(slots, width)
        high, rest = (
            came[:, :, k : k + lanes].reshape(experts, most * lanes)[:, :width].astype(jnp.float32)
            for k in (width, width + lanes)
        )
        router_grad = (high + rest).T

        out_rows = dot(placing, after(out_home, back_sum), jnp.bfloat16, ((0,), (0,)))
        cot_rows = dot(placing, back_home, jnp.bfloat16, ((0,), (0,)))
        out_wide = out_rows.astype(jnp.float32)
        mixed = (gate[:, None] * out_wide).astype(jnp.bfloat16)
        own_slope = jnp.sum(out_grad.astype(jnp.float32) * out_wide, axis=1) * gate * (1.0 - gate)
        named = dot(chosen.astype(jnp.bfloat16), router, dims=((1,), (1,)))
        token_grad = (cot_rows.astype(jnp.float32) + own_slope[:, None] * named).astype(jnp.bfloat16)
        return (mixed, token_grad, up_grad, down_grad, router_grad)

    return per_device


def solution(mesh):
    in_specs = (
        P(("expert", "tensor"), None),
        P(("expert", "tensor"), None),
        P(("expert", "tensor")),
        P(),
        P("expert", None, "tensor"),
        P("expert", "tensor", None),
        P(("expert", "tensor"), None),
    )
    out_specs = (
        P(("expert", "tensor"), None),
        P(("expert", "tensor"), None),
        P("expert", None, "tensor"),
        P("expert", "tensor", None),
        P(),
    )
    return jax.shard_map(
        make(mesh.shape["expert"], mesh.shape["tensor"]),
        mesh=mesh,
        in_specs=in_specs,
        out_specs=out_specs,
        check_vma=False,
    )
```

```python
import functools

import jax
import jax.numpy as jnp
from jax import lax
from jax.experimental import pallas as pl
from jax.experimental.pallas import tpu as pltpu
from jax.sharding import PartitionSpec as P


def dot(a, b, out=jnp.float32, dims=((1,), (0,))):
    return lax.dot_general(a, b, (dims, ((), ())), preferred_element_type=jnp.float32).astype(out)


def joined(blocks):
    return jnp.concatenate(blocks, axis=0)


def after(x, *earlier):
    return lax.optimization_barrier((x,) + earlier)[0]


def added(a, b):
    return (a.astype(jnp.float32) + b.astype(jnp.float32)).astype(jnp.bfloat16)


def call(kernel, grid, in_specs, outs, out_specs, scratch=(), flops=1, moved=1, mib=20):
    return pl.pallas_call(
        kernel,
        grid=(grid,),
        in_specs=in_specs,
        out_specs=out_specs,
        out_shape=outs,
        scratch_shapes=scratch,
        compiler_params=pltpu.CompilerParams(vmem_limit_bytes=mib * 1024 * 1024),
        cost_estimate=pl.CostEstimate(flops=flops, bytes_accessed=moved, transcendentals=0),
    )


def tile_of(size, want):
    return want if size % want == 0 else size


def nt(a, b):
    return lax.dot_general(a, b, (((1,), (1,)), ((), ())), preferred_element_type=jnp.float32)


def forward_kernel(blocks, steps, tile, *refs):
    rows, (up, down) = refs[:blocks], refs[blocks : blocks + 2]
    outs = refs[blocks + 2 : -1]
    hidden, active, term = outs[:blocks], outs[blocks : 2 * blocks], outs[2 * blocks :]
    held = refs[-1]
    step = pl.program_id(0)

    @pl.when(step < steps)
    def _():
        place = pl.ds(pl.multiple_of(step * tile, tile), tile)
        for i in range(blocks):
            value = jnp.dot(rows[i][...], up[...], preferred_element_type=jnp.float32)
            hidden[i][...] = value
            rounded = (value * jax.nn.sigmoid(value)).astype(jnp.bfloat16)
            active[i][...] = rounded
            held[i, :, place] = rounded

    @pl.when(step >= steps)
    def _():
        for i in range(blocks):
            total = jnp.dot(held[i], down[...], preferred_element_type=jnp.float32)
            term[i][...] = total.astype(jnp.bfloat16)


def backward_kernel(blocks, steps, tile, *refs):
    cots, hidden, active = (refs[k * blocks : (k + 1) * blocks] for k in range(3))
    down, up = refs[3 * blocks : 3 * blocks + 2]
    outs = refs[3 * blocks + 2 : -1]
    hidden_cot, slope, term = (outs[k * blocks : (k + 1) * blocks] for k in range(3))
    held = refs[-1]
    step = pl.program_id(0)

    @pl.when(step == 0)
    def _():
        for i in range(blocks):
            slope[i][...] = jnp.zeros_like(slope[i])

    @pl.when(step < steps)
    def _():
        place = pl.ds(pl.multiple_of(step * tile, tile), tile)
        for i in range(blocks):
            back = nt(cots[i][...], down[...])
            value = hidden[i][...]
            sig = jax.nn.sigmoid(value)
            rounded = (back * (sig * (1.0 + value * (1.0 - sig)))).astype(jnp.bfloat16)
            hidden_cot[i][...] = rounded
            held[i, :, place] = rounded
            product = back * active[i][...].astype(jnp.float32)
            lanes = slope[i].shape[1]
            slope[i][...] += sum(product[:, k : k + lanes] for k in range(0, tile, lanes))

    @pl.when(step >= steps)
    def _():
        for i in range(blocks):
            term[i][...] = nt(held[i], up[...]).astype(jnp.bfloat16)


def tiles_for(rows, w_up):
    width, hidden = w_up.shape
    tile, wide = tile_of(hidden, 512), tile_of(width, 1280)
    return rows.shape[0], width, hidden, tile, wide, hidden // tile, width // wide


def whole(shape):
    return pl.BlockSpec(shape, lambda i: (0,) * len(shape), pipeline_mode=pl.Buffered(1))


def forward(rows, w_up, w_down):
    hidden = dot(rows, w_up)
    active = jax.nn.silu(hidden).astype(jnp.bfloat16)
    hidden, active = lax.optimization_barrier((hidden, active))
    return hidden, active, dot(active, w_down, jnp.bfloat16)


def backward(cots, hidden, active, w_up, w_down):
    back = dot(cots, w_down, dims=((1,), (1,)))
    sig = jax.nn.sigmoid(hidden)
    hidden_cot = (back * (sig * (1.0 + hidden * (1.0 - sig)))).astype(jnp.bfloat16)
    slope = jnp.sum(back * active.astype(jnp.float32), axis=1, keepdims=True)
    return hidden_cot, slope, dot(hidden_cot, w_up, jnp.bfloat16, ((1,), (1,)))


def each(function, *lists):
    return map(list, zip(*[function(*items) for items in zip(*lists)]))


def forward_pair(rows, w_up, w_down):
    count, width, hidden, tile, wide, steps, wides = tiles_for(rows[0], w_up)
    n = len(rows)
    first, second = lambda i: jnp.minimum(i, steps - 1), lambda i: jnp.maximum(i - steps, 0)
    part = pl.BlockSpec((count, tile), lambda i: (0, first(i)))
    outs = call(
        functools.partial(forward_kernel, n, steps, tile),
        steps + wides,
        [whole((count, width))] * n
        + [
            pl.BlockSpec((width, tile), lambda i: (0, first(i))),
            pl.BlockSpec((hidden, wide), lambda i: (0, second(i))),
        ],
        [jax.ShapeDtypeStruct((count, hidden), jnp.float32)] * n
        + [jax.ShapeDtypeStruct((count, hidden), jnp.bfloat16)] * n
        + [jax.ShapeDtypeStruct((count, width), jnp.bfloat16)] * n,
        [part] * (2 * n) + [pl.BlockSpec((count, wide), lambda i: (0, second(i)))] * n,
        [pltpu.VMEM((n, count, hidden), jnp.bfloat16)],
        mib=32,
    )(*rows, w_up, w_down)
    return list(outs[:n]), list(outs[n : 2 * n]), list(outs[2 * n :])


def backward_pair(cots, hiddens, actives, w_up, w_down):
    count, width, hidden, tile, wide, steps, wides = tiles_for(cots[0], w_up)
    n = len(cots)
    lanes = tile_of(tile, 128)
    first, second = lambda i: jnp.minimum(i, steps - 1), lambda i: jnp.maximum(i - steps, 0)
    part = pl.BlockSpec((count, tile), lambda i: (0, first(i)))
    outs = call(
        functools.partial(backward_kernel, n, steps, tile),
        steps + wides,
        [whole((count, width))] * n
        + [part] * (2 * n)
        + [
            pl.BlockSpec((tile, width), lambda i: (first(i), 0)),
            pl.BlockSpec((wide, hidden), lambda i: (second(i), 0)),
        ],
        [jax.ShapeDtypeStruct((count, hidden), jnp.bfloat16)] * n
        + [jax.ShapeDtypeStruct((count, lanes), jnp.float32)] * n
        + [jax.ShapeDtypeStruct((count, width), jnp.bfloat16)] * n,
        [part] * n
        + [whole((count, lanes))] * n
        + [pl.BlockSpec((count, wide), lambda i: (0, second(i)))] * n,
        [pltpu.VMEM((n, count, hidden), jnp.bfloat16)],
        mib=32,
    )(*cots, *hiddens, *actives, w_down, w_up)
    return list(outs[:n]), list(outs[n : 2 * n]), list(outs[2 * n :])


def gradient_kernel(blocks, *refs):
    left, right, out = refs[:blocks], refs[blocks : 2 * blocks], refs[-1]
    total = sum(
        lax.dot_general(
            a[...], b[...], (((0,), (0,)), ((), ())), preferred_element_type=jnp.float32
        )
        for a, b in zip(left, right)
    )
    out[...] = total.astype(out.dtype)


def gradient(lefts, rights, want):
    count, height = lefts[0].shape
    width = rights[0].shape[1]
    tile = tile_of(height, want)
    return call(
        functools.partial(gradient_kernel, len(lefts)),
        height // tile,
        [pl.BlockSpec((count, tile), lambda i: (0, i))] * len(lefts)
        + [whole((count, width))] * len(rights),
        jax.ShapeDtypeStruct((height, width), jnp.bfloat16),
        pl.BlockSpec((tile, width), lambda i: (i, 0)),
        flops=2 * len(lefts) * count * height * width,
        moved=2 * (len(lefts) * count * (height + width) + height * width),
    )(*lefts, *rights)


def make(n_expert, n_tensor):
    top, low = n_tensor // 2, n_tensor // 2

    def cross(x, bit):
        return lax.ppermute(x, "tensor", [(i, i ^ bit) for i in range(n_tensor)])

    def gather_low(rows):
        held = [rows]
        bit = 1
        while bit < low:
            held = held + [cross(h, bit) for h in held]
            bit *= 2
        return held

    def sum_low(terms):
        while len(terms) > 1:
            bit = len(terms) // 2
            terms = [added(a, cross(b, bit)) for a, b in zip(terms[:bit], terms[bit:])]
        return terms[0]

    def per_device(tokens, expert_ids, live_counts, router, up_weight, down_weight, out_grad):
        tok_rows, width = tokens.shape
        experts = router.shape[1]
        most = 3 * tok_rows // (2 * experts)
        slots = experts * most
        me = lax.axis_index("expert")
        ids = expert_ids[:, 0]
        live = lax.iota(jnp.int32, tok_rows) < live_counts[0]
        chosen = ids[:, None] == lax.iota(jnp.int32, experts)[None, :]
        chosen_int = chosen.astype(jnp.int32)
        rank = jnp.sum(jnp.cumsum(chosen_int, axis=0) * chosen_int, axis=1) - 1
        target = jnp.where(live, ids * most + rank, -1)
        placing = (lax.iota(jnp.int32, slots)[:, None] == target[None, :]).astype(jnp.bfloat16)
        w_up = up_weight[0]
        w_down = down_weight[0]

        def swap(x):
            return lax.all_to_all(x, "expert", split_axis=0, concat_axis=0, tiled=True)

        def exchange(x):
            return swap(x.reshape(experts, most, width)).reshape(slots, width)

        tok_near = exchange(dot(placing, tokens, jnp.bfloat16))
        logits = dot(tokens, router)
        gate = jax.nn.sigmoid(jnp.sum(logits * chosen.astype(jnp.float32), axis=1))
        out_cot = (gate[:, None] * out_grad.astype(jnp.float32)).astype(jnp.bfloat16)
        cot_near = exchange(after(dot(placing, out_cot, jnp.bfloat16), tok_near))
        tok_far = cross(tok_near, top)
        cot_far = cross(cot_near, top)

        forward_on = lambda x: forward(x, w_up, w_down)
        backward_on = lambda *xs: backward(*xs, w_up, w_down)

        rows = gather_low(after(tok_far, cot_near))
        hidden, active, term = forward_pair(rows, w_up, w_down)
        out_far_sum = sum_low(term)
        cot_far = after(cot_far, *term)
        near = gather_low(tok_near)
        near_hidden, near_active, near_term = each(forward_on, [after(x, cot_far) for x in near])
        rows, hidden, active = rows + near, hidden + near_hidden, active + near_active
        out_far = cross(after(out_far_sum, cot_far), top)
        out_near = sum_low(near_term)

        cots = gather_low(cot_far)
        hidden_cot, slope, term = backward_pair(cots, hidden[:low], active[:low], w_up, w_down)
        slope = [jnp.sum(after(x, *term), axis=1, keepdims=True) for x in slope]
        back_far_sum = sum_low(term)
        back_far = cross(back_far_sum, top)
        out_sum = added(out_near, after(out_far, back_far_sum))
        out_home = exchange(after(out_sum, back_far_sum))
        near = gather_low(cot_near)
        near_hidden_cot, near_slope, term = each(
            backward_on, [after(x, out_sum) for x in near], hidden[low:], active[low:]
        )
        cots, hidden_cot, slope = cots + near, hidden_cot + near_hidden_cot, slope + near_slope
        back_near = sum_low(term)

        column = lax.dynamic_slice_in_dim(router, me, 1, axis=1)
        columns = jnp.zeros((1, width), jnp.float32)
        for x, own in zip(rows, slope):
            own = own * (1.0 - jax.nn.sigmoid(dot(after(x, out_sum), column)))
            high = own.astype(jnp.bfloat16)
            rest = own - high.astype(jnp.float32)
            middle = rest.astype(jnp.bfloat16)
            least = (rest - middle.astype(jnp.float32)).astype(jnp.bfloat16)
            split = jnp.concatenate([high, middle, least], axis=1)
            columns += jnp.sum(dot(split, x, dims=((0,), (0,))), axis=0, keepdims=True)
        bit = 1
        while bit < n_tensor:
            columns = columns + cross(after(columns, back_far) if bit == top else columns, bit)
            bit *= 2
        lanes = -(-width // (most * 128)) * 128
        high = columns.astype(jnp.bfloat16)
        rest = (columns - high.astype(jnp.float32)).astype(jnp.bfloat16)
        beside = jnp.concatenate(
            [
                jnp.pad(x, ((0, 0), (0, most * lanes - width))).reshape(1, most, lanes)
                for x in (high, rest)
            ],
            axis=2,
        )

        back_sum = added(back_near, after(back_far, out_home))

        up_grad = gradient([after(x, back_sum, columns) for x in rows], hidden_cot, 512)[None]
        down_grad = gradient([after(x, back_sum, columns) for x in active], cots, 256)[None]

        back_sum = back_sum.reshape(experts, most, width)
        beside = jnp.broadcast_to(beside, (experts, most, 2 * lanes))
        came = swap(jnp.concatenate([back_sum, beside], axis=2))
        back_home = came[:, :, :width].reshape(slots, width)
        high, rest = (
            came[:, :, k : k + lanes].reshape(experts, most * lanes)[:, :width].astype(jnp.float32)
            for k in (width, width + lanes)
        )
        router_grad = (high + rest).T

        out_rows = dot(placing, after(out_home, back_sum), jnp.bfloat16, ((0,), (0,)))
        cot_rows = dot(placing, back_home, jnp.bfloat16, ((0,), (0,)))
        out_wide = out_rows.astype(jnp.float32)
        mixed = (gate[:, None] * out_wide).astype(jnp.bfloat16)
        own_slope = jnp.sum(out_grad.astype(jnp.float32) * out_wide, axis=1) * gate * (1.0 - gate)
        named = dot(chosen.astype(jnp.bfloat16), router, dims=((1,), (1,)))
        token_grad = (cot_rows.astype(jnp.float32) + own_slope[:, None] * named).astype(jnp.bfloat16)
        return (mixed, token_grad, up_grad, down_grad, router_grad)

    return per_device


def solution(mesh):
    in_specs = (
        P(("expert", "tensor"), None),
        P(("expert", "tensor"), None),
        P(("expert", "tensor")),
        P(),
        P("expert", None, "tensor"),
        P("expert", "tensor", None),
        P(("expert", "tensor"), None),
    )
    out_specs = (
        P(("expert", "tensor"), None),
        P(("expert", "tensor"), None),
        P("expert", None, "tensor"),
        P("expert", "tensor", None),
        P(),
    )
    return jax.shard_map(
        make(mesh.shape["expert"], mesh.shape["tensor"]),
        mesh=mesh,
        in_specs=in_specs,
        out_specs=out_specs,
        check_vma=False,
    )
```

```python
import functools

import jax
import jax.numpy as jnp
from jax import lax
from jax.experimental import pallas as pl
from jax.experimental.pallas import tpu as pltpu
from jax.sharding import PartitionSpec as P


def dot(a, b, out=jnp.float32, dims=((1,), (0,))):
    return lax.dot_general(a, b, (dims, ((), ())), preferred_element_type=jnp.float32).astype(out)


def joined(blocks):
    return jnp.concatenate(blocks, axis=0)


def after(x, *earlier):
    return lax.optimization_barrier((x,) + earlier)[0]


def added(a, b):
    return (a.astype(jnp.float32) + b.astype(jnp.float32)).astype(jnp.bfloat16)


def call(kernel, grid, in_specs, outs, out_specs, scratch=(), flops=1, moved=1, mib=20):
    return pl.pallas_call(
        kernel,
        grid=(grid,),
        in_specs=in_specs,
        out_specs=out_specs,
        out_shape=outs,
        scratch_shapes=scratch,
        compiler_params=pltpu.CompilerParams(vmem_limit_bytes=mib * 1024 * 1024),
        cost_estimate=pl.CostEstimate(flops=flops, bytes_accessed=moved, transcendentals=0),
    )


def tile_of(size, want):
    return want if size % want == 0 else size


def nt(a, b):
    return lax.dot_general(a, b, (((1,), (1,)), ((), ())), preferred_element_type=jnp.float32)


def forward_kernel(blocks, steps, tile, *refs):
    rows, (up, down) = refs[:blocks], refs[blocks : blocks + 2]
    outs = refs[blocks + 2 : -1]
    hidden, active, term = outs[:blocks], outs[blocks : 2 * blocks], outs[2 * blocks :]
    held = refs[-1]
    step = pl.program_id(0)

    @pl.when(step < steps)
    def _():
        place = pl.ds(pl.multiple_of(step * tile, tile), tile)
        for i in range(blocks):
            value = jnp.dot(rows[i][...], up[...], preferred_element_type=jnp.float32)
            hidden[i][...] = value
            rounded = (value * jax.nn.sigmoid(value)).astype(jnp.bfloat16)
            active[i][...] = rounded
            held[i, :, place] = rounded

    @pl.when(step >= steps)
    def _():
        for i in range(blocks):
            total = jnp.dot(held[i], down[...], preferred_element_type=jnp.float32)
            term[i][...] = total.astype(jnp.bfloat16)


def backward_kernel(blocks, steps, tile, *refs):
    cots, hidden, active = (refs[k * blocks : (k + 1) * blocks] for k in range(3))
    down, up = refs[3 * blocks : 3 * blocks + 2]
    outs = refs[3 * blocks + 2 : -1]
    hidden_cot, slope, term = (outs[k * blocks : (k + 1) * blocks] for k in range(3))
    held = refs[-1]
    step = pl.program_id(0)

    @pl.when(step == 0)
    def _():
        for i in range(blocks):
            slope[i][...] = jnp.zeros_like(slope[i])

    @pl.when(step < steps)
    def _():
        place = pl.ds(pl.multiple_of(step * tile, tile), tile)
        for i in range(blocks):
            back = nt(cots[i][...], down[...])
            value = hidden[i][...]
            sig = jax.nn.sigmoid(value)
            rounded = (back * (sig * (1.0 + value * (1.0 - sig)))).astype(jnp.bfloat16)
            hidden_cot[i][...] = rounded
            held[i, :, place] = rounded
            product = back * active[i][...].astype(jnp.float32)
            lanes = slope[i].shape[1]
            slope[i][...] += sum(product[:, k : k + lanes] for k in range(0, tile, lanes))

    @pl.when(step >= steps)
    def _():
        for i in range(blocks):
            term[i][...] = nt(held[i], up[...]).astype(jnp.bfloat16)


def tiles_for(rows, w_up):
    width, hidden = w_up.shape
    tile, wide = tile_of(hidden, 512), tile_of(width, 1280)
    return rows.shape[0], width, hidden, tile, wide, hidden // tile, width // wide


def whole(shape):
    return pl.BlockSpec(shape, lambda i: (0,) * len(shape), pipeline_mode=pl.Buffered(1))


def copy_kernel(a, b, x, y):
    x[...] = a[...]
    y[...] = b[...]


def copied(a, b, parts):
    specs = [
        pl.BlockSpec((x.shape[0] // parts, x.shape[1]), lambda i: (i, 0)) for x in (a, b)
    ]
    outs = [jax.ShapeDtypeStruct(x.shape, x.dtype) for x in (a, b)]
    return call(copy_kernel, parts, specs, outs, specs)(a, b)


def forward(rows, w_up, w_down):
    count, width, hidden, tile, wide, steps, wides = tiles_for(rows[0], w_up)
    n = len(rows)
    first, second = lambda i: jnp.minimum(i, steps - 1), lambda i: jnp.maximum(i - steps, 0)
    part = pl.BlockSpec((count, tile), lambda i: (0, first(i)))
    outs = call(
        functools.partial(forward_kernel, n, steps, tile),
        steps + wides,
        [whole((count, width))] * n
        + [
            pl.BlockSpec((width, tile), lambda i: (0, first(i))),
            pl.BlockSpec((hidden, wide), lambda i: (0, second(i))),
        ],
        [jax.ShapeDtypeStruct((count, hidden), jnp.float32)] * n
        + [jax.ShapeDtypeStruct((count, hidden), jnp.bfloat16)] * n
        + [jax.ShapeDtypeStruct((count, width), jnp.bfloat16)] * n,
        [part] * (2 * n) + [pl.BlockSpec((count, wide), lambda i: (0, second(i)))] * n,
        [pltpu.VMEM((n, count, hidden), jnp.bfloat16)],
        mib=26,
    )(*rows, w_up, w_down)
    return list(outs[:n]), list(outs[n : 2 * n]), list(outs[2 * n :])


def backward(cots, hiddens, actives, w_up, w_down):
    count, width, hidden, tile, wide, steps, wides = tiles_for(cots[0], w_up)
    n = len(cots)
    lanes = tile_of(tile, 128)
    first, second = lambda i: jnp.minimum(i, steps - 1), lambda i: jnp.maximum(i - steps, 0)
    part = pl.BlockSpec((count, tile), lambda i: (0, first(i)))
    outs = call(
        functools.partial(backward_kernel, n, steps, tile),
        steps + wides,
        [whole((count, width))] * n
        + [part] * (2 * n)
        + [
            pl.BlockSpec((tile, width), lambda i: (first(i), 0)),
            pl.BlockSpec((wide, hidden), lambda i: (second(i), 0)),
        ],
        [jax.ShapeDtypeStruct((count, hidden), jnp.bfloat16)] * n
        + [jax.ShapeDtypeStruct((count, lanes), jnp.float32)] * n
        + [jax.ShapeDtypeStruct((count, width), jnp.bfloat16)] * n,
        [part] * n
        + [whole((count, lanes))] * n
        + [pl.BlockSpec((count, wide), lambda i: (0, second(i)))] * n,
        [pltpu.VMEM((n, count, hidden), jnp.bfloat16)],
        mib=26,
    )(*cots, *hiddens, *actives, w_down, w_up)
    return list(outs[:n]), list(outs[n : 2 * n]), list(outs[2 * n :])


def gradient_kernel(blocks, *refs):
    left, right, out = refs[:blocks], refs[blocks : 2 * blocks], refs[-1]
    total = sum(
        lax.dot_general(
            a[...], b[...], (((0,), (0,)), ((), ())), preferred_element_type=jnp.float32
        )
        for a, b in zip(left, right)
    )
    out[...] = total.astype(out.dtype)


def gradient(lefts, rights, want):
    count, height = lefts[0].shape
    width = rights[0].shape[1]
    tile = tile_of(height, want)
    return call(
        functools.partial(gradient_kernel, len(lefts)),
        height // tile,
        [pl.BlockSpec((count, tile), lambda i: (0, i))] * len(lefts)
        + [whole((count, width))] * len(rights),
        jax.ShapeDtypeStruct((height, width), jnp.bfloat16),
        pl.BlockSpec((tile, width), lambda i: (i, 0)),
        flops=2 * len(lefts) * count * height * width,
        moved=2 * (len(lefts) * count * (height + width) + height * width),
    )(*lefts, *rights)


def make(n_expert, n_tensor):
    top, low = n_tensor // 2, n_tensor // 2

    def cross(x, bit):
        return lax.ppermute(x, "tensor", [(i, i ^ bit) for i in range(n_tensor)])

    def gather_low(rows):
        held = [rows]
        bit = 1
        while bit < low:
            held = held + [cross(h, bit) for h in held]
            bit *= 2
        return held

    def sum_low(terms):
        while len(terms) > 1:
            bit = len(terms) // 2
            terms = [added(a, cross(b, bit)) for a, b in zip(terms[:bit], terms[bit:])]
        return terms[0]

    def per_device(tokens, expert_ids, live_counts, router, up_weight, down_weight, out_grad):
        tok_rows, width = tokens.shape
        experts = router.shape[1]
        most = 3 * tok_rows // (2 * experts)
        slots = experts * most
        me = lax.axis_index("expert")
        ids = expert_ids[:, 0]
        live = lax.iota(jnp.int32, tok_rows) < live_counts[0]
        chosen = ids[:, None] == lax.iota(jnp.int32, experts)[None, :]
        chosen_int = chosen.astype(jnp.int32)
        rank = jnp.sum(jnp.cumsum(chosen_int, axis=0) * chosen_int, axis=1) - 1
        target = jnp.where(live, ids * most + rank, -1)
        placing = (lax.iota(jnp.int32, slots)[:, None] == target[None, :]).astype(jnp.bfloat16)
        w_up, w_down = copied(up_weight[0], down_weight[0], 4)

        def swap(x):
            return lax.all_to_all(x, "expert", split_axis=0, concat_axis=0, tiled=True)

        def exchange(x):
            return swap(x.reshape(experts, most, width)).reshape(slots, width)

        tok_near = exchange(dot(placing, tokens, jnp.bfloat16))
        tok_near = after(tok_near, w_up, w_down)
        logits = dot(tokens, router)
        gate = jax.nn.sigmoid(jnp.sum(logits * chosen.astype(jnp.float32), axis=1))
        out_cot = (gate[:, None] * out_grad.astype(jnp.float32)).astype(jnp.bfloat16)
        cot_near = exchange(after(dot(placing, out_cot, jnp.bfloat16), tok_near))
        tok_far = cross(tok_near, top)
        cot_far = cross(cot_near, top)

        rows = gather_low(after(tok_far, cot_near))
        hidden, active, term = forward(rows, w_up, w_down)
        out_far_sum = sum_low(term)
        near = [after(x, *term) for x in gather_low(tok_near)]
        near_hidden, near_active, near_term = forward(near, w_up, w_down)
        out_near = sum_low(near_term)
        rows, active = rows + near, active + near_active
        cot_far = after(cot_far, *term, *near_term)
        out_far = cross(after(out_far_sum, cot_far), top)

        cots = gather_low(cot_far)
        hidden_cot, slope, term = backward(
            [after(x, out_far_sum) for x in cots], hidden, active[:low], w_up, w_down
        )
        back_far_sum = sum_low(term)
        back_far = cross(back_far_sum, top)
        near = [after(x, *term) for x in gather_low(cot_near)]
        near_hidden_cot, near_slope, near_term = backward(
            near, near_hidden, near_active, w_up, w_down
        )
        back_near = sum_low(near_term)
        cots, hidden_cot, slope = cots + near, hidden_cot + near_hidden_cot, slope + near_slope
        column = lax.dynamic_slice_in_dim(router, me, 1, axis=1)
        off = [1.0 - jax.nn.sigmoid(dot(x, column)) for x in rows]
        out_sum = added(out_near, after(out_far, *near_term, *off))
        out_home = exchange(after(out_sum, back_far_sum))

        columns = jnp.zeros((1, width), jnp.float32)
        for x, lane_sums, rate in zip(rows, slope, off):
            own = jnp.sum(after(lane_sums, back_far), axis=1, keepdims=True) * rate
            high = own.astype(jnp.bfloat16)
            rest = own - high.astype(jnp.float32)
            middle = rest.astype(jnp.bfloat16)
            least = (rest - middle.astype(jnp.float32)).astype(jnp.bfloat16)
            split = jnp.concatenate([high, middle, least], axis=1)
            columns += jnp.sum(dot(split, x, dims=((0,), (0,))), axis=0, keepdims=True)
        bit = 1
        while bit < n_tensor:
            columns = columns + cross(columns, bit)
            bit *= 2
        lanes = -(-width // (most * 128)) * 128
        high = columns.astype(jnp.bfloat16)
        rest = (columns - high.astype(jnp.float32)).astype(jnp.bfloat16)
        beside = jnp.concatenate(
            [
                jnp.pad(x, ((0, 0), (0, most * lanes - width))).reshape(1, most, lanes)
                for x in (high, rest)
            ],
            axis=2,
        )

        back_sum = added(back_near, after(back_far, out_home))

        up_grad = gradient([after(x, back_sum, columns) for x in rows], hidden_cot, 512)[None]
        down_grad = gradient([after(x, back_sum, columns) for x in active], cots, 256)[None]

        back_sum = back_sum.reshape(experts, most, width)
        beside = jnp.broadcast_to(beside, (experts, most, 2 * lanes))
        came = swap(jnp.concatenate([back_sum, beside], axis=2))
        back_home = came[:, :, :width].reshape(slots, width)
        high, rest = (
            came[:, :, k : k + lanes].reshape(experts, most * lanes)[:, :width].astype(jnp.float32)
            for k in (width, width + lanes)
        )
        router_grad = (high + rest).T

        out_rows = dot(placing, after(out_home, back_sum), jnp.bfloat16, ((0,), (0,)))
        cot_rows = dot(placing, back_home, jnp.bfloat16, ((0,), (0,)))
        out_wide = out_rows.astype(jnp.float32)
        mixed = (gate[:, None] * out_wide).astype(jnp.bfloat16)
        own_slope = jnp.sum(out_grad.astype(jnp.float32) * out_wide, axis=1) * gate * (1.0 - gate)
        named = dot(chosen.astype(jnp.bfloat16), router, dims=((1,), (1,)))
        token_grad = (cot_rows.astype(jnp.float32) + own_slope[:, None] * named).astype(jnp.bfloat16)
        return (mixed, token_grad, up_grad, down_grad, router_grad)

    return per_device


def solution(mesh):
    in_specs = (
        P(("expert", "tensor"), None),
        P(("expert", "tensor"), None),
        P(("expert", "tensor")),
        P(),
        P("expert", None, "tensor"),
        P("expert", "tensor", None),
        P(("expert", "tensor"), None),
    )
    out_specs = (
        P(("expert", "tensor"), None),
        P(("expert", "tensor"), None),
        P("expert", None, "tensor"),
        P("expert", "tensor", None),
        P(),
    )
    return jax.shard_map(
        make(mesh.shape["expert"], mesh.shape["tensor"]),
        mesh=mesh,
        in_specs=in_specs,
        out_specs=out_specs,
        check_vma=False,
    )
```

```python
import functools

import jax
import jax.numpy as jnp
from jax import lax
from jax.experimental import pallas as pl
from jax.experimental.pallas import tpu as pltpu
from jax.sharding import PartitionSpec as P


def dot(a, b, out=jnp.float32, dims=((1,), (0,))):
    return lax.dot_general(a, b, (dims, ((), ())), preferred_element_type=jnp.float32).astype(out)


def joined(blocks):
    return jnp.concatenate(blocks, axis=0)


def after(x, *earlier):
    return lax.optimization_barrier((x,) + earlier)[0]


def added(a, b):
    return (a.astype(jnp.float32) + b.astype(jnp.float32)).astype(jnp.bfloat16)


def call(kernel, grid, in_specs, outs, out_specs, scratch=(), flops=1, moved=1, mib=20):
    return pl.pallas_call(
        kernel,
        grid=(grid,),
        in_specs=in_specs,
        out_specs=out_specs,
        out_shape=outs,
        scratch_shapes=scratch,
        compiler_params=pltpu.CompilerParams(vmem_limit_bytes=mib * 1024 * 1024),
        cost_estimate=pl.CostEstimate(flops=flops, bytes_accessed=moved, transcendentals=0),
    )


def tile_of(size, want):
    return want if size % want == 0 else size


def nt(a, b):
    return lax.dot_general(a, b, (((1,), (1,)), ((), ())), preferred_element_type=jnp.float32)


def tn(a, b):
    return lax.dot_general(a, b, (((0,), (0,)), ((), ())), preferred_element_type=jnp.float32)


def forward_kernel(blocks, steps, tile, *refs):
    rows, (up, down) = refs[:blocks], refs[blocks : blocks + 2]
    outs = refs[blocks + 2 : -1]
    hidden, active, term = outs[:blocks], outs[blocks : 2 * blocks], outs[2 * blocks :]
    held = refs[-1]
    step = pl.program_id(0)

    @pl.when(step < steps)
    def _():
        place = pl.ds(pl.multiple_of(step * tile, tile), tile)
        for i in range(blocks):
            value = jnp.dot(rows[i][...], up[...], preferred_element_type=jnp.float32)
            hidden[i][...] = value
            rounded = (value * jax.nn.sigmoid(value)).astype(jnp.bfloat16)
            active[i][...] = rounded
            held[i, :, place] = rounded

    @pl.when(step >= steps)
    def _():
        for i in range(blocks):
            total = jnp.dot(held[i], down[...], preferred_element_type=jnp.float32)
            term[i][...] = total.astype(jnp.bfloat16)


def backward_kernel(blocks, steps, last, tile, *refs):
    cots, hidden, active, rows = (refs[k * blocks : (k + 1) * blocks] for k in range(4))
    down, up, column = refs[4 * blocks : 4 * blocks + 3]
    outs = refs[4 * blocks + 3 : -2]
    hidden_cot, term = (outs[k * blocks : (k + 1) * blocks] for k in range(2))
    total = outs[-1]
    held, slope = refs[-2:]
    step = pl.program_id(0)

    @pl.when(step == 0)
    def _():
        for i in range(blocks):
            slope[i] = jnp.zeros_like(slope[i])

    @pl.when(step < steps)
    def _():
        place = pl.ds(pl.multiple_of(step * tile, tile), tile)
        for i in range(blocks):
            back = nt(cots[i][...], down[...])
            value = hidden[i][...]
            sig = jax.nn.sigmoid(value)
            rounded = (back * (sig * (1.0 + value * (1.0 - sig)))).astype(jnp.bfloat16)
            hidden_cot[i][...] = rounded
            held[i, :, place] = rounded
            product = back * active[i][...].astype(jnp.float32)
            lanes = slope.shape[2]
            slope[i] += sum(product[:, k : k + lanes] for k in range(0, tile, lanes))

    @pl.when(step >= steps)
    def _():
        for i in range(blocks):
            term[i][...] = nt(held[i], up[...]).astype(jnp.bfloat16)

    @pl.when(step == last)
    def _():
        add_up = jnp.zeros(total.shape, jnp.float32)
        for i in range(blocks):
            off = 1.0 - jax.nn.sigmoid(nt(rows[i][...], column[...])[:, :1])
            own = jnp.sum(slope[i], axis=1, keepdims=True) * off
            high = own.astype(jnp.bfloat16)
            rest = own - high.astype(jnp.float32)
            middle = rest.astype(jnp.bfloat16)
            least = rest - middle.astype(jnp.float32)
            lane = lax.broadcasted_iota(jnp.int32, slope.shape[1:], 1)
            split = jnp.zeros(slope.shape[1:], jnp.float32)
            for k, part in enumerate((high, middle, least)):
                split = jnp.where(lane == k, part.astype(jnp.float32), split)
            sums = tn(split.astype(jnp.bfloat16), rows[i][...])
            add_up += sums[0:1] + sums[1:2] + sums[2:3]
        total[...] = add_up


def tiles_for(rows, w_up):
    width, hidden = w_up.shape
    tile, wide = tile_of(hidden, 512), tile_of(width, 1280)
    return rows.shape[0], width, hidden, tile, wide, hidden // tile, width // wide


def whole(shape):
    return pl.BlockSpec(shape, lambda i: (0,) * len(shape), pipeline_mode=pl.Buffered(1))


def forward(rows, w_up, w_down):
    count, width, hidden, tile, wide, steps, wides = tiles_for(rows[0], w_up)
    n = len(rows)
    first, second = lambda i: jnp.minimum(i, steps - 1), lambda i: jnp.maximum(i - steps, 0)
    part = pl.BlockSpec((count, tile), lambda i: (0, first(i)))
    outs = call(
        functools.partial(forward_kernel, n, steps, tile),
        steps + wides,
        [whole((count, width))] * n
        + [
            pl.BlockSpec((width, tile), lambda i: (0, first(i))),
            pl.BlockSpec((hidden, wide), lambda i: (0, second(i))),
        ],
        [jax.ShapeDtypeStruct((count, hidden), jnp.float32)] * n
        + [jax.ShapeDtypeStruct((count, hidden), jnp.bfloat16)] * n
        + [jax.ShapeDtypeStruct((count, width), jnp.bfloat16)] * n,
        [part] * (2 * n) + [pl.BlockSpec((count, wide), lambda i: (0, second(i)))] * n,
        [pltpu.VMEM((n, count, hidden), jnp.bfloat16)],
        mib=56,
    )(*rows, w_up, w_down)
    return list(outs[:n]), list(outs[n : 2 * n]), list(outs[2 * n :])


def backward(cots, hiddens, actives, rows, w_up, w_down, column):
    count, width, hidden, tile, wide, steps, wides = tiles_for(cots[0], w_up)
    n = len(cots)
    first, second = lambda i: jnp.minimum(i, steps - 1), lambda i: jnp.maximum(i - steps, 0)
    part = pl.BlockSpec((count, tile), lambda i: (0, first(i)))
    outs = call(
        functools.partial(backward_kernel, n, steps, steps + wides - 1, tile),
        steps + wides,
        [whole((count, width))] * n
        + [part] * (2 * n)
        + [whole((count, width))] * n
        + [
            pl.BlockSpec((tile, width), lambda i: (first(i), 0)),
            pl.BlockSpec((wide, hidden), lambda i: (second(i), 0)),
            whole(column.shape),
        ],
        [jax.ShapeDtypeStruct((count, hidden), jnp.bfloat16)] * n
        + [jax.ShapeDtypeStruct((count, width), jnp.bfloat16)] * n
        + [jax.ShapeDtypeStruct((1, width), jnp.float32)],
        [part] * n
        + [pl.BlockSpec((count, wide), lambda i: (0, second(i)))] * n
        + [pl.BlockSpec((1, width), lambda i: (0, 0))],
        [
            pltpu.VMEM((n, count, hidden), jnp.bfloat16),
            pltpu.VMEM((n, count, tile_of(tile, 128)), jnp.float32),
        ],
        mib=56,
    )(*cots, *hiddens, *actives, *rows, w_down, w_up, column)
    return list(outs[:n]), list(outs[n : 2 * n]), outs[-1]


def gradient_kernel(blocks, *refs):
    left, right, out = refs[:blocks], refs[blocks : 2 * blocks], refs[-1]
    total = sum(tn(a[...], b[...]) for a, b in zip(left, right))
    out[...] = total.astype(out.dtype)


def gradient(lefts, rights, want):
    count, height = lefts[0].shape
    width = rights[0].shape[1]
    tile = tile_of(height, want)
    return call(
        functools.partial(gradient_kernel, len(lefts)),
        height // tile,
        [pl.BlockSpec((count, tile), lambda i: (0, i))] * len(lefts)
        + [whole((count, width))] * len(rights),
        jax.ShapeDtypeStruct((height, width), jnp.bfloat16),
        pl.BlockSpec((tile, width), lambda i: (i, 0)),
        flops=2 * len(lefts) * count * height * width,
        moved=2 * (len(lefts) * count * (height + width) + height * width),
    )(*lefts, *rights)


def make(n_expert, n_tensor):
    top, low = n_tensor // 2, n_tensor // 2

    def cross(x, bit):
        return lax.ppermute(x, "tensor", [(i, i ^ bit) for i in range(n_tensor)])

    def gather_low(rows):
        held = [rows]
        bit = 1
        while bit < low:
            held = held + [cross(h, bit) for h in held]
            bit *= 2
        return held

    def sum_low(terms):
        while len(terms) > 1:
            bit = len(terms) // 2
            terms = [added(a, cross(b, bit)) for a, b in zip(terms[:bit], terms[bit:])]
        return terms[0]

    def per_device(tokens, expert_ids, live_counts, router, up_weight, down_weight, out_grad):
        tok_rows, width = tokens.shape
        experts = router.shape[1]
        most = 3 * tok_rows // (2 * experts)
        slots = experts * most
        me = lax.axis_index("expert")
        ids = expert_ids[:, 0]
        live = lax.iota(jnp.int32, tok_rows) < live_counts[0]
        chosen = ids[:, None] == lax.iota(jnp.int32, experts)[None, :]
        chosen_int = chosen.astype(jnp.int32)
        rank = jnp.sum(jnp.cumsum(chosen_int, axis=0) * chosen_int, axis=1) - 1
        target = jnp.where(live, ids * most + rank, -1)
        placing = (lax.iota(jnp.int32, slots)[:, None] == target[None, :]).astype(jnp.bfloat16)
        w_up, w_down = up_weight[0], down_weight[0]

        def swap(x):
            return lax.all_to_all(x, "expert", split_axis=0, concat_axis=0, tiled=True)

        def exchange(x):
            return swap(x.reshape(experts, most, width)).reshape(slots, width)

        tok_near = exchange(dot(placing, tokens, jnp.bfloat16))
        logits = dot(tokens, router)
        gate = jax.nn.sigmoid(jnp.sum(logits * chosen.astype(jnp.float32), axis=1))
        out_cot = (gate[:, None] * out_grad.astype(jnp.float32)).astype(jnp.bfloat16)
        cot_near = exchange(after(dot(placing, out_cot, jnp.bfloat16), tok_near))
        tok_far = cross(tok_near, top)
        cot_far = cross(cot_near, top)

        rows = gather_low(after(tok_far, cot_near))
        hidden, active, term = forward(rows, w_up, w_down)
        out_far_sum = sum_low(term)
        near = [after(x, *term) for x in gather_low(tok_near)]
        near_hidden, near_active, near_term = forward(near, w_up, w_down)
        out_near = sum_low(near_term)
        rows, active = rows + near, active + near_active
        cot_far = after(cot_far, *term, *near_term)
        out_far = cross(after(out_far_sum, cot_far), top)

        column = lax.dynamic_slice_in_dim(router, me, 1, axis=1).T
        column = jnp.broadcast_to(column, (16, width))
        cots = gather_low(cot_far)
        hidden_cot, far_term, far_column = backward(
            [after(x, out_far_sum) for x in cots],
            hidden,
            active[:low],
            rows[:low],
            w_up,
            w_down,
            column,
        )
        near = [after(x, *far_term) for x in gather_low(cot_near)]
        near_hidden_cot, near_term, near_column = backward(
            near, near_hidden, active[low:], rows[low:], w_up, w_down, column
        )
        cots, hidden_cot = cots + near, hidden_cot + near_hidden_cot
        out_far = after(out_far, *near_term)
        out_sum = added(out_near, out_far)
        out_home = exchange(out_sum)
        back_far = cross(sum_low([after(x, out_far) for x in far_term]), top)
        back_near = sum_low([after(x, out_far) for x in near_term])

        columns = after(far_column + near_column, out_far)
        bit = 1
        while bit < n_tensor:
            columns = columns + cross(after(columns, back_far) if bit == top else columns, bit)
            bit *= 2
        lanes = -(-width // (most * 128)) * 128
        high = columns.astype(jnp.bfloat16)
        rest = (columns - high.astype(jnp.float32)).astype(jnp.bfloat16)
        beside = jnp.concatenate(
            [
                jnp.pad(x, ((0, 0), (0, most * lanes - width))).reshape(1, most, lanes)
                for x in (high, rest)
            ],
            axis=2,
        )

        back_sum = added(back_near, after(back_far, out_home))

        up_grad = gradient([after(x, back_sum, columns) for x in rows], hidden_cot, 512)[None]
        down_grad = gradient([after(x, back_sum, columns) for x in active], cots, 256)[None]

        back_sum = back_sum.reshape(experts, most, width)
        beside = jnp.broadcast_to(beside, (experts, most, 2 * lanes))
        came = swap(jnp.concatenate([back_sum, beside], axis=2))
        back_home = came[:, :, :width].reshape(slots, width)
        high, rest = (
            came[:, :, k : k + lanes].reshape(experts, most * lanes)[:, :width].astype(jnp.float32)
            for k in (width, width + lanes)
        )
        router_grad = (high + rest).T

        out_rows = dot(placing, after(out_home, back_sum), jnp.bfloat16, ((0,), (0,)))
        cot_rows = dot(placing, back_home, jnp.bfloat16, ((0,), (0,)))
        out_wide = out_rows.astype(jnp.float32)
        mixed = (gate[:, None] * out_wide).astype(jnp.bfloat16)
        own_slope = jnp.sum(out_grad.astype(jnp.float32) * out_wide, axis=1) * gate * (1.0 - gate)
        named = dot(chosen.astype(jnp.bfloat16), router, dims=((1,), (1,)))
        token_grad = (cot_rows.astype(jnp.float32) + own_slope[:, None] * named).astype(jnp.bfloat16)
        return (mixed, token_grad, up_grad, down_grad, router_grad)

    return per_device


def solution(mesh):
    in_specs = (
        P(("expert", "tensor"), None),
        P(("expert", "tensor"), None),
        P(("expert", "tensor")),
        P(),
        P("expert", None, "tensor"),
        P("expert", "tensor", None),
        P(("expert", "tensor"), None),
    )
    out_specs = (
        P(("expert", "tensor"), None),
        P(("expert", "tensor"), None),
        P("expert", None, "tensor"),
        P("expert", "tensor", None),
        P(),
    )
    return jax.shard_map(
        make(mesh.shape["expert"], mesh.shape["tensor"]),
        mesh=mesh,
        in_specs=in_specs,
        out_specs=out_specs,
        check_vma=False,
    )
```

```python
import functools

import jax
import jax.numpy as jnp
from jax import lax
from jax.experimental import pallas as pl
from jax.experimental.pallas import tpu as pltpu
from jax.sharding import PartitionSpec as P


def dot(a, b, out=jnp.float32, dims=((1,), (0,))):
    return lax.dot_general(a, b, (dims, ((), ())), preferred_element_type=jnp.float32).astype(out)


def joined(blocks):
    return jnp.concatenate(blocks, axis=0)


def after(x, *earlier):
    return lax.optimization_barrier((x,) + earlier)[0]


def added(a, b):
    return (a.astype(jnp.float32) + b.astype(jnp.float32)).astype(jnp.bfloat16)


def call(kernel, grid, in_specs, outs, out_specs, scratch=(), flops=1, moved=1, mib=20):
    return pl.pallas_call(
        kernel,
        grid=(grid,),
        in_specs=in_specs,
        out_specs=out_specs,
        out_shape=outs,
        scratch_shapes=scratch,
        compiler_params=pltpu.CompilerParams(vmem_limit_bytes=mib * 1024 * 1024),
        cost_estimate=pl.CostEstimate(flops=flops, bytes_accessed=moved, transcendentals=0),
    )


def tile_of(size, want):
    return want if size % want == 0 else size


def nt(a, b):
    return lax.dot_general(a, b, (((1,), (1,)), ((), ())), preferred_element_type=jnp.float32)


def tn(a, b):
    return lax.dot_general(a, b, (((0,), (0,)), ((), ())), preferred_element_type=jnp.float32)


def join_blocks(blocks, joint):
    count = blocks[0].shape[0]
    for i, block in enumerate(blocks):
        joint[i * count : (i + 1) * count] = block[...]


def split_blocks(value, blocks):
    count = blocks[0].shape[0]
    for i, block in enumerate(blocks):
        block[...] = value[i * count : (i + 1) * count].astype(block.dtype)


def forward_kernel(blocks, steps, tile, *refs):
    rows, (up, down) = refs[:blocks], refs[blocks : blocks + 2]
    outs = refs[blocks + 2 : -2]
    hidden, active, term = outs[:blocks], outs[blocks : 2 * blocks], outs[2 * blocks :]
    joint, held = refs[-2:]
    step = pl.program_id(0)

    @pl.when(step == 0)
    def _():
        join_blocks(rows, joint)

    @pl.when(step < steps)
    def _():
        place = pl.ds(pl.multiple_of(step * tile, tile), tile)
        value = jnp.dot(joint[...], up[...], preferred_element_type=jnp.float32)
        split_blocks(value, hidden)
        rounded = (value * jax.nn.sigmoid(value)).astype(jnp.bfloat16)
        split_blocks(rounded, active)
        held[:, place] = rounded

    @pl.when(step >= steps)
    def _():
        split_blocks(jnp.dot(held[...], down[...], preferred_element_type=jnp.float32), term)


def backward_kernel(blocks, steps, last, tile, *refs):
    cots, hidden, active, rows = (refs[k * blocks : (k + 1) * blocks] for k in range(4))
    down, up, column = refs[4 * blocks : 4 * blocks + 3]
    outs = refs[4 * blocks + 3 : -3]
    hidden_cot, term = (outs[k * blocks : (k + 1) * blocks] for k in range(2))
    total = outs[-1]
    joint, held, slope = refs[-3:]
    count = cots[0].shape[0]
    step = pl.program_id(0)

    @pl.when(step == 0)
    def _():
        join_blocks(cots, joint)
        slope[...] = jnp.zeros_like(slope)

    @pl.when(step < steps)
    def _():
        place = pl.ds(pl.multiple_of(step * tile, tile), tile)
        back_all = nt(joint[...], down[...])
        for i in range(blocks):
            back = back_all[i * count : (i + 1) * count]
            value = hidden[i][...]
            sig = jax.nn.sigmoid(value)
            rounded = (back * (sig * (1.0 + value * (1.0 - sig)))).astype(jnp.bfloat16)
            hidden_cot[i][...] = rounded
            held[i * count : (i + 1) * count, place] = rounded
            product = back * active[i][...].astype(jnp.float32)
            lanes = slope.shape[2]
            slope[i] += sum(product[:, k : k + lanes] for k in range(0, tile, lanes))

    @pl.when(step >= steps)
    def _():
        split_blocks(nt(held[...], up[...]), term)

    @pl.when(step == last)
    def _():
        add_up = jnp.zeros(total.shape, jnp.float32)
        for i in range(blocks):
            off = 1.0 - jax.nn.sigmoid(nt(rows[i][...], column[...])[:, :1])
            own = jnp.sum(slope[i], axis=1, keepdims=True) * off
            high = own.astype(jnp.bfloat16)
            rest = own - high.astype(jnp.float32)
            middle = rest.astype(jnp.bfloat16)
            least = rest - middle.astype(jnp.float32)
            lane = lax.broadcasted_iota(jnp.int32, slope.shape[1:], 1)
            split = jnp.zeros(slope.shape[1:], jnp.float32)
            for k, part in enumerate((high, middle, least)):
                split = jnp.where(lane == k, part.astype(jnp.float32), split)
            sums = tn(split.astype(jnp.bfloat16), rows[i][...])
            add_up += sums[0:1] + sums[1:2] + sums[2:3]
        total[...] = add_up


def tiles_for(rows, w_up):
    width, hidden = w_up.shape
    tile, wide = tile_of(hidden, 512), tile_of(width, 1280)
    return rows.shape[0], width, hidden, tile, wide, hidden // tile, width // wide


def whole(shape):
    return pl.BlockSpec(shape, lambda i: (0,) * len(shape), pipeline_mode=pl.Buffered(1))


def forward(rows, w_up, w_down):
    count, width, hidden, tile, wide, steps, wides = tiles_for(rows[0], w_up)
    n = len(rows)
    first, second = lambda i: jnp.minimum(i, steps - 1), lambda i: jnp.maximum(i - steps, 0)
    part = pl.BlockSpec((count, tile), lambda i: (0, first(i)))
    outs = call(
        functools.partial(forward_kernel, n, steps, tile),
        steps + wides,
        [whole((count, width))] * n
        + [
            pl.BlockSpec((width, tile), lambda i: (0, first(i))),
            pl.BlockSpec((hidden, wide), lambda i: (0, second(i))),
        ],
        [jax.ShapeDtypeStruct((count, hidden), jnp.float32)] * n
        + [jax.ShapeDtypeStruct((count, hidden), jnp.bfloat16)] * n
        + [jax.ShapeDtypeStruct((count, width), jnp.bfloat16)] * n,
        [part] * (2 * n) + [pl.BlockSpec((count, wide), lambda i: (0, second(i)))] * n,
        [
            pltpu.VMEM((n * count, width), jnp.bfloat16),
            pltpu.VMEM((n * count, hidden), jnp.bfloat16),
        ],
        mib=56,
    )(*rows, w_up, w_down)
    return list(outs[:n]), list(outs[n : 2 * n]), list(outs[2 * n :])


def backward(cots, hiddens, actives, rows, w_up, w_down, column):
    count, width, hidden, tile, wide, steps, wides = tiles_for(cots[0], w_up)
    n = len(cots)
    first, second = lambda i: jnp.minimum(i, steps - 1), lambda i: jnp.maximum(i - steps, 0)
    part = pl.BlockSpec((count, tile), lambda i: (0, first(i)))
    outs = call(
        functools.partial(backward_kernel, n, steps, steps + wides - 1, tile),
        steps + wides,
        [whole((count, width))] * n
        + [part] * (2 * n)
        + [whole((count, width))] * n
        + [
            pl.BlockSpec((tile, width), lambda i: (first(i), 0)),
            pl.BlockSpec((wide, hidden), lambda i: (second(i), 0)),
            whole(column.shape),
        ],
        [jax.ShapeDtypeStruct((count, hidden), jnp.bfloat16)] * n
        + [jax.ShapeDtypeStruct((count, width), jnp.bfloat16)] * n
        + [jax.ShapeDtypeStruct((1, width), jnp.float32)],
        [part] * n
        + [pl.BlockSpec((count, wide), lambda i: (0, second(i)))] * n
        + [pl.BlockSpec((1, width), lambda i: (0, 0))],
        [
            pltpu.VMEM((n * count, width), jnp.bfloat16),
            pltpu.VMEM((n * count, hidden), jnp.bfloat16),
            pltpu.VMEM((n, count, tile_of(tile, 128)), jnp.float32),
        ],
        mib=56,
    )(*cots, *hiddens, *actives, *rows, w_down, w_up, column)
    return list(outs[:n]), list(outs[n : 2 * n]), outs[-1]


def gradient_kernel(blocks, *refs):
    left, right, out = refs[:blocks], refs[blocks : 2 * blocks], refs[-1]
    total = sum(tn(a[...], b[...]) for a, b in zip(left, right))
    out[...] = total.astype(out.dtype)


def gradient(lefts, rights, want):
    count, height = lefts[0].shape
    width = rights[0].shape[1]
    tile = tile_of(height, want)
    return call(
        functools.partial(gradient_kernel, len(lefts)),
        height // tile,
        [pl.BlockSpec((count, tile), lambda i: (0, i))] * len(lefts)
        + [whole((count, width))] * len(rights),
        jax.ShapeDtypeStruct((height, width), jnp.bfloat16),
        pl.BlockSpec((tile, width), lambda i: (i, 0)),
        flops=2 * len(lefts) * count * height * width,
        moved=2 * (len(lefts) * count * (height + width) + height * width),
    )(*lefts, *rights)


def make(n_expert, n_tensor):
    top, low = n_tensor // 2, n_tensor // 2

    def cross(x, bit):
        return lax.ppermute(x, "tensor", [(i, i ^ bit) for i in range(n_tensor)])

    def gather_low(rows):
        held = [rows]
        bit = 1
        while bit < low:
            held = held + [cross(h, bit) for h in held]
            bit *= 2
        return held

    def sum_low(terms):
        while len(terms) > 1:
            bit = len(terms) // 2
            terms = [added(a, cross(b, bit)) for a, b in zip(terms[:bit], terms[bit:])]
        return terms[0]

    def per_device(tokens, expert_ids, live_counts, router, up_weight, down_weight, out_grad):
        tok_rows, width = tokens.shape
        experts = router.shape[1]
        most = 3 * tok_rows // (2 * experts)
        slots = experts * most
        me = lax.axis_index("expert")
        ids = expert_ids[:, 0]
        live = lax.iota(jnp.int32, tok_rows) < live_counts[0]
        chosen = ids[:, None] == lax.iota(jnp.int32, experts)[None, :]
        chosen_int = chosen.astype(jnp.int32)
        rank = jnp.sum(jnp.cumsum(chosen_int, axis=0) * chosen_int, axis=1) - 1
        target = jnp.where(live, ids * most + rank, -1)
        placing = (lax.iota(jnp.int32, slots)[:, None] == target[None, :]).astype(jnp.bfloat16)
        w_up, w_down = up_weight[0], down_weight[0]

        def swap(x):
            return lax.all_to_all(x, "expert", split_axis=0, concat_axis=0, tiled=True)

        def exchange(x):
            return swap(x.reshape(experts, most, width)).reshape(slots, width)

        tok_near = exchange(dot(placing, tokens, jnp.bfloat16))
        logits = dot(tokens, router)
        gate = jax.nn.sigmoid(jnp.sum(logits * chosen.astype(jnp.float32), axis=1))
        out_cot = (gate[:, None] * out_grad.astype(jnp.float32)).astype(jnp.bfloat16)
        cot_near = exchange(after(dot(placing, out_cot, jnp.bfloat16), tok_near))
        tok_far = cross(tok_near, top)
        cot_far = cross(cot_near, top)

        rows = gather_low(after(tok_far, cot_near))
        hidden, active, term = forward(rows, w_up, w_down)
        out_far_sum = sum_low(term)
        near = [after(x, *term) for x in gather_low(tok_near)]
        near_hidden, near_active, near_term = forward(near, w_up, w_down)
        out_near = sum_low(near_term)
        rows, active = rows + near, active + near_active
        cot_far = after(cot_far, *term, *near_term)
        out_far = cross(after(out_far_sum, cot_far), top)

        column = lax.dynamic_slice_in_dim(router, me, 1, axis=1).T
        column = jnp.broadcast_to(column, (16, width))
        cots = gather_low(cot_far)
        hidden_cot, far_term, far_column = backward(
            [after(x, out_far_sum) for x in cots],
            hidden,
            active[:low],
            rows[:low],
            w_up,
            w_down,
            column,
        )
        out_far = after(out_far, *far_term)
        out_sum = added(out_near, out_far)
        out_home = exchange(out_sum)
        back_far_sum = sum_low([after(x, out_far) for x in far_term])
        back_far = cross(back_far_sum, top)

        near = [after(x, out_sum, back_far_sum) for x in gather_low(cot_near)]
        near_hidden_cot, near_term, near_column = backward(
            near, near_hidden, active[low:], rows[low:], w_up, w_down, column
        )
        back_near = sum_low([after(x, back_far) for x in near_term])
        cots, hidden_cot = cots + near, hidden_cot + near_hidden_cot

        columns = after(far_column + near_column, back_far)
        bit = 1
        while bit < n_tensor:
            columns = columns + cross(after(columns, out_home) if bit == top else columns, bit)
            bit *= 2
        lanes = -(-width // (most * 128)) * 128
        high = columns.astype(jnp.bfloat16)
        rest = (columns - high.astype(jnp.float32)).astype(jnp.bfloat16)
        beside = jnp.concatenate(
            [
                jnp.pad(x, ((0, 0), (0, most * lanes - width))).reshape(1, most, lanes)
                for x in (high, rest)
            ],
            axis=2,
        )

        back_sum = added(back_near, after(back_far, out_home))

        up_grad = gradient([after(x, back_sum, columns) for x in rows], hidden_cot, 512)[None]
        down_grad = gradient([after(x, back_sum, columns) for x in active], cots, 256)[None]

        back_sum = back_sum.reshape(experts, most, width)
        beside = jnp.broadcast_to(beside, (experts, most, 2 * lanes))
        came = swap(jnp.concatenate([back_sum, beside], axis=2))
        back_home = came[:, :, :width].reshape(slots, width)
        high, rest = (
            came[:, :, k : k + lanes].reshape(experts, most * lanes)[:, :width].astype(jnp.float32)
            for k in (width, width + lanes)
        )
        router_grad = (high + rest).T

        out_rows = dot(placing, after(out_home, back_sum), jnp.bfloat16, ((0,), (0,)))
        cot_rows = dot(placing, back_home, jnp.bfloat16, ((0,), (0,)))
        out_wide = out_rows.astype(jnp.float32)
        mixed = (gate[:, None] * out_wide).astype(jnp.bfloat16)
        own_slope = jnp.sum(out_grad.astype(jnp.float32) * out_wide, axis=1) * gate * (1.0 - gate)
        named = dot(chosen.astype(jnp.bfloat16), router, dims=((1,), (1,)))
        token_grad = (cot_rows.astype(jnp.float32) + own_slope[:, None] * named).astype(jnp.bfloat16)
        return (mixed, token_grad, up_grad, down_grad, router_grad)

    return per_device


def solution(mesh):
    in_specs = (
        P(("expert", "tensor"), None),
        P(("expert", "tensor"), None),
        P(("expert", "tensor")),
        P(),
        P("expert", None, "tensor"),
        P("expert", "tensor", None),
        P(("expert", "tensor"), None),
    )
    out_specs = (
        P(("expert", "tensor"), None),
        P(("expert", "tensor"), None),
        P("expert", None, "tensor"),
        P("expert", "tensor", None),
        P(),
    )
    return jax.shard_map(
        make(mesh.shape["expert"], mesh.shape["tensor"]),
        mesh=mesh,
        in_specs=in_specs,
        out_specs=out_specs,
        check_vma=False,
    )
```

```python
import functools

import jax
import jax.numpy as jnp
from jax import lax
from jax.experimental import pallas as pl
from jax.experimental.pallas import tpu as pltpu
from jax.sharding import PartitionSpec as P


def dot(a, b, out=jnp.float32, dims=((1,), (0,))):
    return lax.dot_general(a, b, (dims, ((), ())), preferred_element_type=jnp.float32).astype(out)


def joined(blocks):
    return jnp.concatenate(blocks, axis=0)


def after(x, *earlier):
    return lax.optimization_barrier((x,) + earlier)[0]


def added(a, b):
    return (a.astype(jnp.float32) + b.astype(jnp.float32)).astype(jnp.bfloat16)


def call(kernel, grid, in_specs, outs, out_specs, scratch=(), flops=1, moved=1, mib=20):
    return pl.pallas_call(
        kernel,
        grid=(grid,),
        in_specs=in_specs,
        out_specs=out_specs,
        out_shape=outs,
        scratch_shapes=scratch,
        compiler_params=pltpu.CompilerParams(vmem_limit_bytes=mib * 1024 * 1024),
        cost_estimate=pl.CostEstimate(flops=flops, bytes_accessed=moved, transcendentals=0),
    )


def tile_of(size, want):
    return want if size % want == 0 else size


def nt(a, b):
    return lax.dot_general(a, b, (((1,), (1,)), ((), ())), preferred_element_type=jnp.float32)


def tn(a, b):
    return lax.dot_general(a, b, (((0,), (0,)), ((), ())), preferred_element_type=jnp.float32)


def join_blocks(blocks, joint):
    count = blocks[0].shape[0]
    for i, block in enumerate(blocks):
        joint[i * count : (i + 1) * count] = block[...]


def split_blocks(value, blocks):
    count = blocks[0].shape[0]
    for i, block in enumerate(blocks):
        block[...] = value[i * count : (i + 1) * count].astype(block.dtype)


def forward_kernel(blocks, steps, tile, *refs):
    rows, (up, down) = refs[:blocks], refs[blocks : blocks + 2]
    outs = refs[blocks + 2 : -2]
    hidden, active, term = outs[:blocks], outs[blocks : 2 * blocks], outs[2 * blocks :]
    joint, held = refs[-2:]
    step = pl.program_id(0)

    @pl.when(step == 0)
    def _():
        join_blocks(rows, joint)

    @pl.when(step < steps)
    def _():
        place = pl.ds(pl.multiple_of(step * tile, tile), tile)
        value = jnp.dot(joint[...], up[...], preferred_element_type=jnp.float32)
        split_blocks(value, hidden)
        rounded = (value * jax.nn.sigmoid(value)).astype(jnp.bfloat16)
        split_blocks(rounded, active)
        held[:, place] = rounded

    @pl.when(step >= steps)
    def _():
        split_blocks(jnp.dot(held[...], down[...], preferred_element_type=jnp.float32), term)


def backward_kernel(blocks, steps, last, tile, *refs):
    cots, hidden, active, rows = (refs[k * blocks : (k + 1) * blocks] for k in range(4))
    down, up, column = refs[4 * blocks : 4 * blocks + 3]
    outs = refs[4 * blocks + 3 : -3]
    hidden_cot, term = (outs[k * blocks : (k + 1) * blocks] for k in range(2))
    total = outs[-1]
    joint, held, slope = refs[-3:]
    count = cots[0].shape[0]
    step = pl.program_id(0)

    @pl.when(step == 0)
    def _():
        join_blocks(cots, joint)
        slope[...] = jnp.zeros_like(slope)

    @pl.when(step < steps)
    def _():
        place = pl.ds(pl.multiple_of(step * tile, tile), tile)
        back_all = nt(joint[...], down[...])
        for i in range(blocks):
            back = back_all[i * count : (i + 1) * count]
            value = hidden[i][...]
            sig = jax.nn.sigmoid(value)
            rounded = (back * (sig * (1.0 + value * (1.0 - sig)))).astype(jnp.bfloat16)
            hidden_cot[i][...] = rounded
            held[i * count : (i + 1) * count, place] = rounded
            product = back * active[i][...].astype(jnp.float32)
            lanes = slope.shape[2]
            slope[i] += sum(product[:, k : k + lanes] for k in range(0, tile, lanes))

    @pl.when(step >= steps)
    def _():
        split_blocks(nt(held[...], up[...]), term)

    @pl.when(step == last)
    def _():
        add_up = jnp.zeros(total.shape, jnp.float32)
        for i in range(blocks):
            off = 1.0 - jax.nn.sigmoid(nt(rows[i][...], column[...])[:, :1])
            own = jnp.sum(slope[i], axis=1, keepdims=True) * off
            high = own.astype(jnp.bfloat16)
            rest = own - high.astype(jnp.float32)
            middle = rest.astype(jnp.bfloat16)
            least = rest - middle.astype(jnp.float32)
            lane = lax.broadcasted_iota(jnp.int32, slope.shape[1:], 1)
            split = jnp.zeros(slope.shape[1:], jnp.float32)
            for k, part in enumerate((high, middle, least)):
                split = jnp.where(lane == k, part.astype(jnp.float32), split)
            sums = tn(split.astype(jnp.bfloat16), rows[i][...])
            add_up += sums[0:1] + sums[1:2] + sums[2:3]
        total[...] = add_up


def tiles_for(rows, w_up):
    width, hidden = w_up.shape
    tile, wide = tile_of(hidden, 512), tile_of(width, 1280)
    return rows.shape[0], width, hidden, tile, wide, hidden // tile, width // wide


def whole(shape):
    return pl.BlockSpec(shape, lambda i: (0,) * len(shape), pipeline_mode=pl.Buffered(1))


def forward(rows, w_up, w_down):
    count, width, hidden, tile, wide, steps, wides = tiles_for(rows[0], w_up)
    n = len(rows)
    first, second = lambda i: jnp.minimum(i, steps - 1), lambda i: jnp.maximum(i - steps, 0)
    part = pl.BlockSpec((count, tile), lambda i: (0, first(i)))
    outs = call(
        functools.partial(forward_kernel, n, steps, tile),
        steps + wides,
        [whole((count, width))] * n
        + [
            pl.BlockSpec((width, tile), lambda i: (0, first(i))),
            pl.BlockSpec((hidden, wide), lambda i: (0, second(i))),
        ],
        [jax.ShapeDtypeStruct((count, hidden), jnp.float32)] * n
        + [jax.ShapeDtypeStruct((count, hidden), jnp.bfloat16)] * n
        + [jax.ShapeDtypeStruct((count, width), jnp.bfloat16)] * n,
        [part] * (2 * n) + [pl.BlockSpec((count, wide), lambda i: (0, second(i)))] * n,
        [
            pltpu.VMEM((n * count, width), jnp.bfloat16),
            pltpu.VMEM((n * count, hidden), jnp.bfloat16),
        ],
        mib=56,
    )(*rows, w_up, w_down)
    return list(outs[:n]), list(outs[n : 2 * n]), list(outs[2 * n :])


def backward(cots, hiddens, actives, rows, w_up, w_down, column):
    count, width, hidden, tile, wide, steps, wides = tiles_for(cots[0], w_up)
    n = len(cots)
    first, second = lambda i: jnp.minimum(i, steps - 1), lambda i: jnp.maximum(i - steps, 0)
    part = pl.BlockSpec((count, tile), lambda i: (0, first(i)))
    outs = call(
        functools.partial(backward_kernel, n, steps, steps + wides - 1, tile),
        steps + wides,
        [whole((count, width))] * n
        + [part] * (2 * n)
        + [whole((count, width))] * n
        + [
            pl.BlockSpec((tile, width), lambda i: (first(i), 0)),
            pl.BlockSpec((wide, hidden), lambda i: (second(i), 0)),
            whole(column.shape),
        ],
        [jax.ShapeDtypeStruct((count, hidden), jnp.bfloat16)] * n
        + [jax.ShapeDtypeStruct((count, width), jnp.bfloat16)] * n
        + [jax.ShapeDtypeStruct((1, width), jnp.float32)],
        [part] * n
        + [pl.BlockSpec((count, wide), lambda i: (0, second(i)))] * n
        + [pl.BlockSpec((1, width), lambda i: (0, 0))],
        [
            pltpu.VMEM((n * count, width), jnp.bfloat16),
            pltpu.VMEM((n * count, hidden), jnp.bfloat16),
            pltpu.VMEM((n, count, tile_of(tile, 128)), jnp.float32),
        ],
        mib=56,
    )(*cots, *hiddens, *actives, *rows, w_down, w_up, column)
    return list(outs[:n]), list(outs[n : 2 * n]), outs[-1]


def gradient_kernel(blocks, *refs):
    left, right, out = refs[:blocks], refs[blocks : 2 * blocks], refs[-1]
    total = sum(tn(a[...], b[...]) for a, b in zip(left, right))
    out[...] = total.astype(out.dtype)


def gradient(lefts, rights, want):
    count, height = lefts[0].shape
    width = rights[0].shape[1]
    tile = tile_of(height, want)
    return call(
        functools.partial(gradient_kernel, len(lefts)),
        height // tile,
        [pl.BlockSpec((count, tile), lambda i: (0, i))] * len(lefts)
        + [whole((count, width))] * len(rights),
        jax.ShapeDtypeStruct((height, width), jnp.bfloat16),
        pl.BlockSpec((tile, width), lambda i: (i, 0)),
        flops=2 * len(lefts) * count * height * width,
        moved=2 * (len(lefts) * count * (height + width) + height * width),
    )(*lefts, *rights)


def make(n_expert, n_tensor):
    top, low = n_tensor // 2, n_tensor // 2

    def cross(x, bit):
        return lax.ppermute(x, "tensor", [(i, i ^ bit) for i in range(n_tensor)])

    def gather_low(rows):
        held = [rows]
        bit = 1
        while bit < low:
            held = held + [cross(h, bit) for h in held]
            bit *= 2
        return held

    def sum_low(terms):
        while len(terms) > 1:
            bit = len(terms) // 2
            terms = [added(a, cross(b, bit)) for a, b in zip(terms[:bit], terms[bit:])]
        return terms[0]

    def per_device(tokens, expert_ids, live_counts, router, up_weight, down_weight, out_grad):
        tok_rows, width = tokens.shape
        experts = router.shape[1]
        most = 3 * tok_rows // (2 * experts)
        slots = experts * most
        me = lax.axis_index("expert")
        ids = expert_ids[:, 0]
        live = lax.iota(jnp.int32, tok_rows) < live_counts[0]
        chosen = ids[:, None] == lax.iota(jnp.int32, experts)[None, :]
        chosen_int = chosen.astype(jnp.int32)
        rank = jnp.sum(jnp.cumsum(chosen_int, axis=0) * chosen_int, axis=1) - 1
        target = jnp.where(live, ids * most + rank, -1)
        placing = (lax.iota(jnp.int32, slots)[:, None] == target[None, :]).astype(jnp.bfloat16)
        w_up, w_down = up_weight[0], down_weight[0]

        def swap(x):
            return lax.all_to_all(x, "expert", split_axis=0, concat_axis=0, tiled=True)

        def exchange(x):
            return swap(x.reshape(experts, most, width)).reshape(slots, width)

        tok_near = exchange(dot(placing, tokens, jnp.bfloat16))
        logits = dot(tokens, router)
        gate = jax.nn.sigmoid(jnp.sum(logits * chosen.astype(jnp.float32), axis=1))
        out_cot = (gate[:, None] * out_grad.astype(jnp.float32)).astype(jnp.bfloat16)
        cot_near = exchange(after(dot(placing, out_cot, jnp.bfloat16), tok_near))
        tok_far = cross(tok_near, top)
        cot_far = cross(cot_near, top)

        rows = gather_low(after(tok_far, cot_near)) + gather_low(tok_near)
        hidden, active, term = forward(rows, w_up, w_down)
        out_far_sum, out_near = sum_low(term[:low]), sum_low(term[low:])
        cot_far = after(cot_far, *term)
        out_far = cross(after(out_far_sum, cot_far), top)

        column = lax.dynamic_slice_in_dim(router, me, 1, axis=1).T
        column = jnp.broadcast_to(column, (16, width))
        cots = gather_low(cot_far)
        hidden_cot, far_term, far_column = backward(
            [after(x, out_far_sum) for x in cots],
            hidden[:low],
            active[:low],
            rows[:low],
            w_up,
            w_down,
            column,
        )
        out_far = after(out_far, *far_term)
        out_sum = added(out_near, out_far)
        out_home = exchange(out_sum)
        back_far_sum = sum_low([after(x, out_far) for x in far_term])
        back_far = cross(back_far_sum, top)

        near = [after(x, out_sum, back_far_sum) for x in gather_low(cot_near)]
        near_hidden_cot, near_term, near_column = backward(
            near, hidden[low:], active[low:], rows[low:], w_up, w_down, column
        )
        back_near = sum_low([after(x, back_far) for x in near_term])
        cots, hidden_cot = cots + near, hidden_cot + near_hidden_cot

        columns = far_column + near_column
        bit = 1
        while bit < n_tensor:
            columns = columns + cross(columns, bit)
            bit *= 2
        columns = after(columns, out_home)
        lanes = -(-width // (most * 128)) * 128
        high = columns.astype(jnp.bfloat16)
        rest = (columns - high.astype(jnp.float32)).astype(jnp.bfloat16)
        beside = jnp.concatenate(
            [
                jnp.pad(x, ((0, 0), (0, most * lanes - width))).reshape(1, most, lanes)
                for x in (high, rest)
            ],
            axis=2,
        )

        back_sum = added(back_near, after(back_far, out_home))

        up_grad = gradient([after(x, back_sum, columns) for x in rows], hidden_cot, 512)[None]
        down_grad = gradient([after(x, back_sum, columns) for x in active], cots, 256)[None]

        back_sum = back_sum.reshape(experts, most, width)
        beside = jnp.broadcast_to(beside, (experts, most, 2 * lanes))
        came = swap(jnp.concatenate([back_sum, beside], axis=2))
        back_home = came[:, :, :width].reshape(slots, width)
        high, rest = (
            came[:, :, k : k + lanes].reshape(experts, most * lanes)[:, :width].astype(jnp.float32)
            for k in (width, width + lanes)
        )
        router_grad = (high + rest).T

        out_rows = dot(placing, after(out_home, back_sum), jnp.bfloat16, ((0,), (0,)))
        cot_rows = dot(placing, back_home, jnp.bfloat16, ((0,), (0,)))
        out_wide = out_rows.astype(jnp.float32)
        mixed = (gate[:, None] * out_wide).astype(jnp.bfloat16)
        own_slope = jnp.sum(out_grad.astype(jnp.float32) * out_wide, axis=1) * gate * (1.0 - gate)
        named = dot(chosen.astype(jnp.bfloat16), router, dims=((1,), (1,)))
        token_grad = (cot_rows.astype(jnp.float32) + own_slope[:, None] * named).astype(jnp.bfloat16)
        return (mixed, token_grad, up_grad, down_grad, router_grad)

    return per_device


def solution(mesh):
    in_specs = (
        P(("expert", "tensor"), None),
        P(("expert", "tensor"), None),
        P(("expert", "tensor")),
        P(),
        P("expert", None, "tensor"),
        P("expert", "tensor", None),
        P(("expert", "tensor"), None),
    )
    out_specs = (
        P(("expert", "tensor"), None),
        P(("expert", "tensor"), None),
        P("expert", None, "tensor"),
        P("expert", "tensor", None),
        P(),
    )
    return jax.shard_map(
        make(mesh.shape["expert"], mesh.shape["tensor"]),
        mesh=mesh,
        in_specs=in_specs,
        out_specs=out_specs,
        check_vma=False,
    )
```

```python
import functools

import jax
import jax.numpy as jnp
from jax import lax
from jax.experimental import pallas as pl
from jax.experimental.pallas import tpu as pltpu
from jax.sharding import PartitionSpec as P


def dot(a, b, out=jnp.float32, dims=((1,), (0,))):
    return lax.dot_general(a, b, (dims, ((), ())), preferred_element_type=jnp.float32).astype(out)


def joined(blocks):
    return jnp.concatenate(blocks, axis=0)


def after(x, *earlier):
    return lax.optimization_barrier((x,) + earlier)[0]


def added(a, b):
    return (a.astype(jnp.float32) + b.astype(jnp.float32)).astype(jnp.bfloat16)


def call(kernel, grid, in_specs, outs, out_specs, scratch=(), flops=1, moved=1, mib=20):
    return pl.pallas_call(
        kernel,
        grid=(grid,),
        in_specs=in_specs,
        out_specs=out_specs,
        out_shape=outs,
        scratch_shapes=scratch,
        compiler_params=pltpu.CompilerParams(vmem_limit_bytes=mib * 1024 * 1024),
        cost_estimate=pl.CostEstimate(flops=flops, bytes_accessed=moved, transcendentals=0),
    )


def tile_of(size, want):
    return want if size % want == 0 else size


def nt(a, b):
    return lax.dot_general(a, b, (((1,), (1,)), ((), ())), preferred_element_type=jnp.float32)


def tn(a, b):
    return lax.dot_general(a, b, (((0,), (0,)), ((), ())), preferred_element_type=jnp.float32)


def join_blocks(blocks, joint):
    count = blocks[0].shape[0]
    for i, block in enumerate(blocks):
        joint[i * count : (i + 1) * count] = block[...]


def split_blocks(value, blocks):
    count = blocks[0].shape[0]
    for i, block in enumerate(blocks):
        block[...] = value[i * count : (i + 1) * count].astype(block.dtype)


def forward_kernel(blocks, steps, tile, *refs):
    rows, (up, down) = refs[:blocks], refs[blocks : blocks + 2]
    outs = refs[blocks + 2 : -2]
    hidden, active, term = outs[:blocks], outs[blocks : 2 * blocks], outs[2 * blocks :]
    joint, held = refs[-2:]
    step = pl.program_id(0)

    @pl.when(step == 0)
    def _():
        join_blocks(rows, joint)

    @pl.when(step < steps)
    def _():
        place = pl.ds(pl.multiple_of(step * tile, tile), tile)
        value = jnp.dot(joint[...], up[...], preferred_element_type=jnp.float32)
        split_blocks(value, hidden)
        rounded = (value * jax.nn.sigmoid(value)).astype(jnp.bfloat16)
        split_blocks(rounded, active)
        held[:, place] = rounded

    @pl.when(step >= steps)
    def _():
        split_blocks(jnp.dot(held[...], down[...], preferred_element_type=jnp.float32), term)


def backward_kernel(blocks, steps, last, tile, *refs):
    cots, hidden, active, rows = (refs[k * blocks : (k + 1) * blocks] for k in range(4))
    down, up, column = refs[4 * blocks : 4 * blocks + 3]
    outs = refs[4 * blocks + 3 : -3]
    hidden_cot, term = (outs[k * blocks : (k + 1) * blocks] for k in range(2))
    total = outs[-1]
    joint, held, slope = refs[-3:]
    count = cots[0].shape[0]
    step = pl.program_id(0)

    @pl.when(step == 0)
    def _():
        join_blocks(cots, joint)
        slope[...] = jnp.zeros_like(slope)

    @pl.when(step < steps)
    def _():
        place = pl.ds(pl.multiple_of(step * tile, tile), tile)
        back_all = nt(joint[...], down[...])
        for i in range(blocks):
            back = back_all[i * count : (i + 1) * count]
            value = hidden[i][...]
            sig = jax.nn.sigmoid(value)
            rounded = (back * (sig * (1.0 + value * (1.0 - sig)))).astype(jnp.bfloat16)
            hidden_cot[i][...] = rounded
            held[i * count : (i + 1) * count, place] = rounded
            product = back * active[i][...].astype(jnp.float32)
            lanes = slope.shape[2]
            slope[i] += sum(product[:, k : k + lanes] for k in range(0, tile, lanes))

    @pl.when(step >= steps)
    def _():
        split_blocks(nt(held[...], up[...]), term)

    @pl.when(step == last)
    def _():
        add_up = jnp.zeros(total.shape, jnp.float32)
        for i in range(blocks):
            off = 1.0 - jax.nn.sigmoid(nt(rows[i][...], column[...])[:, :1])
            own = jnp.sum(slope[i], axis=1, keepdims=True) * off
            high = own.astype(jnp.bfloat16)
            rest = own - high.astype(jnp.float32)
            middle = rest.astype(jnp.bfloat16)
            least = rest - middle.astype(jnp.float32)
            lane = lax.broadcasted_iota(jnp.int32, slope.shape[1:], 1)
            split = jnp.zeros(slope.shape[1:], jnp.float32)
            for k, part in enumerate((high, middle, least)):
                split = jnp.where(lane == k, part.astype(jnp.float32), split)
            sums = tn(split.astype(jnp.bfloat16), rows[i][...])
            add_up += sums[0:1] + sums[1:2] + sums[2:3]
        total[...] = add_up


def tiles_for(rows, w_up):
    width, hidden = w_up.shape
    tile, wide = tile_of(hidden, 512), tile_of(width, 1280)
    return rows.shape[0], width, hidden, tile, wide, hidden // tile, width // wide


def whole(shape):
    return pl.BlockSpec(shape, lambda i: (0,) * len(shape), pipeline_mode=pl.Buffered(1))


def forward(rows, w_up, w_down):
    count, width, hidden, tile, wide, steps, wides = tiles_for(rows[0], w_up)
    n = len(rows)
    first, second = lambda i: jnp.minimum(i, steps - 1), lambda i: jnp.maximum(i - steps, 0)
    part = pl.BlockSpec((count, tile), lambda i: (0, first(i)))
    outs = call(
        functools.partial(forward_kernel, n, steps, tile),
        steps + wides,
        [whole((count, width))] * n
        + [
            pl.BlockSpec((width, tile), lambda i: (0, first(i))),
            pl.BlockSpec((hidden, wide), lambda i: (0, second(i))),
        ],
        [jax.ShapeDtypeStruct((count, hidden), jnp.float32)] * n
        + [jax.ShapeDtypeStruct((count, hidden), jnp.bfloat16)] * n
        + [jax.ShapeDtypeStruct((count, width), jnp.bfloat16)] * n,
        [part] * (2 * n) + [pl.BlockSpec((count, wide), lambda i: (0, second(i)))] * n,
        [
            pltpu.VMEM((n * count, width), jnp.bfloat16),
            pltpu.VMEM((n * count, hidden), jnp.bfloat16),
        ],
        mib=56,
    )(*rows, w_up, w_down)
    return list(outs[:n]), list(outs[n : 2 * n]), list(outs[2 * n :])


def backward(cots, hiddens, actives, rows, w_up, w_down, column):
    count, width, hidden, tile, wide, steps, wides = tiles_for(cots[0], w_up)
    n = len(cots)
    first, second = lambda i: jnp.minimum(i, steps - 1), lambda i: jnp.maximum(i - steps, 0)
    part = pl.BlockSpec((count, tile), lambda i: (0, first(i)))
    outs = call(
        functools.partial(backward_kernel, n, steps, steps + wides - 1, tile),
        steps + wides,
        [whole((count, width))] * n
        + [part] * (2 * n)
        + [whole((count, width))] * n
        + [
            pl.BlockSpec((tile, width), lambda i: (first(i), 0)),
            pl.BlockSpec((wide, hidden), lambda i: (second(i), 0)),
            whole(column.shape),
        ],
        [jax.ShapeDtypeStruct((count, hidden), jnp.bfloat16)] * n
        + [jax.ShapeDtypeStruct((count, width), jnp.bfloat16)] * n
        + [jax.ShapeDtypeStruct((1, width), jnp.float32)],
        [part] * n
        + [pl.BlockSpec((count, wide), lambda i: (0, second(i)))] * n
        + [pl.BlockSpec((1, width), lambda i: (0, 0))],
        [
            pltpu.VMEM((n * count, width), jnp.bfloat16),
            pltpu.VMEM((n * count, hidden), jnp.bfloat16),
            pltpu.VMEM((n, count, tile_of(tile, 128)), jnp.float32),
        ],
        mib=56,
    )(*cots, *hiddens, *actives, *rows, w_down, w_up, column)
    return list(outs[:n]), list(outs[n : 2 * n]), outs[-1]


def gradient_kernel(blocks, *refs):
    left, right, out = refs[:blocks], refs[blocks : 2 * blocks], refs[-1]
    total = sum(tn(a[...], b[...]) for a, b in zip(left, right))
    out[...] = total.astype(out.dtype)


def gradient(lefts, rights, want):
    count, height = lefts[0].shape
    width = rights[0].shape[1]
    tile = tile_of(height, want)
    return call(
        functools.partial(gradient_kernel, len(lefts)),
        height // tile,
        [pl.BlockSpec((count, tile), lambda i: (0, i))] * len(lefts)
        + [whole((count, width))] * len(rights),
        jax.ShapeDtypeStruct((height, width), jnp.bfloat16),
        pl.BlockSpec((tile, width), lambda i: (i, 0)),
        flops=2 * len(lefts) * count * height * width,
        moved=2 * (len(lefts) * count * (height + width) + height * width),
    )(*lefts, *rights)


def make(n_expert, n_tensor):
    top, low = n_tensor // 2, n_tensor // 2

    def cross(x, bit):
        return lax.ppermute(x, "tensor", [(i, i ^ bit) for i in range(n_tensor)])

    def gather_low(rows):
        held = [rows]
        bit = 1
        while bit < low:
            held = held + [cross(h, bit) for h in held]
            bit *= 2
        return held

    def sum_low_after(terms, earlier):
        while len(terms) > 1:
            bit = len(terms) // 2
            came = [cross(b, bit) for b in terms[bit:]]
            if bit == 1:
                came = [after(c, earlier) for c in came]
            terms = [added(a, c) for a, c in zip(terms[:bit], came)]
        return terms[0]

    def sum_low(terms):
        while len(terms) > 1:
            bit = len(terms) // 2
            terms = [added(a, cross(b, bit)) for a, b in zip(terms[:bit], terms[bit:])]
        return terms[0]

    def per_device(tokens, expert_ids, live_counts, router, up_weight, down_weight, out_grad):
        tok_rows, width = tokens.shape
        experts = router.shape[1]
        most = 3 * tok_rows // (2 * experts)
        slots = experts * most
        me = lax.axis_index("expert")
        ids = expert_ids[:, 0]
        live = lax.iota(jnp.int32, tok_rows) < live_counts[0]
        chosen = ids[:, None] == lax.iota(jnp.int32, experts)[None, :]
        chosen_int = chosen.astype(jnp.int32)
        rank = jnp.sum(jnp.cumsum(chosen_int, axis=0) * chosen_int, axis=1) - 1
        target = jnp.where(live, ids * most + rank, -1)
        placing = (lax.iota(jnp.int32, slots)[:, None] == target[None, :]).astype(jnp.bfloat16)
        w_up, w_down = up_weight[0], down_weight[0]

        def swap(x):
            return lax.all_to_all(x, "expert", split_axis=0, concat_axis=0, tiled=True)

        def exchange(x):
            return swap(x.reshape(experts, most, width)).reshape(slots, width)

        tok_near = exchange(dot(placing, tokens, jnp.bfloat16))
        logits = dot(tokens, router)
        gate = jax.nn.sigmoid(jnp.sum(logits * chosen.astype(jnp.float32), axis=1))
        out_cot = (gate[:, None] * out_grad.astype(jnp.float32)).astype(jnp.bfloat16)
        cot_near = exchange(after(dot(placing, out_cot, jnp.bfloat16), tok_near))
        tok_far = cross(tok_near, top)
        cot_far = cross(cot_near, top)

        rows = gather_low(after(tok_far, cot_near)) + gather_low(tok_near)
        hidden, active, term = forward(rows, w_up, w_down)
        out_far_sum, out_near = sum_low(term[:low]), sum_low(term[low:])
        cot_far = after(cot_far, *term)
        out_far = cross(after(out_far_sum, cot_far), top)

        column = lax.dynamic_slice_in_dim(router, me, 1, axis=1).T
        column = jnp.broadcast_to(column, (16, width))
        cots = gather_low(cot_far)
        hidden_cot, far_term, far_column = backward(
            [after(x, out_far_sum) for x in cots],
            hidden[:low],
            active[:low],
            rows[:low],
            w_up,
            w_down,
            column,
        )
        out_far = after(out_far, *far_term)
        out_sum = added(out_near, out_far)
        out_home = exchange(out_sum)
        back_far_sum = sum_low_after(far_term, out_far)
        back_far = cross(back_far_sum, top)

        near = [after(x, out_sum, back_far_sum) for x in gather_low(cot_near)]
        near_hidden_cot, near_term, near_column = backward(
            near, hidden[low:], active[low:], rows[low:], w_up, w_down, column
        )
        back_near = sum_low([after(x, back_far) for x in near_term])
        cots, hidden_cot = cots + near, hidden_cot + near_hidden_cot

        columns = far_column + near_column
        bit = 1
        while bit < n_tensor:
            columns = columns + cross(columns, bit)
            bit *= 2
        columns = after(columns, out_home)
        lanes = -(-width // (most * 128)) * 128
        high = columns.astype(jnp.bfloat16)
        rest = (columns - high.astype(jnp.float32)).astype(jnp.bfloat16)
        beside = jnp.concatenate(
            [
                jnp.pad(x, ((0, 0), (0, most * lanes - width))).reshape(1, most, lanes)
                for x in (high, rest)
            ],
            axis=2,
        )

        back_sum = added(back_near, after(back_far, out_home))

        up_grad = gradient([after(x, back_sum, columns) for x in rows], hidden_cot, 512)[None]
        down_grad = gradient([after(x, back_sum, columns) for x in active], cots, 256)[None]

        back_sum = back_sum.reshape(experts, most, width)
        beside = jnp.broadcast_to(beside, (experts, most, 2 * lanes))
        came = swap(jnp.concatenate([back_sum, beside], axis=2))
        back_home = came.reshape(slots, width + 2 * lanes)
        high, rest = (
            came[:, :, k : k + lanes].reshape(experts, most * lanes)[:, :width].astype(jnp.float32)
            for k in (width, width + lanes)
        )
        router_grad = (high + rest).T

        out_rows = dot(placing, after(out_home, back_sum), jnp.bfloat16, ((0,), (0,)))
        cot_rows = dot(placing, back_home, jnp.bfloat16, ((0,), (0,)))[:, :width]
        out_wide = out_rows.astype(jnp.float32)
        mixed = (gate[:, None] * out_wide).astype(jnp.bfloat16)
        own_slope = jnp.sum(out_grad.astype(jnp.float32) * out_wide, axis=1) * gate * (1.0 - gate)
        named = dot(chosen.astype(jnp.bfloat16), router, dims=((1,), (1,)))
        token_grad = (cot_rows.astype(jnp.float32) + own_slope[:, None] * named).astype(jnp.bfloat16)
        return (mixed, token_grad, up_grad, down_grad, router_grad)

    return per_device


def solution(mesh):
    in_specs = (
        P(("expert", "tensor"), None),
        P(("expert", "tensor"), None),
        P(("expert", "tensor")),
        P(),
        P("expert", None, "tensor"),
        P("expert", "tensor", None),
        P(("expert", "tensor"), None),
    )
    out_specs = (
        P(("expert", "tensor"), None),
        P(("expert", "tensor"), None),
        P("expert", None, "tensor"),
        P("expert", "tensor", None),
        P(),
    )
    return jax.shard_map(
        make(mesh.shape["expert"], mesh.shape["tensor"]),
        mesh=mesh,
        in_specs=in_specs,
        out_specs=out_specs,
        check_vma=False,
    )
```

```python
import functools

import jax
import jax.numpy as jnp
from jax import lax
from jax.experimental import pallas as pl
from jax.experimental.pallas import tpu as pltpu
from jax.sharding import PartitionSpec as P


def dot(a, b, out=jnp.float32, dims=((1,), (0,))):
    return lax.dot_general(a, b, (dims, ((), ())), preferred_element_type=jnp.float32).astype(out)


def joined(blocks):
    return jnp.concatenate(blocks, axis=0)


def after(x, *earlier):
    return lax.optimization_barrier((x,) + earlier)[0]


def added(*parts):
    return sum(part.astype(jnp.float32) for part in parts).astype(jnp.bfloat16)


def call(kernel, grid, in_specs, outs, out_specs, scratch=(), flops=1, moved=1, mib=20):
    return pl.pallas_call(
        kernel,
        grid=(grid,),
        in_specs=in_specs,
        out_specs=out_specs,
        out_shape=outs,
        scratch_shapes=scratch,
        compiler_params=pltpu.CompilerParams(vmem_limit_bytes=mib * 1024 * 1024),
        cost_estimate=pl.CostEstimate(flops=flops, bytes_accessed=moved, transcendentals=0),
    )


def tile_of(size, want):
    return want if size % want == 0 else size


def nt(a, b):
    return lax.dot_general(a, b, (((1,), (1,)), ((), ())), preferred_element_type=jnp.float32)


def tn(a, b):
    return lax.dot_general(a, b, (((0,), (0,)), ((), ())), preferred_element_type=jnp.float32)


def join_blocks(blocks, joint):
    count = blocks[0].shape[0]
    for i, block in enumerate(blocks):
        joint[i * count : (i + 1) * count] = block[...]


def split_blocks(value, blocks):
    count = blocks[0].shape[0]
    for i, block in enumerate(blocks):
        block[...] = value[i * count : (i + 1) * count].astype(block.dtype)


def forward_kernel(blocks, steps, tile, *refs):
    rows, (up, down) = refs[:blocks], refs[blocks : blocks + 2]
    outs = refs[blocks + 2 : -2]
    hidden, active, term = outs[:blocks], outs[blocks : 2 * blocks], outs[2 * blocks :]
    joint, held = refs[-2:]
    step = pl.program_id(0)

    @pl.when(step == 0)
    def _():
        join_blocks(rows, joint)

    @pl.when(step < steps)
    def _():
        place = pl.ds(pl.multiple_of(step * tile, tile), tile)
        value = jnp.dot(joint[...], up[...], preferred_element_type=jnp.float32)
        split_blocks(value, hidden)
        rounded = (value * jax.nn.sigmoid(value)).astype(jnp.bfloat16)
        split_blocks(rounded, active)
        held[:, place] = rounded

    @pl.when(step >= steps)
    def _():
        split_blocks(jnp.dot(held[...], down[...], preferred_element_type=jnp.float32), term)


def backward_kernel(blocks, steps, last, tile, *refs):
    cots, hidden, active, rows = (refs[k * blocks : (k + 1) * blocks] for k in range(4))
    down, up, column = refs[4 * blocks : 4 * blocks + 3]
    outs = refs[4 * blocks + 3 : -3]
    hidden_cot, term = (outs[k * blocks : (k + 1) * blocks] for k in range(2))
    total = outs[-1]
    joint, held, slope = refs[-3:]
    count = cots[0].shape[0]
    step = pl.program_id(0)

    @pl.when(step == 0)
    def _():
        join_blocks(cots, joint)
        slope[...] = jnp.zeros_like(slope)

    @pl.when(step < steps)
    def _():
        place = pl.ds(pl.multiple_of(step * tile, tile), tile)
        back_all = nt(joint[...], down[...])
        for i in range(blocks):
            back = back_all[i * count : (i + 1) * count]
            value = hidden[i][...]
            sig = jax.nn.sigmoid(value)
            rounded = (back * (sig * (1.0 + value * (1.0 - sig)))).astype(jnp.bfloat16)
            hidden_cot[i][...] = rounded
            held[i * count : (i + 1) * count, place] = rounded
            product = back * active[i][...].astype(jnp.float32)
            lanes = slope.shape[2]
            slope[i] += sum(product[:, k : k + lanes] for k in range(0, tile, lanes))

    @pl.when(step >= steps)
    def _():
        split_blocks(nt(held[...], up[...]), term)

    @pl.when(step == last)
    def _():
        add_up = jnp.zeros(total.shape, jnp.float32)
        for i in range(blocks):
            off = 1.0 - jax.nn.sigmoid(nt(rows[i][...], column[...])[:, :1])
            own = jnp.sum(slope[i], axis=1, keepdims=True) * off
            high = own.astype(jnp.bfloat16)
            rest = own - high.astype(jnp.float32)
            middle = rest.astype(jnp.bfloat16)
            least = rest - middle.astype(jnp.float32)
            lane = lax.broadcasted_iota(jnp.int32, slope.shape[1:], 1)
            split = jnp.zeros(slope.shape[1:], jnp.float32)
            for k, part in enumerate((high, middle, least)):
                split = jnp.where(lane == k, part.astype(jnp.float32), split)
            sums = tn(split.astype(jnp.bfloat16), rows[i][...])
            add_up += sums[0:1] + sums[1:2] + sums[2:3]
        total[...] = add_up


def tiles_for(rows, w_up):
    width, hidden = w_up.shape
    tile, wide = tile_of(hidden, 512), tile_of(width, 1280)
    return rows.shape[0], width, hidden, tile, wide, hidden // tile, width // wide


def whole(shape):
    return pl.BlockSpec(shape, lambda i: (0,) * len(shape), pipeline_mode=pl.Buffered(1))


def forward(rows, w_up, w_down):
    count, width, hidden, tile, wide, steps, wides = tiles_for(rows[0], w_up)
    n = len(rows)
    first, second = lambda i: jnp.minimum(i, steps - 1), lambda i: jnp.maximum(i - steps, 0)
    part = pl.BlockSpec((count, tile), lambda i: (0, first(i)))
    outs = call(
        functools.partial(forward_kernel, n, steps, tile),
        steps + wides,
        [whole((count, width))] * n
        + [
            pl.BlockSpec((width, tile), lambda i: (0, first(i))),
            pl.BlockSpec((hidden, wide), lambda i: (0, second(i))),
        ],
        [jax.ShapeDtypeStruct((count, hidden), jnp.float32)] * n
        + [jax.ShapeDtypeStruct((count, hidden), jnp.bfloat16)] * n
        + [jax.ShapeDtypeStruct((count, width), jnp.bfloat16)] * n,
        [part] * (2 * n) + [pl.BlockSpec((count, wide), lambda i: (0, second(i)))] * n,
        [
            pltpu.VMEM((n * count, width), jnp.bfloat16),
            pltpu.VMEM((n * count, hidden), jnp.bfloat16),
        ],
        mib=56,
    )(*rows, w_up, w_down)
    return list(outs[:n]), list(outs[n : 2 * n]), list(outs[2 * n :])


def backward(cots, hiddens, actives, rows, w_up, w_down, column):
    count, width, hidden, tile, wide, steps, wides = tiles_for(cots[0], w_up)
    n = len(cots)
    first, second = lambda i: jnp.minimum(i, steps - 1), lambda i: jnp.maximum(i - steps, 0)
    part = pl.BlockSpec((count, tile), lambda i: (0, first(i)))
    outs = call(
        functools.partial(backward_kernel, n, steps, steps + wides - 1, tile),
        steps + wides,
        [whole((count, width))] * n
        + [part] * (2 * n)
        + [whole((count, width))] * n
        + [
            pl.BlockSpec((tile, width), lambda i: (first(i), 0)),
            pl.BlockSpec((wide, hidden), lambda i: (second(i), 0)),
            whole(column.shape),
        ],
        [jax.ShapeDtypeStruct((count, hidden), jnp.bfloat16)] * n
        + [jax.ShapeDtypeStruct((count, width), jnp.bfloat16)] * n
        + [jax.ShapeDtypeStruct((1, width), jnp.float32)],
        [part] * n
        + [pl.BlockSpec((count, wide), lambda i: (0, second(i)))] * n
        + [pl.BlockSpec((1, width), lambda i: (0, 0))],
        [
            pltpu.VMEM((n * count, width), jnp.bfloat16),
            pltpu.VMEM((n * count, hidden), jnp.bfloat16),
            pltpu.VMEM((n, count, tile_of(tile, 128)), jnp.float32),
        ],
        mib=56,
    )(*cots, *hiddens, *actives, *rows, w_down, w_up, column)
    return list(outs[:n]), list(outs[n : 2 * n]), outs[-1]


def gradient_kernel(blocks, *refs):
    left, right, out = refs[:blocks], refs[blocks : 2 * blocks], refs[-1]
    total = sum(tn(a[...], b[...]) for a, b in zip(left, right))
    out[...] = total.astype(out.dtype)


def gradient(lefts, rights, want):
    count, height = lefts[0].shape
    width = rights[0].shape[1]
    tile = tile_of(height, want)
    return call(
        functools.partial(gradient_kernel, len(lefts)),
        height // tile,
        [pl.BlockSpec((count, tile), lambda i: (0, i))] * len(lefts)
        + [whole((count, width))] * len(rights),
        jax.ShapeDtypeStruct((height, width), jnp.bfloat16),
        pl.BlockSpec((tile, width), lambda i: (i, 0)),
        flops=2 * len(lefts) * count * height * width,
        moved=2 * (len(lefts) * count * (height + width) + height * width),
    )(*lefts, *rights)


def make(n_expert, n_tensor):
    top, low = n_tensor // 2, n_tensor // 2

    def cross(x, bit):
        return lax.ppermute(x, "tensor", [(i, i ^ bit) for i in range(n_tensor)])

    def gather_low(rows):
        held = [rows]
        bit = 1
        while bit < low:
            held = held + [cross(h, bit) for h in held]
            bit *= 2
        return held

    def sum_low_after(terms, earlier):
        count = terms[0].shape[0] // 2
        halves = []
        for k in (0, count):
            cut = [t[k : k + count] for t in terms]
            while len(cut) > 1:
                bit = len(cut) // 2
                came = [cross(b, bit) for b in cut[bit:]]
                if bit == 1:
                    came = [after(c, earlier) for c in came]
                cut = [added(a, c) for a, c in zip(cut[:bit], came)]
            halves.append(cut[0])
        return joined(halves)

    def last_two(terms):
        while len(terms) > 2:
            bit = len(terms) // 2
            terms = [added(a, cross(b, bit)) for a, b in zip(terms[:bit], terms[bit:])]
        return terms if len(terms) == 1 else [terms[0], cross(terms[1], 1)]

    def sum_low(terms):
        while len(terms) > 1:
            bit = len(terms) // 2
            terms = [added(a, cross(b, bit)) for a, b in zip(terms[:bit], terms[bit:])]
        return terms[0]

    def per_device(tokens, expert_ids, live_counts, router, up_weight, down_weight, out_grad):
        tok_rows, width = tokens.shape
        experts = router.shape[1]
        most = 3 * tok_rows // (2 * experts)
        slots = experts * most
        me = lax.axis_index("expert")
        ids = expert_ids[:, 0]
        live = lax.iota(jnp.int32, tok_rows) < live_counts[0]
        chosen = ids[:, None] == lax.iota(jnp.int32, experts)[None, :]
        chosen_int = chosen.astype(jnp.int32)
        rank = jnp.sum(jnp.cumsum(chosen_int, axis=0) * chosen_int, axis=1) - 1
        target = jnp.where(live, ids * most + rank, -1)
        placing = (lax.iota(jnp.int32, slots)[:, None] == target[None, :]).astype(jnp.bfloat16)
        w_up, w_down = up_weight[0], down_weight[0]

        def swap(x):
            return lax.all_to_all(x, "expert", split_axis=0, concat_axis=0, tiled=True)

        def exchange(x):
            return swap(x.reshape(experts, most, x.shape[1])).reshape(x.shape)

        tok_near = exchange(dot(placing, tokens, jnp.bfloat16))
        logits = dot(tokens, router)
        gate = jax.nn.sigmoid(jnp.sum(logits * chosen.astype(jnp.float32), axis=1))
        out_cot = (gate[:, None] * out_grad.astype(jnp.float32)).astype(jnp.bfloat16)
        cot_near = exchange(after(dot(placing, out_cot, jnp.bfloat16), tok_near))
        tok_far = cross(tok_near, top)
        cot_far = cross(cot_near, top)

        rows = gather_low(after(tok_far, cot_near)) + gather_low(tok_near)
        hidden, active, term = forward(rows, w_up, w_down)
        out_far_sum, out_near = sum_low(term[:low]), last_two(term[low:])
        cot_far = after(cot_far, *term)
        cut = width // 2
        out_far = after(out_far_sum, cot_far)
        out_far_left = cross(out_far[:, :cut], top)
        out_far_right = cross(out_far[:, cut:], top)

        column = lax.dynamic_slice_in_dim(router, me, 1, axis=1).T
        column = jnp.broadcast_to(column, (16, width))
        cots = gather_low(cot_far)
        hidden_cot, far_term, far_column = backward(
            [after(x, out_far_sum) for x in cots],
            hidden[:low],
            active[:low],
            rows[:low],
            w_up,
            w_down,
            column,
        )
        out_far_left = after(out_far_left, *far_term)
        out_home_left = exchange(added(*[x[:, :cut] for x in out_near], out_far_left))
        back_far_sum = sum_low_after(far_term, out_far_left)
        back_far = cross(back_far_sum, top)
        out_far_right = after(out_far_right, back_far_sum)
        out_sum = added(*[x[:, cut:] for x in out_near], out_far_right)
        out_home_right = exchange(out_sum)

        near = [after(x, out_sum, back_far_sum) for x in gather_low(cot_near)]
        near_hidden_cot, near_term, near_column = backward(
            near, hidden[low:], active[low:], rows[low:], w_up, w_down, column
        )
        back_near = sum_low([after(x, back_far) for x in near_term])
        cots, hidden_cot = cots + near, hidden_cot + near_hidden_cot

        columns = far_column + near_column
        bit = 1
        while bit < n_tensor:
            columns = columns + cross(columns, bit)
            bit *= 2
        columns = after(columns, out_home_left, out_home_right)
        lanes = -(-width // (most * 128)) * 128
        high = columns.astype(jnp.bfloat16)
        rest = (columns - high.astype(jnp.float32)).astype(jnp.bfloat16)
        beside = jnp.concatenate(
            [
                jnp.pad(x, ((0, 0), (0, most * lanes - width))).reshape(1, most, lanes)
                for x in (high, rest)
            ],
            axis=2,
        )

        back_sum = added(back_near, after(back_far, out_home_left, out_home_right))

        up_grad = gradient([after(x, back_sum, columns) for x in rows], hidden_cot, 512)[None]
        down_grad = gradient([after(x, back_sum, columns) for x in active], cots, 256)[None]

        back_sum = back_sum.reshape(experts, most, width)
        beside = jnp.broadcast_to(beside, (experts, most, 2 * lanes))
        came = swap(jnp.concatenate([back_sum, beside], axis=2))
        back_home = came.reshape(slots, width + 2 * lanes)
        high, rest = (
            came[:, :, k : k + lanes].reshape(experts, most * lanes)[:, :width].astype(jnp.float32)
            for k in (width, width + lanes)
        )
        router_grad = (high + rest).T

        out_home = jnp.concatenate([after(out_home_left, back_sum), out_home_right], axis=1)
        out_rows = dot(placing, out_home, jnp.bfloat16, ((0,), (0,)))
        cot_rows = dot(placing, back_home, jnp.bfloat16, ((0,), (0,)))[:, :width]
        out_wide = out_rows.astype(jnp.float32)
        mixed = (gate[:, None] * out_wide).astype(jnp.bfloat16)
        own_slope = jnp.sum(out_grad.astype(jnp.float32) * out_wide, axis=1) * gate * (1.0 - gate)
        named = dot(chosen.astype(jnp.bfloat16), router, dims=((1,), (1,)))
        token_grad = (cot_rows.astype(jnp.float32) + own_slope[:, None] * named).astype(jnp.bfloat16)
        return (mixed, token_grad, up_grad, down_grad, router_grad)

    return per_device


def solution(mesh):
    in_specs = (
        P(("expert", "tensor"), None),
        P(("expert", "tensor"), None),
        P(("expert", "tensor")),
        P(),
        P("expert", None, "tensor"),
        P("expert", "tensor", None),
        P(("expert", "tensor"), None),
    )
    out_specs = (
        P(("expert", "tensor"), None),
        P(("expert", "tensor"), None),
        P("expert", None, "tensor"),
        P("expert", "tensor", None),
        P(),
    )
    return jax.shard_map(
        make(mesh.shape["expert"], mesh.shape["tensor"]),
        mesh=mesh,
        in_specs=in_specs,
        out_specs=out_specs,
        check_vma=False,
    )
```

```python
import functools

import jax
import jax.numpy as jnp
from jax import lax
from jax.experimental import pallas as pl
from jax.experimental.pallas import tpu as pltpu
from jax.sharding import PartitionSpec as P


def dot(a, b, out=jnp.float32, dims=((1,), (0,))):
    return lax.dot_general(a, b, (dims, ((), ())), preferred_element_type=jnp.float32).astype(out)


def joined(blocks):
    return jnp.concatenate(blocks, axis=0)


def after(x, *earlier):
    return lax.optimization_barrier((x,) + earlier)[0]


def added(*parts):
    return sum(part.astype(jnp.float32) for part in parts).astype(jnp.bfloat16)


def call(kernel, grid, in_specs, outs, out_specs, scratch=(), flops=1, moved=1, mib=20):
    return pl.pallas_call(
        kernel,
        grid=(grid,),
        in_specs=in_specs,
        out_specs=out_specs,
        out_shape=outs,
        scratch_shapes=scratch,
        compiler_params=pltpu.CompilerParams(vmem_limit_bytes=mib * 1024 * 1024),
        cost_estimate=pl.CostEstimate(flops=flops, bytes_accessed=moved, transcendentals=0),
    )


def tile_of(size, want):
    return want if size % want == 0 else size


def nt(a, b):
    return lax.dot_general(a, b, (((1,), (1,)), ((), ())), preferred_element_type=jnp.float32)


def tn(a, b):
    return lax.dot_general(a, b, (((0,), (0,)), ((), ())), preferred_element_type=jnp.float32)


def join_blocks(blocks, joint):
    count = blocks[0].shape[0]
    for i, block in enumerate(blocks):
        joint[i * count : (i + 1) * count] = block[...]


def split_blocks(value, blocks):
    count = blocks[0].shape[0]
    for i, block in enumerate(blocks):
        block[...] = value[i * count : (i + 1) * count].astype(block.dtype)


def forward_kernel(blocks, steps, tile, *refs):
    rows, (up, down) = refs[:blocks], refs[blocks : blocks + 2]
    outs = refs[blocks + 2 : -2]
    hidden, active, term = outs[:blocks], outs[blocks : 2 * blocks], outs[2 * blocks :]
    joint, held = refs[-2:]
    step = pl.program_id(0)

    @pl.when(step == 0)
    def _():
        join_blocks(rows, joint)

    @pl.when(step < steps)
    def _():
        place = pl.ds(pl.multiple_of(step * tile, tile), tile)
        value = jnp.dot(joint[...], up[...], preferred_element_type=jnp.float32)
        split_blocks(value, hidden)
        rounded = (value * jax.nn.sigmoid(value)).astype(jnp.bfloat16)
        split_blocks(rounded, active)
        held[:, place] = rounded

    @pl.when(step >= steps)
    def _():
        split_blocks(jnp.dot(held[...], down[...], preferred_element_type=jnp.float32), term)


def backward_kernel(blocks, steps, last, tile, *refs):
    cots, hidden, active, rows = (refs[k * blocks : (k + 1) * blocks] for k in range(4))
    down, up, column = refs[4 * blocks : 4 * blocks + 3]
    outs = refs[4 * blocks + 3 : -3]
    hidden_cot, term = (outs[k * blocks : (k + 1) * blocks] for k in range(2))
    total = outs[-1]
    joint, held, slope = refs[-3:]
    count = cots[0].shape[0]
    step = pl.program_id(0)

    @pl.when(step == 0)
    def _():
        join_blocks(cots, joint)
        slope[...] = jnp.zeros_like(slope)

    @pl.when(step < steps)
    def _():
        place = pl.ds(pl.multiple_of(step * tile, tile), tile)
        back_all = nt(joint[...], down[...])
        for i in range(blocks):
            back = back_all[i * count : (i + 1) * count]
            value = hidden[i][...]
            sig = jax.nn.sigmoid(value)
            rounded = (back * (sig * (1.0 + value * (1.0 - sig)))).astype(jnp.bfloat16)
            hidden_cot[i][...] = rounded
            held[i * count : (i + 1) * count, place] = rounded
            product = back * active[i][...].astype(jnp.float32)
            lanes = slope.shape[2]
            slope[i] += sum(product[:, k : k + lanes] for k in range(0, tile, lanes))

    @pl.when(step >= steps)
    def _():
        split_blocks(nt(held[...], up[...]), term)

    @pl.when(step == last)
    def _():
        add_up = jnp.zeros(total.shape, jnp.float32)
        for i in range(blocks):
            off = 1.0 - jax.nn.sigmoid(nt(rows[i][...], column[...])[:, :1])
            own = jnp.sum(slope[i], axis=1, keepdims=True) * off
            high = own.astype(jnp.bfloat16)
            rest = own - high.astype(jnp.float32)
            middle = rest.astype(jnp.bfloat16)
            least = rest - middle.astype(jnp.float32)
            lane = lax.broadcasted_iota(jnp.int32, slope.shape[1:], 1)
            split = jnp.zeros(slope.shape[1:], jnp.float32)
            for k, part in enumerate((high, middle, least)):
                split = jnp.where(lane == k, part.astype(jnp.float32), split)
            sums = tn(split.astype(jnp.bfloat16), rows[i][...])
            add_up += sums[0:1] + sums[1:2] + sums[2:3]
        total[...] = add_up


def tiles_for(rows, w_up):
    width, hidden = w_up.shape
    tile, wide = tile_of(hidden, 512), tile_of(width, 1280)
    return rows.shape[0], width, hidden, tile, wide, hidden // tile, width // wide


def whole(shape):
    return pl.BlockSpec(shape, lambda i: (0,) * len(shape), pipeline_mode=pl.Buffered(1))


def forward(rows, w_up, w_down):
    count, width, hidden, tile, wide, steps, wides = tiles_for(rows[0], w_up)
    n = len(rows)
    first, second = lambda i: jnp.minimum(i, steps - 1), lambda i: jnp.maximum(i - steps, 0)
    part = pl.BlockSpec((count, tile), lambda i: (0, first(i)))
    outs = call(
        functools.partial(forward_kernel, n, steps, tile),
        steps + wides,
        [whole((count, width))] * n
        + [
            pl.BlockSpec((width, tile), lambda i: (0, first(i))),
            pl.BlockSpec((hidden, wide), lambda i: (0, second(i))),
        ],
        [jax.ShapeDtypeStruct((count, hidden), jnp.float32)] * n
        + [jax.ShapeDtypeStruct((count, hidden), jnp.bfloat16)] * n
        + [jax.ShapeDtypeStruct((count, width), jnp.bfloat16)] * n,
        [part] * (2 * n) + [pl.BlockSpec((count, wide), lambda i: (0, second(i)))] * n,
        [
            pltpu.VMEM((n * count, width), jnp.bfloat16),
            pltpu.VMEM((n * count, hidden), jnp.bfloat16),
        ],
        mib=56,
    )(*rows, w_up, w_down)
    return list(outs[:n]), list(outs[n : 2 * n]), list(outs[2 * n :])


def backward(cots, hiddens, actives, rows, w_up, w_down, column):
    count, width, hidden, tile, wide, steps, wides = tiles_for(cots[0], w_up)
    n = len(cots)
    first, second = lambda i: jnp.minimum(i, steps - 1), lambda i: jnp.maximum(i - steps, 0)
    part = pl.BlockSpec((count, tile), lambda i: (0, first(i)))
    outs = call(
        functools.partial(backward_kernel, n, steps, steps + wides - 1, tile),
        steps + wides,
        [whole((count, width))] * n
        + [part] * (2 * n)
        + [whole((count, width))] * n
        + [
            pl.BlockSpec((tile, width), lambda i: (first(i), 0)),
            pl.BlockSpec((wide, hidden), lambda i: (second(i), 0)),
            whole(column.shape),
        ],
        [jax.ShapeDtypeStruct((count, hidden), jnp.bfloat16)] * n
        + [jax.ShapeDtypeStruct((count, width), jnp.bfloat16)] * n
        + [jax.ShapeDtypeStruct((1, width), jnp.float32)],
        [part] * n
        + [pl.BlockSpec((count, wide), lambda i: (0, second(i)))] * n
        + [pl.BlockSpec((1, width), lambda i: (0, 0))],
        [
            pltpu.VMEM((n * count, width), jnp.bfloat16),
            pltpu.VMEM((n * count, hidden), jnp.bfloat16),
            pltpu.VMEM((n, count, tile_of(tile, 128)), jnp.float32),
        ],
        mib=56,
    )(*cots, *hiddens, *actives, *rows, w_down, w_up, column)
    return list(outs[:n]), list(outs[n : 2 * n]), outs[-1]


def gradient_kernel(blocks, *refs):
    left, right, out = refs[:blocks], refs[blocks : 2 * blocks], refs[-1]
    total = sum(tn(a[...], b[...]) for a, b in zip(left, right))
    out[...] = total.astype(out.dtype)


def gradient(lefts, rights, want):
    count, height = lefts[0].shape
    width = rights[0].shape[1]
    tile = tile_of(height, want)
    return call(
        functools.partial(gradient_kernel, len(lefts)),
        height // tile,
        [pl.BlockSpec((count, tile), lambda i: (0, i))] * len(lefts)
        + [whole((count, width))] * len(rights),
        jax.ShapeDtypeStruct((height, width), jnp.bfloat16),
        pl.BlockSpec((tile, width), lambda i: (i, 0)),
        flops=2 * len(lefts) * count * height * width,
        moved=2 * (len(lefts) * count * (height + width) + height * width),
    )(*lefts, *rights)


def make(n_expert, n_tensor):
    top, low = n_tensor // 2, n_tensor // 2

    def cross(x, bit):
        return lax.ppermute(x, "tensor", [(i, i ^ bit) for i in range(n_tensor)])

    def gather_low(rows):
        held = [rows]
        bit = 1
        while bit < low:
            held = held + [cross(h, bit) for h in held]
            bit *= 2
        return held

    def sum_low_after(terms, earlier):
        count = terms[0].shape[0] // 2
        halves = []
        for k in (0, count):
            cut = [t[k : k + count] for t in terms]
            while len(cut) > 1:
                bit = len(cut) // 2
                came = [cross(b, bit) for b in cut[bit:]]
                if bit == 1:
                    came = [after(c, earlier) for c in came]
                cut = [added(a, c) for a, c in zip(cut[:bit], came)]
            halves.append(cut[0])
        return joined(halves)

    def last_two(terms):
        while len(terms) > 2:
            bit = len(terms) // 2
            terms = [added(a, cross(b, bit)) for a, b in zip(terms[:bit], terms[bit:])]
        return terms if len(terms) == 1 else [terms[0], cross(terms[1], 1)]

    def sum_low(terms):
        while len(terms) > 1:
            bit = len(terms) // 2
            terms = [added(a, cross(b, bit)) for a, b in zip(terms[:bit], terms[bit:])]
        return terms[0]

    def per_device(tokens, expert_ids, live_counts, router, up_weight, down_weight, out_grad):
        tok_rows, width = tokens.shape
        experts = router.shape[1]
        most = 3 * tok_rows // (2 * experts)
        slots = experts * most
        me = lax.axis_index("expert")
        ids = expert_ids[:, 0]
        live = lax.iota(jnp.int32, tok_rows) < live_counts[0]
        chosen = ids[:, None] == lax.iota(jnp.int32, experts)[None, :]
        chosen_int = chosen.astype(jnp.int32)
        rank = jnp.sum(jnp.cumsum(chosen_int, axis=0) * chosen_int, axis=1) - 1
        target = jnp.where(live, ids * most + rank, -1)
        placing = (lax.iota(jnp.int32, slots)[:, None] == target[None, :]).astype(jnp.bfloat16)
        w_up, w_down = up_weight[0], down_weight[0]

        def swap(x):
            return lax.all_to_all(x, "expert", split_axis=0, concat_axis=0, tiled=True)

        def exchange(x):
            return swap(x.reshape(experts, most, x.shape[1])).reshape(x.shape)

        tok_near = exchange(dot(placing, tokens, jnp.bfloat16))
        logits = dot(tokens, router)
        gate = jax.nn.sigmoid(jnp.sum(logits * chosen.astype(jnp.float32), axis=1))
        out_cot = (gate[:, None] * out_grad.astype(jnp.float32)).astype(jnp.bfloat16)
        cot_near = exchange(after(dot(placing, out_cot, jnp.bfloat16), tok_near))
        tok_far = cross(tok_near, top)
        cot_far = cross(cot_near, top)

        rows = gather_low(after(tok_far, cot_near)) + gather_low(tok_near)
        hidden, active, term = forward(rows, w_up, w_down)
        out_far_sum, out_near = sum_low(term[:low]), last_two(term[low:])
        cot_far = after(cot_far, *term)
        cut = width // 2
        out_far = after(out_far_sum, cot_far)
        out_far_left = cross(out_far[:, :cut], top)
        out_far_right = cross(out_far[:, cut:], top)

        column = lax.dynamic_slice_in_dim(router, me, 1, axis=1).T
        column = jnp.broadcast_to(column, (16, width))
        cots = gather_low(cot_far)
        hidden_cot, far_term, far_column = backward(
            [after(x, out_far_sum) for x in cots],
            hidden[:low],
            active[:low],
            rows[:low],
            w_up,
            w_down,
            column,
        )
        out_far_left = after(out_far_left, *far_term)
        out_left = added(*[x[:, :cut] for x in out_near], out_far_left)
        out_home_left = exchange(out_left)
        back_far_sum = sum_low_after(far_term, out_far_left)
        back_far = cross(back_far_sum, top)
        out_far_right = after(out_far_right, back_far_sum, out_home_left)
        out_sum = added(*[x[:, cut:] for x in out_near], out_far_right)
        out_home_right = exchange(out_sum)

        near = [after(x, out_left, back_far_sum) for x in gather_low(cot_near)]
        near_hidden_cot, near_term, near_column = backward(
            near, hidden[low:], active[low:], rows[low:], w_up, w_down, column
        )
        back_near = sum_low([after(x, back_far) for x in near_term])
        cots, hidden_cot = cots + near, hidden_cot + near_hidden_cot

        columns = far_column + near_column
        bit = 1
        while bit < n_tensor:
            columns = columns + cross(columns, bit)
            bit *= 2
        columns = after(columns, out_home_left, out_home_right)
        lanes = -(-width // (most * 128)) * 128
        high = columns.astype(jnp.bfloat16)
        rest = (columns - high.astype(jnp.float32)).astype(jnp.bfloat16)
        beside = jnp.concatenate(
            [
                jnp.pad(x, ((0, 0), (0, most * lanes - width))).reshape(1, most, lanes)
                for x in (high, rest)
            ],
            axis=2,
        )

        back_sum = added(back_near, after(back_far, out_home_left, out_home_right))

        up_grad = gradient([after(x, back_sum, columns) for x in rows], hidden_cot, 512)[None]
        down_grad = gradient([after(x, back_sum, columns) for x in active], cots, 256)[None]

        back_sum = back_sum.reshape(experts, most, width)
        beside = jnp.broadcast_to(beside, (experts, most, 2 * lanes))
        came = swap(jnp.concatenate([back_sum, beside], axis=2))
        back_home = came.reshape(slots, width + 2 * lanes)
        high, rest = (
            came[:, :, k : k + lanes].reshape(experts, most * lanes)[:, :width].astype(jnp.float32)
            for k in (width, width + lanes)
        )
        router_grad = (high + rest).T

        out_home = jnp.concatenate([after(out_home_left, back_sum), out_home_right], axis=1)
        out_rows = dot(placing, out_home, jnp.bfloat16, ((0,), (0,)))
        cot_rows = dot(placing, back_home, jnp.bfloat16, ((0,), (0,)))[:, :width]
        out_wide = out_rows.astype(jnp.float32)
        mixed = (gate[:, None] * out_wide).astype(jnp.bfloat16)
        own_slope = jnp.sum(out_grad.astype(jnp.float32) * out_wide, axis=1) * gate * (1.0 - gate)
        named = dot(chosen.astype(jnp.bfloat16), router, dims=((1,), (1,)))
        token_grad = (cot_rows.astype(jnp.float32) + own_slope[:, None] * named).astype(jnp.bfloat16)
        return (mixed, token_grad, up_grad, down_grad, router_grad)

    return per_device


def solution(mesh):
    in_specs = (
        P(("expert", "tensor"), None),
        P(("expert", "tensor"), None),
        P(("expert", "tensor")),
        P(),
        P("expert", None, "tensor"),
        P("expert", "tensor", None),
        P(("expert", "tensor"), None),
    )
    out_specs = (
        P(("expert", "tensor"), None),
        P(("expert", "tensor"), None),
        P("expert", None, "tensor"),
        P("expert", "tensor", None),
        P(),
    )
    return jax.shard_map(
        make(mesh.shape["expert"], mesh.shape["tensor"]),
        mesh=mesh,
        in_specs=in_specs,
        out_specs=out_specs,
        check_vma=False,
    )
```

```python
import functools

import jax
import jax.numpy as jnp
from jax import lax
from jax.experimental import pallas as pl
from jax.experimental.pallas import tpu as pltpu
from jax.sharding import PartitionSpec as P


def dot(a, b, out=jnp.float32, dims=((1,), (0,))):
    return lax.dot_general(a, b, (dims, ((), ())), preferred_element_type=jnp.float32).astype(out)


def joined(blocks):
    return jnp.concatenate(blocks, axis=0)


def after(x, *earlier):
    return lax.optimization_barrier((x,) + earlier)[0]


def added(*parts):
    return sum(part.astype(jnp.float32) for part in parts).astype(jnp.bfloat16)


def call(kernel, grid, in_specs, outs, out_specs, scratch=(), flops=1, moved=1, mib=20):
    return pl.pallas_call(
        kernel,
        grid=(grid,),
        in_specs=in_specs,
        out_specs=out_specs,
        out_shape=outs,
        scratch_shapes=scratch,
        compiler_params=pltpu.CompilerParams(vmem_limit_bytes=mib * 1024 * 1024),
        cost_estimate=pl.CostEstimate(flops=flops, bytes_accessed=moved, transcendentals=0),
    )


def tile_of(size, want):
    return want if size % want == 0 else size


def nt(a, b):
    return lax.dot_general(a, b, (((1,), (1,)), ((), ())), preferred_element_type=jnp.float32)


def tn(a, b):
    return lax.dot_general(a, b, (((0,), (0,)), ((), ())), preferred_element_type=jnp.float32)


def join_blocks(blocks, joint):
    count = blocks[0].shape[0]
    for i, block in enumerate(blocks):
        joint[i * count : (i + 1) * count] = block[...]


def split_blocks(value, blocks):
    count = blocks[0].shape[0]
    for i, block in enumerate(blocks):
        block[...] = value[i * count : (i + 1) * count].astype(block.dtype)


def forward_kernel(blocks, steps, tile, *refs):
    rows, (up, down) = refs[:blocks], refs[blocks : blocks + 2]
    outs = refs[blocks + 2 : -2]
    hidden, active, term = outs[:blocks], outs[blocks : 2 * blocks], outs[2 * blocks :]
    joint, held = refs[-2:]
    step = pl.program_id(0)

    @pl.when(step == 0)
    def _():
        join_blocks(rows, joint)

    @pl.when(step < steps)
    def _():
        place = pl.ds(pl.multiple_of(step * tile, tile), tile)
        value = jnp.dot(joint[...], up[...], preferred_element_type=jnp.float32)
        split_blocks(value, hidden)
        rounded = (value * jax.nn.sigmoid(value)).astype(jnp.bfloat16)
        split_blocks(rounded, active)
        held[:, place] = rounded

    @pl.when(step >= steps)
    def _():
        split_blocks(jnp.dot(held[...], down[...], preferred_element_type=jnp.float32), term)


def backward_kernel(blocks, steps, last, tile, *refs):
    cots, hidden, active, rows = (refs[k * blocks : (k + 1) * blocks] for k in range(4))
    down, up, column = refs[4 * blocks : 4 * blocks + 3]
    outs = refs[4 * blocks + 3 : -3]
    hidden_cot, term = (outs[k * blocks : (k + 1) * blocks] for k in range(2))
    total = outs[-1]
    joint, held, slope = refs[-3:]
    count = cots[0].shape[0]
    step = pl.program_id(0)

    @pl.when(step == 0)
    def _():
        join_blocks(cots, joint)
        slope[...] = jnp.zeros_like(slope)

    @pl.when(step < steps)
    def _():
        place = pl.ds(pl.multiple_of(step * tile, tile), tile)
        back_all = nt(joint[...], down[...])
        for i in range(blocks):
            back = back_all[i * count : (i + 1) * count]
            value = hidden[i][...]
            sig = jax.nn.sigmoid(value)
            rounded = (back * (sig * (1.0 + value * (1.0 - sig)))).astype(jnp.bfloat16)
            hidden_cot[i][...] = rounded
            held[i * count : (i + 1) * count, place] = rounded
            product = back * active[i][...].astype(jnp.float32)
            lanes = slope.shape[2]
            slope[i] += sum(product[:, k : k + lanes] for k in range(0, tile, lanes))

    @pl.when(step >= steps)
    def _():
        split_blocks(nt(held[...], up[...]), term)

    @pl.when(step == last)
    def _():
        add_up = jnp.zeros(total.shape, jnp.float32)
        for i in range(blocks):
            off = 1.0 - jax.nn.sigmoid(nt(rows[i][...], column[...])[:, :1])
            own = jnp.sum(slope[i], axis=1, keepdims=True) * off
            high = own.astype(jnp.bfloat16)
            rest = own - high.astype(jnp.float32)
            middle = rest.astype(jnp.bfloat16)
            least = rest - middle.astype(jnp.float32)
            lane = lax.broadcasted_iota(jnp.int32, slope.shape[1:], 1)
            split = jnp.zeros(slope.shape[1:], jnp.float32)
            for k, part in enumerate((high, middle, least)):
                split = jnp.where(lane == k, part.astype(jnp.float32), split)
            sums = tn(split.astype(jnp.bfloat16), rows[i][...])
            add_up += sums[0:1] + sums[1:2] + sums[2:3]
        total[...] = add_up


def tiles_for(rows, w_up):
    width, hidden = w_up.shape
    tile, wide = tile_of(hidden, 512), tile_of(width, 1280)
    return rows.shape[0], width, hidden, tile, wide, hidden // tile, width // wide


def whole(shape):
    return pl.BlockSpec(shape, lambda i: (0,) * len(shape), pipeline_mode=pl.Buffered(1))


def forward(rows, w_up, w_down):
    count, width, hidden, tile, wide, steps, wides = tiles_for(rows[0], w_up)
    n = len(rows)
    first, second = lambda i: jnp.minimum(i, steps - 1), lambda i: jnp.maximum(i - steps, 0)
    part = pl.BlockSpec((count, tile), lambda i: (0, first(i)))
    outs = call(
        functools.partial(forward_kernel, n, steps, tile),
        steps + wides,
        [whole((count, width))] * n
        + [
            pl.BlockSpec((width, tile), lambda i: (0, first(i))),
            pl.BlockSpec((hidden, wide), lambda i: (0, second(i))),
        ],
        [jax.ShapeDtypeStruct((count, hidden), jnp.float32)] * n
        + [jax.ShapeDtypeStruct((count, hidden), jnp.bfloat16)] * n
        + [jax.ShapeDtypeStruct((count, width), jnp.bfloat16)] * n,
        [part] * (2 * n) + [pl.BlockSpec((count, wide), lambda i: (0, second(i)))] * n,
        [
            pltpu.VMEM((n * count, width), jnp.bfloat16),
            pltpu.VMEM((n * count, hidden), jnp.bfloat16),
        ],
        mib=56,
    )(*rows, w_up, w_down)
    return list(outs[:n]), list(outs[n : 2 * n]), list(outs[2 * n :])


def backward(cots, hiddens, actives, rows, w_up, w_down, column):
    count, width, hidden, tile, wide, steps, wides = tiles_for(cots[0], w_up)
    n = len(cots)
    first, second = lambda i: jnp.minimum(i, steps - 1), lambda i: jnp.maximum(i - steps, 0)
    part = pl.BlockSpec((count, tile), lambda i: (0, first(i)))
    outs = call(
        functools.partial(backward_kernel, n, steps, steps + wides - 1, tile),
        steps + wides,
        [whole((count, width))] * n
        + [part] * (2 * n)
        + [whole((count, width))] * n
        + [
            pl.BlockSpec((tile, width), lambda i: (first(i), 0)),
            pl.BlockSpec((wide, hidden), lambda i: (second(i), 0)),
            whole(column.shape),
        ],
        [jax.ShapeDtypeStruct((count, hidden), jnp.bfloat16)] * n
        + [jax.ShapeDtypeStruct((count, width), jnp.bfloat16)] * n
        + [jax.ShapeDtypeStruct((1, width), jnp.float32)],
        [part] * n
        + [pl.BlockSpec((count, wide), lambda i: (0, second(i)))] * n
        + [pl.BlockSpec((1, width), lambda i: (0, 0))],
        [
            pltpu.VMEM((n * count, width), jnp.bfloat16),
            pltpu.VMEM((n * count, hidden), jnp.bfloat16),
            pltpu.VMEM((n, count, tile_of(tile, 128)), jnp.float32),
        ],
        mib=56,
    )(*cots, *hiddens, *actives, *rows, w_down, w_up, column)
    return list(outs[:n]), list(outs[n : 2 * n]), outs[-1]


def gradient_kernel(blocks, *refs):
    left, right, out = refs[:blocks], refs[blocks : 2 * blocks], refs[-1]
    total = sum(tn(a[...], b[...]) for a, b in zip(left, right))
    out[...] = total.astype(out.dtype)


def gradient(lefts, rights, want):
    count, height = lefts[0].shape
    width = rights[0].shape[1]
    tile = tile_of(height, want)
    return call(
        functools.partial(gradient_kernel, len(lefts)),
        height // tile,
        [pl.BlockSpec((count, tile), lambda i: (0, i))] * len(lefts)
        + [whole((count, width))] * len(rights),
        jax.ShapeDtypeStruct((height, width), jnp.bfloat16),
        pl.BlockSpec((tile, width), lambda i: (i, 0)),
        flops=2 * len(lefts) * count * height * width,
        moved=2 * (len(lefts) * count * (height + width) + height * width),
    )(*lefts, *rights)


def make(n_expert, n_tensor):
    top, low = n_tensor // 2, n_tensor // 2

    def cross(x, bit):
        return lax.ppermute(x, "tensor", [(i, i ^ bit) for i in range(n_tensor)])

    def gather_low(rows):
        held = [rows]
        bit = 1
        while bit < low:
            held = held + [cross(h, bit) for h in held]
            bit *= 2
        return held

    def sum_low_after(terms, earlier):
        count = terms[0].shape[0] // 2
        halves = []
        for k in (0, count):
            cut = [t[k : k + count] for t in terms]
            while len(cut) > 1:
                bit = len(cut) // 2
                came = [cross(b, bit) for b in cut[bit:]]
                if bit == 1:
                    came = [after(c, earlier) for c in came]
                cut = [added(a, c) for a, c in zip(cut[:bit], came)]
            halves.append(cut[0])
        return joined(halves)

    def last_two(terms):
        while len(terms) > 2:
            bit = len(terms) // 2
            terms = [added(a, cross(b, bit)) for a, b in zip(terms[:bit], terms[bit:])]
        return terms if len(terms) == 1 else [terms[0], cross(terms[1], 1)]

    def sum_low(terms):
        while len(terms) > 1:
            bit = len(terms) // 2
            terms = [added(a, cross(b, bit)) for a, b in zip(terms[:bit], terms[bit:])]
        return terms[0]

    def per_device(tokens, expert_ids, live_counts, router, up_weight, down_weight, out_grad):
        tok_rows, width = tokens.shape
        experts = router.shape[1]
        most = 3 * tok_rows // (2 * experts)
        slots = experts * most
        me = lax.axis_index("expert")
        ids = expert_ids[:, 0]
        live = lax.iota(jnp.int32, tok_rows) < live_counts[0]
        chosen = ids[:, None] == lax.iota(jnp.int32, experts)[None, :]
        chosen_int = chosen.astype(jnp.int32)
        rank = jnp.sum(jnp.cumsum(chosen_int, axis=0) * chosen_int, axis=1) - 1
        target = jnp.where(live, ids * most + rank, -1)
        placing = (lax.iota(jnp.int32, slots)[:, None] == target[None, :]).astype(jnp.bfloat16)
        w_up, w_down = up_weight[0], down_weight[0]

        def swap(x):
            return lax.all_to_all(x, "expert", split_axis=0, concat_axis=0, tiled=True)

        def exchange(x):
            return swap(x.reshape(experts, most, x.shape[1])).reshape(x.shape)

        tok_near = exchange(dot(placing, tokens, jnp.bfloat16))
        logits = dot(tokens, router)
        gate = jax.nn.sigmoid(jnp.sum(logits * chosen.astype(jnp.float32), axis=1))
        out_cot = (gate[:, None] * out_grad.astype(jnp.float32)).astype(jnp.bfloat16)
        cot_near = exchange(after(dot(placing, out_cot, jnp.bfloat16), tok_near))
        tok_far = cross(tok_near, top)
        cot_far = cross(cot_near, top)

        rows = gather_low(after(tok_far, cot_near)) + gather_low(tok_near)
        hidden, active, term = forward(rows, w_up, w_down)
        out_far_sum, out_near = sum_low(term[:low]), last_two(term[low:])
        cot_far = after(cot_far, *term)
        cut = width // 2
        out_far = after(out_far_sum, cot_far)
        out_far_left = cross(out_far[:, :cut], top)
        out_far_right = cross(out_far[:, cut:], top)

        column = lax.dynamic_slice_in_dim(router, me, 1, axis=1).T
        column = jnp.broadcast_to(column, (16, width))
        cots = gather_low(cot_far)
        hidden_cot, far_term, far_column = backward(
            [after(x, out_far_sum) for x in cots],
            hidden[:low],
            active[:low],
            rows[:low],
            w_up,
            w_down,
            column,
        )
        out_far_left = after(out_far_left, *far_term)
        out_left = added(*[x[:, :cut] for x in out_near], out_far_left)
        out_home_left = exchange(out_left)
        back_far_sum = sum_low_after(far_term, out_far_left)
        back_far = cross(back_far_sum, top)

        near = [after(x, out_left, back_far_sum) for x in gather_low(cot_near)]
        near_hidden_cot, near_term, near_column = backward(
            near, hidden[low:], active[low:], rows[low:], w_up, w_down, column
        )
        out_far_right = after(out_far_right, back_far_sum, out_home_left, *near_term)
        out_sum = added(*[x[:, cut:] for x in out_near], out_far_right)
        out_home_right = exchange(out_sum)
        back_near = sum_low([after(x, back_far) for x in near_term])
        cots, hidden_cot = cots + near, hidden_cot + near_hidden_cot

        columns = far_column + near_column
        bit = 1
        while bit < n_tensor:
            columns = columns + cross(columns, bit)
            bit *= 2
        columns = after(columns, out_home_left)
        lanes = -(-width // (most * 128)) * 128
        high = columns.astype(jnp.bfloat16)
        rest = (columns - high.astype(jnp.float32)).astype(jnp.bfloat16)
        beside = jnp.concatenate(
            [
                jnp.pad(x, ((0, 0), (0, most * lanes - width))).reshape(1, most, lanes)
                for x in (high, rest)
            ],
            axis=2,
        )

        back_sum = added(back_near, after(back_far, out_home_left))

        back_sum = back_sum.reshape(experts, most, width)
        beside = jnp.broadcast_to(beside, (experts, most, 2 * lanes))
        ready = after(jnp.concatenate([back_sum, beside], axis=2), out_home_right)
        came = swap(ready)

        up_grad = gradient([after(x, ready) for x in rows], hidden_cot, 512)[None]
        down_grad = gradient([after(x, ready) for x in active], cots, 256)[None]

        back_home = came.reshape(slots, width + 2 * lanes)
        high, rest = (
            came[:, :, k : k + lanes].reshape(experts, most * lanes)[:, :width].astype(jnp.float32)
            for k in (width, width + lanes)
        )
        router_grad = (high + rest).T

        out_home = jnp.concatenate([after(out_home_left, ready), out_home_right], axis=1)
        out_rows = dot(placing, out_home, jnp.bfloat16, ((0,), (0,)))
        cot_rows = dot(placing, back_home, jnp.bfloat16, ((0,), (0,)))[:, :width]
        out_wide = out_rows.astype(jnp.float32)
        mixed = (gate[:, None] * out_wide).astype(jnp.bfloat16)
        own_slope = jnp.sum(out_grad.astype(jnp.float32) * out_wide, axis=1) * gate * (1.0 - gate)
        named = dot(chosen.astype(jnp.bfloat16), router, dims=((1,), (1,)))
        token_grad = (cot_rows.astype(jnp.float32) + own_slope[:, None] * named).astype(jnp.bfloat16)
        return (mixed, token_grad, up_grad, down_grad, router_grad)

    return per_device


def solution(mesh):
    in_specs = (
        P(("expert", "tensor"), None),
        P(("expert", "tensor"), None),
        P(("expert", "tensor")),
        P(),
        P("expert", None, "tensor"),
        P("expert", "tensor", None),
        P(("expert", "tensor"), None),
    )
    out_specs = (
        P(("expert", "tensor"), None),
        P(("expert", "tensor"), None),
        P("expert", None, "tensor"),
        P("expert", "tensor", None),
        P(),
    )
    return jax.shard_map(
        make(mesh.shape["expert"], mesh.shape["tensor"]),
        mesh=mesh,
        in_specs=in_specs,
        out_specs=out_specs,
        check_vma=False,
    )
```

```python
import functools

import jax
import jax.numpy as jnp
from jax import lax
from jax.experimental import pallas as pl
from jax.experimental.pallas import tpu as pltpu
from jax.sharding import PartitionSpec as P


def dot(a, b, out=jnp.float32, dims=((1,), (0,))):
    return lax.dot_general(a, b, (dims, ((), ())), preferred_element_type=jnp.float32).astype(out)


def joined(blocks):
    return jnp.concatenate(blocks, axis=0)


def after(x, *earlier):
    return lax.optimization_barrier((x,) + earlier)[0]


def added(a, b):
    return (a.astype(jnp.float32) + b.astype(jnp.float32)).astype(jnp.bfloat16)


def call(kernel, grid, in_specs, outs, out_specs, scratch=(), flops=1, moved=1, mib=20):
    return pl.pallas_call(
        kernel,
        grid=(grid,),
        in_specs=in_specs,
        out_specs=out_specs,
        out_shape=outs,
        scratch_shapes=scratch,
        compiler_params=pltpu.CompilerParams(vmem_limit_bytes=mib * 1024 * 1024),
        cost_estimate=pl.CostEstimate(flops=flops, bytes_accessed=moved, transcendentals=0),
    )


def tile_of(size, want):
    return want if size % want == 0 else size


def nt(a, b):
    return lax.dot_general(a, b, (((1,), (1,)), ((), ())), preferred_element_type=jnp.float32)


def tn(a, b):
    return lax.dot_general(a, b, (((0,), (0,)), ((), ())), preferred_element_type=jnp.float32)


def join_blocks(blocks, joint):
    count = blocks[0].shape[0]
    for i, block in enumerate(blocks):
        joint[i * count : (i + 1) * count] = block[...]


def split_blocks(value, blocks):
    count = blocks[0].shape[0]
    for i, block in enumerate(blocks):
        block[...] = value[i * count : (i + 1) * count].astype(block.dtype)


def forward_kernel(blocks, steps, tile, *refs):
    rows, (up, down) = refs[:blocks], refs[blocks : blocks + 2]
    outs = refs[blocks + 2 : -2]
    hidden, active, term = outs[:blocks], outs[blocks : 2 * blocks], outs[2 * blocks :]
    joint, held = refs[-2:]
    step = pl.program_id(0)

    @pl.when(step == 0)
    def _():
        join_blocks(rows, joint)

    @pl.when(step < steps)
    def _():
        place = pl.ds(pl.multiple_of(step * tile, tile), tile)
        value = jnp.dot(joint[...], up[...], preferred_element_type=jnp.float32)
        split_blocks(value, hidden)
        rounded = (value * jax.nn.sigmoid(value)).astype(jnp.bfloat16)
        split_blocks(rounded, active)
        held[:, place] = rounded

    @pl.when(step >= steps)
    def _():
        split_blocks(jnp.dot(held[...], down[...], preferred_element_type=jnp.float32), term)


def backward_kernel(blocks, steps, last, tile, *refs):
    cots, hidden, active, rows = (refs[k * blocks : (k + 1) * blocks] for k in range(4))
    down, up, column = refs[4 * blocks : 4 * blocks + 3]
    outs = refs[4 * blocks + 3 : -3]
    hidden_cot, term = (outs[k * blocks : (k + 1) * blocks] for k in range(2))
    total = outs[-1]
    joint, held, slope = refs[-3:]
    count = cots[0].shape[0]
    step = pl.program_id(0)

    @pl.when(step == 0)
    def _():
        join_blocks(cots, joint)
        slope[...] = jnp.zeros_like(slope)

    @pl.when(step < steps)
    def _():
        place = pl.ds(pl.multiple_of(step * tile, tile), tile)
        back_all = nt(joint[...], down[...])
        for i in range(blocks):
            back = back_all[i * count : (i + 1) * count]
            value = hidden[i][...]
            sig = jax.nn.sigmoid(value)
            rounded = (back * (sig * (1.0 + value * (1.0 - sig)))).astype(jnp.bfloat16)
            hidden_cot[i][...] = rounded
            held[i * count : (i + 1) * count, place] = rounded
            product = back * active[i][...].astype(jnp.float32)
            lanes = slope.shape[2]
            slope[i] += sum(product[:, k : k + lanes] for k in range(0, tile, lanes))

    @pl.when(step >= steps)
    def _():
        split_blocks(nt(held[...], up[...]), term)

    @pl.when(step == last)
    def _():
        add_up = jnp.zeros(total.shape, jnp.float32)
        for i in range(blocks):
            off = 1.0 - jax.nn.sigmoid(nt(rows[i][...], column[...])[:, :1])
            own = jnp.sum(slope[i], axis=1, keepdims=True) * off
            high = own.astype(jnp.bfloat16)
            rest = own - high.astype(jnp.float32)
            middle = rest.astype(jnp.bfloat16)
            least = rest - middle.astype(jnp.float32)
            lane = lax.broadcasted_iota(jnp.int32, slope.shape[1:], 1)
            split = jnp.zeros(slope.shape[1:], jnp.float32)
            for k, part in enumerate((high, middle, least)):
                split = jnp.where(lane == k, part.astype(jnp.float32), split)
            sums = tn(split.astype(jnp.bfloat16), rows[i][...])
            add_up += sums[0:1] + sums[1:2] + sums[2:3]
        total[...] = add_up


def tiles_for(rows, w_up):
    width, hidden = w_up.shape
    tile, wide = tile_of(hidden, 512), tile_of(width, 1280)
    return rows.shape[0], width, hidden, tile, wide, hidden // tile, width // wide


def whole(shape):
    return pl.BlockSpec(shape, lambda i: (0,) * len(shape), pipeline_mode=pl.Buffered(1))


def forward(rows, w_up, w_down):
    count, width, hidden, tile, wide, steps, wides = tiles_for(rows[0], w_up)
    n = len(rows)
    first, second = lambda i: jnp.minimum(i, steps - 1), lambda i: jnp.maximum(i - steps, 0)
    part = pl.BlockSpec((count, tile), lambda i: (0, first(i)))
    outs = call(
        functools.partial(forward_kernel, n, steps, tile),
        steps + wides,
        [whole((count, width))] * n
        + [
            pl.BlockSpec((width, tile), lambda i: (0, first(i))),
            pl.BlockSpec((hidden, wide), lambda i: (0, second(i))),
        ],
        [jax.ShapeDtypeStruct((count, hidden), jnp.float32)] * n
        + [jax.ShapeDtypeStruct((count, hidden), jnp.bfloat16)] * n
        + [jax.ShapeDtypeStruct((count, width), jnp.bfloat16)] * n,
        [part] * (2 * n) + [pl.BlockSpec((count, wide), lambda i: (0, second(i)))] * n,
        [
            pltpu.VMEM((n * count, width), jnp.bfloat16),
            pltpu.VMEM((n * count, hidden), jnp.bfloat16),
        ],
        mib=56,
    )(*rows, w_up, w_down)
    return list(outs[:n]), list(outs[n : 2 * n]), list(outs[2 * n :])


def backward(cots, hiddens, actives, rows, w_up, w_down, column):
    count, width, hidden, tile, wide, steps, wides = tiles_for(cots[0], w_up)
    n = len(cots)
    first, second = lambda i: jnp.minimum(i, steps - 1), lambda i: jnp.maximum(i - steps, 0)
    part = pl.BlockSpec((count, tile), lambda i: (0, first(i)))
    outs = call(
        functools.partial(backward_kernel, n, steps, steps + wides - 1, tile),
        steps + wides,
        [whole((count, width))] * n
        + [part] * (2 * n)
        + [whole((count, width))] * n
        + [
            pl.BlockSpec((tile, width), lambda i: (first(i), 0)),
            pl.BlockSpec((wide, hidden), lambda i: (second(i), 0)),
            whole(column.shape),
        ],
        [jax.ShapeDtypeStruct((count, hidden), jnp.bfloat16)] * n
        + [jax.ShapeDtypeStruct((count, width), jnp.bfloat16)] * n
        + [jax.ShapeDtypeStruct((1, width), jnp.float32)],
        [part] * n
        + [pl.BlockSpec((count, wide), lambda i: (0, second(i)))] * n
        + [pl.BlockSpec((1, width), lambda i: (0, 0))],
        [
            pltpu.VMEM((n * count, width), jnp.bfloat16),
            pltpu.VMEM((n * count, hidden), jnp.bfloat16),
            pltpu.VMEM((n, count, tile_of(tile, 128)), jnp.float32),
        ],
        mib=56,
    )(*cots, *hiddens, *actives, *rows, w_down, w_up, column)
    return list(outs[:n]), list(outs[n : 2 * n]), outs[-1]


def gradient_kernel(blocks, *refs):
    left, right, out = refs[:blocks], refs[blocks : 2 * blocks], refs[-1]
    total = sum(tn(a[...], b[...]) for a, b in zip(left, right))
    out[...] = total.astype(out.dtype)


def gradient(lefts, rights, want):
    count, height = lefts[0].shape
    width = rights[0].shape[1]
    tile = tile_of(height, want)
    return call(
        functools.partial(gradient_kernel, len(lefts)),
        height // tile,
        [pl.BlockSpec((count, tile), lambda i: (0, i))] * len(lefts)
        + [whole((count, width))] * len(rights),
        jax.ShapeDtypeStruct((height, width), jnp.bfloat16),
        pl.BlockSpec((tile, width), lambda i: (i, 0)),
        flops=2 * len(lefts) * count * height * width,
        moved=2 * (len(lefts) * count * (height + width) + height * width),
    )(*lefts, *rights)


def make(n_expert, n_tensor):
    top, low = n_tensor // 2, n_tensor // 2

    def cross(x, bit):
        return lax.ppermute(x, "tensor", [(i, i ^ bit) for i in range(n_tensor)])

    def gather_low(rows):
        held = [rows]
        bit = 1
        while bit < low:
            held = held + [cross(h, bit) for h in held]
            bit *= 2
        return held

    def sum_low_after(terms, earlier):
        while len(terms) > 1:
            bit = len(terms) // 2
            came = [cross(b, bit) for b in terms[bit:]]
            if bit == 1:
                came = [after(c, earlier) for c in came]
            terms = [added(a, c) for a, c in zip(terms[:bit], came)]
        return terms[0]

    def sum_low(terms):
        while len(terms) > 1:
            bit = len(terms) // 2
            terms = [added(a, cross(b, bit)) for a, b in zip(terms[:bit], terms[bit:])]
        return terms[0]

    def per_device(tokens, expert_ids, live_counts, router, up_weight, down_weight, out_grad):
        tok_rows, width = tokens.shape
        experts = router.shape[1]
        most = 3 * tok_rows // (2 * experts)
        slots = experts * most
        me = lax.axis_index("expert")
        ids = expert_ids[:, 0]
        live = lax.iota(jnp.int32, tok_rows) < live_counts[0]
        chosen = ids[:, None] == lax.iota(jnp.int32, experts)[None, :]
        chosen_int = chosen.astype(jnp.int32)
        rank = jnp.sum(jnp.cumsum(chosen_int, axis=0) * chosen_int, axis=1) - 1
        target = jnp.where(live, ids * most + rank, -1)
        placing = (lax.iota(jnp.int32, slots)[:, None] == target[None, :]).astype(jnp.bfloat16)
        w_up, w_down = up_weight[0], down_weight[0]

        def swap(x):
            return lax.all_to_all(x, "expert", split_axis=0, concat_axis=0, tiled=True)

        def exchange(x):
            return swap(x.reshape(experts, most, width)).reshape(slots, width)

        tok_near = exchange(dot(placing, tokens, jnp.bfloat16))
        logits = dot(tokens, router)
        gate = jax.nn.sigmoid(jnp.sum(logits * chosen.astype(jnp.float32), axis=1))
        out_cot = (gate[:, None] * out_grad.astype(jnp.float32)).astype(jnp.bfloat16)
        cot_near = exchange(after(dot(placing, out_cot, jnp.bfloat16), tok_near))
        tok_far = cross(tok_near, top)
        cot_far = cross(cot_near, top)

        rows = gather_low(after(tok_far, cot_near)) + gather_low(tok_near)
        hidden, active, term = forward(rows, w_up, w_down)
        out_far_sum, out_near = sum_low(term[:low]), sum_low(term[low:])
        cot_far = after(cot_far, *term)
        out_far = cross(after(out_far_sum, cot_far), top)

        column = lax.dynamic_slice_in_dim(router, me, 1, axis=1).T
        column = jnp.broadcast_to(column, (16, width))
        cots = gather_low(cot_far)
        hidden_cot, far_term, far_column = backward(
            [after(x, out_far_sum) for x in cots],
            hidden[:low],
            active[:low],
            rows[:low],
            w_up,
            w_down,
            column,
        )
        out_far = after(out_far, *far_term)
        out_sum = added(out_near, out_far)
        out_home = exchange(out_sum)
        back_far_sum = sum_low_after(far_term, out_far)
        back_far = cross(back_far_sum, top)

        near = [after(x, out_sum, back_far_sum) for x in gather_low(cot_near)]
        near_hidden_cot, near_term, near_column = backward(
            near, hidden[low:], active[low:], rows[low:], w_up, w_down, column
        )
        cots, hidden_cot = cots + near, hidden_cot + near_hidden_cot

        columns = far_column + near_column
        bit = 1
        while bit < n_tensor:
            columns = columns + cross(columns, bit)
            bit *= 2
        back_far = after(back_far, columns)
        back_near = sum_low([after(x, back_far) for x in near_term])
        columns = after(columns, out_home)
        lanes = -(-width // (most * 128)) * 128
        high = columns.astype(jnp.bfloat16)
        rest = (columns - high.astype(jnp.float32)).astype(jnp.bfloat16)
        beside = jnp.concatenate(
            [
                jnp.pad(x, ((0, 0), (0, most * lanes - width))).reshape(1, most, lanes)
                for x in (high, rest)
            ],
            axis=2,
        )

        back_sum = added(back_near, after(back_far, out_home))

        up_grad = gradient([after(x, back_sum, columns) for x in rows], hidden_cot, 512)[None]
        down_grad = gradient([after(x, back_sum, columns) for x in active], cots, 256)[None]

        back_sum = back_sum.reshape(experts, most, width)
        beside = jnp.broadcast_to(beside, (experts, most, 2 * lanes))
        came = swap(jnp.concatenate([back_sum, beside], axis=2))
        back_home = came.reshape(slots, width + 2 * lanes)
        high, rest = (
            came[:, :, k : k + lanes].reshape(experts, most * lanes)[:, :width].astype(jnp.float32)
            for k in (width, width + lanes)
        )
        router_grad = (high + rest).T

        out_rows = dot(placing, after(out_home, back_sum), jnp.bfloat16, ((0,), (0,)))
        cot_rows = dot(placing, back_home, jnp.bfloat16, ((0,), (0,)))[:, :width]
        out_wide = out_rows.astype(jnp.float32)
        mixed = (gate[:, None] * out_wide).astype(jnp.bfloat16)
        own_slope = jnp.sum(out_grad.astype(jnp.float32) * out_wide, axis=1) * gate * (1.0 - gate)
        named = dot(chosen.astype(jnp.bfloat16), router, dims=((1,), (1,)))
        token_grad = (cot_rows.astype(jnp.float32) + own_slope[:, None] * named).astype(jnp.bfloat16)
        return (mixed, token_grad, up_grad, down_grad, router_grad)

    return per_device


def solution(mesh):
    in_specs = (
        P(("expert", "tensor"), None),
        P(("expert", "tensor"), None),
        P(("expert", "tensor")),
        P(),
        P("expert", None, "tensor"),
        P("expert", "tensor", None),
        P(("expert", "tensor"), None),
    )
    out_specs = (
        P(("expert", "tensor"), None),
        P(("expert", "tensor"), None),
        P("expert", None, "tensor"),
        P("expert", "tensor", None),
        P(),
    )
    return jax.shard_map(
        make(mesh.shape["expert"], mesh.shape["tensor"]),
        mesh=mesh,
        in_specs=in_specs,
        out_specs=out_specs,
        check_vma=False,
    )
```

```python
import functools

import jax
import jax.numpy as jnp
from jax import lax
from jax.experimental import pallas as pl
from jax.experimental.pallas import tpu as pltpu
from jax.sharding import PartitionSpec as P


def dot(a, b, out=jnp.float32, dims=((1,), (0,))):
    return lax.dot_general(a, b, (dims, ((), ())), preferred_element_type=jnp.float32).astype(out)


def joined(blocks):
    return jnp.concatenate(blocks, axis=0)


def after(x, *earlier):
    return lax.optimization_barrier((x,) + earlier)[0]


def added(a, b):
    return (a.astype(jnp.float32) + b.astype(jnp.float32)).astype(jnp.bfloat16)


def call(kernel, grid, in_specs, outs, out_specs, scratch=(), flops=1, moved=1, mib=20):
    return pl.pallas_call(
        kernel,
        grid=(grid,),
        in_specs=in_specs,
        out_specs=out_specs,
        out_shape=outs,
        scratch_shapes=scratch,
        compiler_params=pltpu.CompilerParams(vmem_limit_bytes=mib * 1024 * 1024),
        cost_estimate=pl.CostEstimate(flops=flops, bytes_accessed=moved, transcendentals=0),
    )


def tile_of(size, want):
    return want if size % want == 0 else size


def nt(a, b):
    return lax.dot_general(a, b, (((1,), (1,)), ((), ())), preferred_element_type=jnp.float32)


def tn(a, b):
    return lax.dot_general(a, b, (((0,), (0,)), ((), ())), preferred_element_type=jnp.float32)


def join_blocks(blocks, joint):
    count = blocks[0].shape[0]
    for i, block in enumerate(blocks):
        joint[i * count : (i + 1) * count] = block[...]


def split_blocks(value, blocks):
    count = blocks[0].shape[0]
    for i, block in enumerate(blocks):
        block[...] = value[i * count : (i + 1) * count].astype(block.dtype)


def forward_kernel(blocks, steps, tile, *refs):
    rows, (up, down) = refs[:blocks], refs[blocks : blocks + 2]
    outs = refs[blocks + 2 : -2]
    hidden, active, term = outs[:blocks], outs[blocks : 2 * blocks], outs[2 * blocks :]
    joint, held = refs[-2:]
    step = pl.program_id(0)

    @pl.when(step == 0)
    def _():
        join_blocks(rows, joint)

    @pl.when(step < steps)
    def _():
        place = pl.ds(pl.multiple_of(step * tile, tile), tile)
        value = jnp.dot(joint[...], up[...], preferred_element_type=jnp.float32)
        split_blocks(value, hidden)
        rounded = (value * jax.nn.sigmoid(value)).astype(jnp.bfloat16)
        split_blocks(rounded, active)
        held[:, place] = rounded

    @pl.when(step >= steps)
    def _():
        split_blocks(jnp.dot(held[...], down[...], preferred_element_type=jnp.float32), term)


def backward_kernel(blocks, steps, last, tile, *refs):
    cots, hidden, active, rows = (refs[k * blocks : (k + 1) * blocks] for k in range(4))
    down, up, column = refs[4 * blocks : 4 * blocks + 3]
    outs = refs[4 * blocks + 3 : -3]
    hidden_cot, term = (outs[k * blocks : (k + 1) * blocks] for k in range(2))
    total = outs[-1]
    joint, held, slope = refs[-3:]
    count = cots[0].shape[0]
    step = pl.program_id(0)

    @pl.when(step == 0)
    def _():
        join_blocks(cots, joint)
        slope[...] = jnp.zeros_like(slope)

    @pl.when(step < steps)
    def _():
        place = pl.ds(pl.multiple_of(step * tile, tile), tile)
        back_all = nt(joint[...], down[...])
        for i in range(blocks):
            back = back_all[i * count : (i + 1) * count]
            value = hidden[i][...]
            sig = jax.nn.sigmoid(value)
            rounded = (back * (sig * (1.0 + value * (1.0 - sig)))).astype(jnp.bfloat16)
            hidden_cot[i][...] = rounded
            held[i * count : (i + 1) * count, place] = rounded
            product = back * active[i][...].astype(jnp.float32)
            lanes = slope.shape[2]
            slope[i] += sum(product[:, k : k + lanes] for k in range(0, tile, lanes))

    @pl.when(step >= steps)
    def _():
        split_blocks(nt(held[...], up[...]), term)

    @pl.when(step == last)
    def _():
        add_up = jnp.zeros(total.shape, jnp.float32)
        for i in range(blocks):
            off = 1.0 - jax.nn.sigmoid(nt(rows[i][...], column[...])[:, :1])
            own = jnp.sum(slope[i], axis=1, keepdims=True) * off
            high = own.astype(jnp.bfloat16)
            rest = own - high.astype(jnp.float32)
            middle = rest.astype(jnp.bfloat16)
            least = rest - middle.astype(jnp.float32)
            lane = lax.broadcasted_iota(jnp.int32, slope.shape[1:], 1)
            split = jnp.zeros(slope.shape[1:], jnp.float32)
            for k, part in enumerate((high, middle, least)):
                split = jnp.where(lane == k, part.astype(jnp.float32), split)
            sums = tn(split.astype(jnp.bfloat16), rows[i][...])
            add_up += sums[0:1] + sums[1:2] + sums[2:3]
        total[...] = add_up


def tiles_for(rows, w_up):
    width, hidden = w_up.shape
    tile, wide = tile_of(hidden, 512), tile_of(width, 1280)
    return rows.shape[0], width, hidden, tile, wide, hidden // tile, width // wide


def whole(shape):
    return pl.BlockSpec(shape, lambda i: (0,) * len(shape), pipeline_mode=pl.Buffered(1))


def forward(rows, w_up, w_down):
    count, width, hidden, tile, wide, steps, wides = tiles_for(rows[0], w_up)
    n = len(rows)
    first, second = lambda i: jnp.minimum(i, steps - 1), lambda i: jnp.maximum(i - steps, 0)
    part = pl.BlockSpec((count, tile), lambda i: (0, first(i)))
    outs = call(
        functools.partial(forward_kernel, n, steps, tile),
        steps + wides,
        [whole((count, width))] * n
        + [
            pl.BlockSpec((width, tile), lambda i: (0, first(i))),
            pl.BlockSpec((hidden, wide), lambda i: (0, second(i))),
        ],
        [jax.ShapeDtypeStruct((count, hidden), jnp.float32)] * n
        + [jax.ShapeDtypeStruct((count, hidden), jnp.bfloat16)] * n
        + [jax.ShapeDtypeStruct((count, width), jnp.bfloat16)] * n,
        [part] * (2 * n) + [pl.BlockSpec((count, wide), lambda i: (0, second(i)))] * n,
        [
            pltpu.VMEM((n * count, width), jnp.bfloat16),
            pltpu.VMEM((n * count, hidden), jnp.bfloat16),
        ],
        mib=56,
    )(*rows, w_up, w_down)
    return list(outs[:n]), list(outs[n : 2 * n]), list(outs[2 * n :])


def backward(cots, hiddens, actives, rows, w_up, w_down, column):
    count, width, hidden, tile, wide, steps, wides = tiles_for(cots[0], w_up)
    n = len(cots)
    first, second = lambda i: jnp.minimum(i, steps - 1), lambda i: jnp.maximum(i - steps, 0)
    part = pl.BlockSpec((count, tile), lambda i: (0, first(i)))
    outs = call(
        functools.partial(backward_kernel, n, steps, steps + wides - 1, tile),
        steps + wides,
        [whole((count, width))] * n
        + [part] * (2 * n)
        + [whole((count, width))] * n
        + [
            pl.BlockSpec((tile, width), lambda i: (first(i), 0)),
            pl.BlockSpec((wide, hidden), lambda i: (second(i), 0)),
            whole(column.shape),
        ],
        [jax.ShapeDtypeStruct((count, hidden), jnp.bfloat16)] * n
        + [jax.ShapeDtypeStruct((count, width), jnp.bfloat16)] * n
        + [jax.ShapeDtypeStruct((1, width), jnp.float32)],
        [part] * n
        + [pl.BlockSpec((count, wide), lambda i: (0, second(i)))] * n
        + [pl.BlockSpec((1, width), lambda i: (0, 0))],
        [
            pltpu.VMEM((n * count, width), jnp.bfloat16),
            pltpu.VMEM((n * count, hidden), jnp.bfloat16),
            pltpu.VMEM((n, count, tile_of(tile, 128)), jnp.float32),
        ],
        mib=56,
    )(*cots, *hiddens, *actives, *rows, w_down, w_up, column)
    return list(outs[:n]), list(outs[n : 2 * n]), outs[-1]


def gradient_kernel(blocks, *refs):
    left, right, out = refs[:blocks], refs[blocks : 2 * blocks], refs[-1]
    total = sum(tn(a[...], b[...]) for a, b in zip(left, right))
    out[...] = total.astype(out.dtype)


def gradient(lefts, rights, want):
    count, height = lefts[0].shape
    width = rights[0].shape[1]
    tile = tile_of(height, want)
    return call(
        functools.partial(gradient_kernel, len(lefts)),
        height // tile,
        [pl.BlockSpec((count, tile), lambda i: (0, i))] * len(lefts)
        + [whole((count, width))] * len(rights),
        jax.ShapeDtypeStruct((height, width), jnp.bfloat16),
        pl.BlockSpec((tile, width), lambda i: (i, 0)),
        flops=2 * len(lefts) * count * height * width,
        moved=2 * (len(lefts) * count * (height + width) + height * width),
    )(*lefts, *rights)


def make(n_expert, n_tensor):
    top, low = n_tensor // 2, n_tensor // 2

    def cross(x, bit):
        return lax.ppermute(x, "tensor", [(i, i ^ bit) for i in range(n_tensor)])

    def gather_low(rows):
        held = [rows]
        bit = 1
        while bit < low:
            held = held + [cross(h, bit) for h in held]
            bit *= 2
        return held

    def sum_low_after(terms, earlier):
        while len(terms) > 1:
            bit = len(terms) // 2
            came = [cross(b, bit) for b in terms[bit:]]
            if bit == 1:
                came = [after(c, earlier) for c in came]
            terms = [added(a, c) for a, c in zip(terms[:bit], came)]
        return terms[0]

    def sum_low(terms):
        while len(terms) > 1:
            bit = len(terms) // 2
            terms = [added(a, cross(b, bit)) for a, b in zip(terms[:bit], terms[bit:])]
        return terms[0]

    def per_device(tokens, expert_ids, live_counts, router, up_weight, down_weight, out_grad):
        tok_rows, width = tokens.shape
        experts = router.shape[1]
        most = 3 * tok_rows // (2 * experts)
        slots = experts * most
        me = lax.axis_index("expert")
        ids = expert_ids[:, 0]
        live = lax.iota(jnp.int32, tok_rows) < live_counts[0]
        chosen = ids[:, None] == lax.iota(jnp.int32, experts)[None, :]
        place = lax.iota(jnp.int32, tok_rows)
        ahead = (place[None, :] < place[:, None]).astype(jnp.bfloat16)
        counts = dot(ahead, chosen.astype(jnp.bfloat16))
        rank = jnp.sum(jnp.where(chosen, counts, 0.0), axis=1).astype(jnp.int32)
        target = jnp.where(live, ids * most + rank, -1)
        placing = (lax.iota(jnp.int32, slots)[:, None] == target[None, :]).astype(jnp.bfloat16)
        w_up, w_down = up_weight[0], down_weight[0]

        def swap(x):
            return lax.all_to_all(x, "expert", split_axis=0, concat_axis=0, tiled=True)

        def exchange(x):
            return swap(x.reshape(experts, most, width)).reshape(slots, width)

        tok_near = exchange(dot(placing, tokens, jnp.bfloat16))
        logits = dot(tokens, router)
        gate = jax.nn.sigmoid(jnp.sum(logits * chosen.astype(jnp.float32), axis=1))
        out_cot = (gate[:, None] * out_grad.astype(jnp.float32)).astype(jnp.bfloat16)
        cot_near = exchange(after(dot(placing, out_cot, jnp.bfloat16), tok_near))
        tok_far = cross(tok_near, top)
        cot_far = cross(cot_near, top)

        rows = gather_low(after(tok_far, cot_near)) + gather_low(tok_near)
        hidden, active, term = forward(rows, w_up, w_down)
        out_far_sum, out_near = sum_low(term[:low]), sum_low(term[low:])
        cot_far = after(cot_far, *term)
        out_far = cross(after(out_far_sum, cot_far), top)

        column = lax.dynamic_slice_in_dim(router, me, 1, axis=1).T
        column = jnp.broadcast_to(column, (16, width))
        cots = gather_low(cot_far)
        hidden_cot, far_term, far_column = backward(
            [after(x, out_far_sum) for x in cots],
            hidden[:low],
            active[:low],
            rows[:low],
            w_up,
            w_down,
            column,
        )
        out_far = after(out_far, *far_term)
        out_sum = added(out_near, out_far)
        out_home = exchange(out_sum)
        back_far_sum = sum_low_after(far_term, out_far)
        back_far = cross(back_far_sum, top)

        near = [after(x, out_sum, back_far_sum) for x in gather_low(cot_near)]
        near_hidden_cot, near_term, near_column = backward(
            near, hidden[low:], active[low:], rows[low:], w_up, w_down, column
        )
        cots, hidden_cot = cots + near, hidden_cot + near_hidden_cot

        columns = far_column + near_column
        bit = 1
        while bit < n_tensor:
            columns = columns + cross(columns, bit)
            bit *= 2
        back_far = after(back_far, columns)
        back_near = sum_low([after(x, back_far) for x in near_term])
        columns = after(columns, out_home)
        lanes = -(-width // (most * 128)) * 128
        high = columns.astype(jnp.bfloat16)
        rest = (columns - high.astype(jnp.float32)).astype(jnp.bfloat16)
        beside = jnp.concatenate(
            [
                jnp.pad(x, ((0, 0), (0, most * lanes - width))).reshape(1, most, lanes)
                for x in (high, rest)
            ],
            axis=2,
        )

        back_sum = added(back_near, after(back_far, out_home))

        up_grad = gradient([after(x, back_sum, columns) for x in rows], hidden_cot, 512)[None]
        down_grad = gradient([after(x, back_sum, columns) for x in active], cots, 256)[None]

        back_sum = back_sum.reshape(experts, most, width)
        beside = jnp.broadcast_to(beside, (experts, most, 2 * lanes))
        came = swap(jnp.concatenate([back_sum, beside], axis=2))
        back_home = came.reshape(slots, width + 2 * lanes)
        high, rest = (
            came[:, :, k : k + lanes].reshape(experts, most * lanes)[:, :width].astype(jnp.float32)
            for k in (width, width + lanes)
        )
        router_grad = (high + rest).T

        out_rows = dot(placing, after(out_home, back_sum), jnp.bfloat16, ((0,), (0,)))
        cot_rows = dot(placing, back_home, jnp.bfloat16, ((0,), (0,)))[:, :width]
        out_wide = out_rows.astype(jnp.float32)
        mixed = (gate[:, None] * out_wide).astype(jnp.bfloat16)
        own_slope = jnp.sum(out_grad.astype(jnp.float32) * out_wide, axis=1) * gate * (1.0 - gate)
        named = dot(chosen.astype(jnp.bfloat16), router, dims=((1,), (1,)))
        token_grad = (cot_rows.astype(jnp.float32) + own_slope[:, None] * named).astype(jnp.bfloat16)
        return (mixed, token_grad, up_grad, down_grad, router_grad)

    return per_device


def solution(mesh):
    in_specs = (
        P(("expert", "tensor"), None),
        P(("expert", "tensor"), None),
        P(("expert", "tensor")),
        P(),
        P("expert", None, "tensor"),
        P("expert", "tensor", None),
        P(("expert", "tensor"), None),
    )
    out_specs = (
        P(("expert", "tensor"), None),
        P(("expert", "tensor"), None),
        P("expert", None, "tensor"),
        P("expert", "tensor", None),
        P(),
    )
    return jax.shard_map(
        make(mesh.shape["expert"], mesh.shape["tensor"]),
        mesh=mesh,
        in_specs=in_specs,
        out_specs=out_specs,
        check_vma=False,
    )
```
